32 devices in a mesh: ep: 8 (over y, x, core), tp: 4 (over z).
Axes of the slice: x: 2, y: 2, z: 4, core: 2. Of those that a mesh axis runs over, the one named last changes fastest.
Arguments:
- inputs: bfloat16 [8192, 1536], P('ep'), may hold values from -6 to 6
- routes: int32 [8192, 4], P('ep'), may hold values from 0 to 7, all different within a row; in each aligned block of 1024 rows (0 to 1023, 1024 to 2047, ...) at most 640 rows name the same one
- norm_gain: float32 [1536], replicated, may hold values from 0.1 to 1.9
- query_weight: bfloat16 [1536, 1536], P(None, 'tp'), may hold values from -0.15625 to 0.15625
- key_weight: bfloat16 [1536, 512], P(None, 'tp'), may hold values from -0.15625 to 0.15625
- value_weight: bfloat16 [1536, 512], P(None, 'tp'), may hold values from -0.15625 to 0.15625
- output_weight: bfloat16 [1536, 1536], P('tp'), may hold values from -0.875 to 0.875
- mixer_gain: float32 [1536], replicated, may hold values from 0.1 to 1.9
- router_weight: bfloat16 [1536, 8], replicated, may hold values from -0.078125 to 0.078125
- gate_weight: bfloat16 [8, 1536, 512], P('ep', None, 'tp'), may hold values from -0.15625 to 0.15625
- up_weight: bfloat16 [8, 1536, 512], P('ep', None, 'tp'), may hold values from -0.15625 to 0.15625
- down_weight: bfloat16 [8, 512, 1536], P('ep', 'tp'), may hold values from -1 to 1
- cotangent: bfloat16 [8192, 1536], P('ep'), may hold values from -6 to 6
Outputs:
- result: bfloat16 [8192, 1536], P('ep')
- grad_inputs: bfloat16 [8192, 1536], P('ep')
- grad_norm_gain: float32 [1536], replicated
- grad_query_weight: float32 [1536, 1536], P(None, 'tp')
- grad_key_weight: float32 [1536, 512], P(None, 'tp')
- grad_value_weight: float32 [1536, 512], P(None, 'tp')
- grad_output_weight: float32 [1536, 1536], P('tp')
- grad_mixer_gain: float32 [1536], replicated
- grad_router_weight: float32 [1536, 8], replicated
- grad_gate_weight: float32 [8, 1536, 512], P('ep', None, 'tp')
- grad_up_weight: float32 [8, 1536, 512], P('ep', None, 'tp')
- grad_down_weight: float32 [8, 512, 1536], P('ep', 'tp')
The draws below stay inside these ranges and needn't reach their ends.
Inputs may be any that keep to these rules, and one draw needn't show every extreme that they name: `routes`: each row names 4 different experts. Among the 1024 rows of one index of ep no expert is named more than 640 times, and in every draw some expert is named exactly 640 times by the rows of some index; every expert is named by some row.
All inputs are finite; a program needn't handle non-finite values.
Results may differ from the reference program's by a relative error of at most 0.025.
Values may be sent and summed in bfloat16 or wider, within the bound.
No kernel may reach another device: no remote copies, remote signals or barrier semaphores. Data moves between devices by JAX's collectives and lax.ppermute only.
A program may use at most 384 MiB of HBM per device.

```python
import math
import jax
import jax.numpy as jnp
import numpy as np
from jax import lax

D = 1536
HEADS = 24
KV = 8
HD = 64
FF = 512
LEN = 1024
TOK_DEV = 1024
TOKENS = 8192
EXPERTS = 8
TOP = 4
CAP = 640
N_TP = 4


def levels(stream_key, extent, shards, low, top_value):
    level = 1.0
    for axis_at, blocks in shards:
        steps = jax.random.uniform(jax.random.fold_in(jax.random.fold_in(stream_key, 6), axis_at), (blocks,), jnp.float32, low / len(shards), top_value / len(shards))
        level = level * jnp.repeat(jnp.exp(steps), extent[axis_at] // blocks).reshape((-1,) + (1,) * (len(extent) - 1 - axis_at))
    return level


def shared_out(stream_key, own, number, rows, count, top, bound, lean):
    sequence = jax.random.permutation(stream_key, count)
    crowded, common = portions_of(count, rows * top, bound, lean, True), portions_of(count, rows * top, bound, lean, False)
    places = jnp.arange(count)

    def named(sizes, rotation):
        used = int((sizes > 0).sum())
        fixed = max(1, used // 4)
        passed = fixed + (places - fixed + rotation * (used - fixed)) % max(1, count - fixed)
        return jnp.zeros((count,), jnp.int32).at[sequence[jnp.where(places < fixed, places, passed)]].set(jnp.asarray(sizes, jnp.int32))

    sizes = jnp.where(number % 4 == 0, named(crowded, number // 4), named(common, number - number // 4 - 1))
    mixed = jax.random.permutation(jax.random.fold_in(own, 3), count)
    giver, sink = mixed[0:count // 2 * 2:2], mixed[1:count // 2 * 2:2]
    margin = jnp.minimum(sizes[giver] - 1, bound - sizes[sink]) // 2
    margin = jnp.where((giver == sequence[0]) | (sink == sequence[0]) | (sizes[sink] == 0), 0, jnp.maximum(margin, 0))
    passed = jax.random.randint(jax.random.fold_in(own, 4), (count // 2,), 0, 1 << 20) % (margin + 1)
    sizes = sizes.at[giver].add(-passed).at[sink].add(passed)
    members = jnp.searchsorted(jnp.cumsum(sizes), jnp.arange(rows * top), side="right").astype(jnp.int32)
    grid = members.reshape(top, rows).T
    grid = grid[jax.random.permutation(jax.random.fold_in(own, 1), rows)]
    rotation = jax.random.randint(jax.random.fold_in(own, 2), (rows, 1), 0, top)
    return jnp.take_along_axis(grid, (jnp.arange(top)[None, :] + rotation) % top, axis=1)


def portions_of(number_of, total, limit, skew, full):
    loads = [(1 << 20) // math.isqrt(grade ** skew) + 1 for grade in range(1, number_of + 1)]
    largest = limit if full else min(limit, max(-(-total // number_of), total * loads[0] // sum(loads)))
    least = 1 if total - largest >= number_of - 1 else 0
    counts, rest = [largest] + [least] * (number_of - 1), total - largest - least * (number_of - 1)
    while rest > 0:
        free = [i for i in range(1, number_of) if counts[i] < largest] or [i for i in range(1, number_of) if counts[i] < limit]
        whole, budget = sum([loads[i] for i in free]), rest
        for i in free:
            more = min(limit - counts[i], max(1, budget * loads[i] // whole), rest)
            counts[i] = counts[i] + more
            rest = rest - more
    return np.array(counts)


def bell_draw(own_key, dims, spread, limit, shards=(), kind=jnp.bfloat16):
    loudness = levels(own_key, dims, shards, -0.22, 0.18) if shards else 1.0
    drawn = jax.random.normal(own_key, dims, jnp.float32) * spread * loudness
    return jnp.minimum(jnp.maximum(drawn, -limit), limit).astype(kind)


def setup_inputs(seed: int = 0) -> dict:
    key_of = jax.random.split(jax.random.key(seed), 14)
    inputs = bell_draw(key_of[0], (TOKENS, D), 1.0, 6.0, ((0, 8),))
    routes_keys = jax.random.split(jax.random.fold_in(key_of[1], 1), TOKENS // TOK_DEV)
    routes_turns = jax.random.permutation(jax.random.fold_in(key_of[1], 3), TOKENS // TOK_DEV)
    routes = jax.vmap(lambda own, number: shared_out(jax.random.fold_in(key_of[1], 2), own, number, TOK_DEV, EXPERTS, TOP, CAP, 1))(routes_keys, routes_turns).reshape((TOKENS, TOP))
    norm_gain = jnp.clip(1.0 + 0.18 * jax.random.normal(key_of[2], (D,), jnp.float32), 0.1, 1.9)
    query_weight = bell_draw(key_of[3], (D, HEADS * HD), D ** -0.5, 0.15625, ((1, 4),))
    key_weight = bell_draw(key_of[4], (D, KV * HD), D ** -0.5, 0.15625, ((1, 4),))
    value_weight = bell_draw(key_of[5], (D, KV * HD), D ** -0.5, 0.15625, ((1, 4),))
    output_weight = bell_draw(key_of[6], (HEADS * HD, D), (HEADS * HD // 32) ** -0.5, 0.875, ((0, 4),))
    mixer_gain = jnp.clip(1.0 + 0.18 * jax.random.normal(key_of[7], (D,), jnp.float32), 0.1, 1.9)
    router_weight = bell_draw(key_of[8], (D, EXPERTS), (4 * D) ** -0.5, 0.078125)
    gate_weight = bell_draw(key_of[9], (EXPERTS, D, FF), D ** -0.5, 0.15625, ((0, 8), (2, 4)))
    up_weight = bell_draw(key_of[10], (EXPERTS, D, FF), D ** -0.5, 0.15625, ((0, 8), (2, 4)))
    down_weight = bell_draw(key_of[11], (EXPERTS, FF, D), (FF // 16) ** -0.5, 1.0, ((0, 8), (1, 4)))
    cotangent = bell_draw(key_of[12], (TOKENS, D), 1.0, 6.0, ((0, 8),))
    return {"inputs": inputs, "routes": routes, "norm_gain": norm_gain, "query_weight": query_weight, "key_weight": key_weight, "value_weight": value_weight, "output_weight": output_weight, "mixer_gain": mixer_gain, "router_weight": router_weight, "gate_weight": gate_weight, "up_weight": up_weight, "down_weight": down_weight, "cotangent": cotangent}


@jax.custom_vjp
def low(v):
    return lax.optimization_barrier(v.astype(jnp.bfloat16)).astype(jnp.float32)

@jax.custom_vjp
def low_back(v):
    return v

def low_keep(v):
    return (low(v), None)

def low_pass(kept, grad):
    return (grad,)

def back_keep(v):
    return (v, None)

def back_low(kept, grad):
    return (low(grad),)
low.defvjp(low_keep, low_pass)
low_back.defvjp(back_keep, back_low)
EPS = 1e-06
HIGH = lax.Precision.HIGHEST

def rms_norm(values, gain):
    inverse = lax.rsqrt(lax.optimization_barrier(jnp.mean(values * values, axis=-1, keepdims=True)) + EPS)
    return values * inverse * gain

def rotary_tables(positions, depth):
    half = depth // 2
    freqs = 10000.0 ** (-jnp.arange(half, dtype=jnp.float32) * 2.0 / depth)
    angles = positions[:, None] * freqs[None, :]
    return (jnp.cos(angles), jnp.sin(angles))

def rotate(values, cosine, sine):
    half = values.shape[-1] // 2
    first = values[..., :half]
    second = values[..., half:]
    cos_b = cosine[:, None, :]
    sin_b = sine[:, None, :]
    return jnp.concatenate([first * cos_b - second * sin_b, second * cos_b + first * sin_b], axis=-1)

def sequence_attention(pieces):
    query, key, value = pieces
    repeat = HEADS // KV
    query = query.reshape(LEN, KV, repeat, HD)
    scores = jnp.einsum('qgrd,kgd->grqk', query, key, precision=HIGH) * HD ** (-0.5)
    scores = low_back(scores)
    causal = jnp.arange(LEN)[:, None] >= jnp.arange(LEN)[None, :]
    scores = jnp.where(causal, scores, -1e+30)
    peak = lax.optimization_barrier(jnp.max(scores, axis=-1, keepdims=True))
    weights = jnp.exp(scores - peak)
    probs = weights / lax.optimization_barrier(jnp.sum(weights, axis=-1, keepdims=True))
    mixed = jnp.einsum('grqk,kgd->qgrd', low(probs), value, precision=HIGH)
    return mixed.reshape(LEN, HEADS * HD)

def forward(inputs, norm_gain, query_weight, key_weight, value_weight, output_weight, mixer_gain, router_weight, gate_weight, up_weight, down_weight, routes):
    normed = low(rms_norm(inputs, norm_gain))
    query = low_back(jnp.dot(normed, query_weight, precision=HIGH))
    key = low_back(jnp.dot(normed, key_weight, precision=HIGH))
    value = low(low_back(jnp.dot(normed, value_weight, precision=HIGH)))
    seqs = TOKENS // LEN
    cosine, sine = rotary_tables(jnp.arange(LEN, dtype=jnp.float32), HD)
    query = low(rotate(query.reshape(seqs, LEN, HEADS, HD), cosine, sine))
    key = low(rotate(key.reshape(seqs, LEN, KV, HD), cosine, sine))
    value = value.reshape(seqs, LEN, KV, HD)
    mixed = lax.map(jax.checkpoint(sequence_attention), (query, key, value))
    mixed = low(low_back(mixed.reshape(TOKENS, HEADS * HD)))
    attended = inputs + low_back(jnp.dot(mixed, output_weight, precision=HIGH))
    routed_in = low(rms_norm(attended, mixer_gain))
    logits = low_back(jnp.dot(routed_in, router_weight, precision=HIGH))
    picked = jnp.take_along_axis(logits, routes, axis=1)
    gates = jax.nn.softmax(picked, axis=-1)
    chosen = (routes[:, :, None] == jnp.arange(EXPERTS, dtype=jnp.int32)[None, None, :]).astype(jnp.float32)
    weights_table = lax.optimization_barrier(jnp.sum(gates[:, :, None] * chosen, axis=1))
    shard = FF // N_TP
    total = jnp.zeros_like(attended)
    for expert in range(EXPERTS):
        out_sum = jnp.zeros_like(attended)
        for part in range(N_TP):
            lower = part * shard
            local_in = low_back(routed_in)
            gate_vals = low_back(jnp.dot(local_in, gate_weight[expert][:, lower:lower + shard], precision=HIGH))
            up_vals = low_back(jnp.dot(local_in, up_weight[expert][:, lower:lower + shard], precision=HIGH))
            hidden = low(jax.nn.silu(gate_vals) * up_vals)
            out_sum = out_sum + low(jnp.dot(hidden, down_weight[expert][lower:lower + shard, :], precision=HIGH))
        total = total + weights_table[:, expert:expert + 1] * low_back(out_sum)
    return attended + total

def reference(inputs, routes, norm_gain, query_weight, key_weight, value_weight, output_weight, mixer_gain, router_weight, gate_weight, up_weight, down_weight, cotangent):
    params = [inputs, norm_gain, query_weight, key_weight, value_weight, output_weight, mixer_gain, router_weight, gate_weight, up_weight, down_weight]
    floats = [item.astype(jnp.float32) for item in params]

    def closed(*values):
        return forward(*values, routes)
    result, pullback = jax.vjp(closed, *floats)
    grads = pullback(cotangent.astype(jnp.float32))
    return (result.astype(jnp.bfloat16), grads[0].astype(jnp.bfloat16), grads[1], grads[2], grads[3], grads[4], grads[5], grads[6], grads[7], grads[8], grads[9], grads[10])
```

```python
import jax
import jax.numpy as jnp
from jax import lax
from jax.sharding import PartitionSpec as P

HD = 64
LEN = 1024
EPS = 1e-06
MASKED = -1e30
BF = jnp.bfloat16
F32 = jnp.float32


def rotary_tables(positions, depth):
    half = depth // 2
    freqs = 10000.0 ** (-jnp.arange(half, dtype=jnp.float32) * 2.0 / depth)
    angles = positions[:, None] * freqs[None, :]
    return (jnp.cos(angles), jnp.sin(angles))


def rotate(values, cosine, sine):
    half = values.shape[-1] // 2
    first = values[..., :half]
    second = values[..., half:]
    cos_b = cosine[:, None, :]
    sin_b = sine[:, None, :]
    return jnp.concatenate(
        [first * cos_b - second * sin_b, second * cos_b + first * sin_b], axis=-1
    )


def unrotate(grads, cosine, sine):
    return rotate(grads, cosine, -sine)


def block_scores(query_block, keys, start, scale):
    scores = jnp.einsum("qgrd,kgd->grqk", query_block, keys, preferred_element_type=F32) * scale
    rows_at = start + jnp.arange(query_block.shape[0])[:, None]
    cols_at = jnp.arange(keys.shape[0])[None, :]
    return jnp.where(rows_at >= cols_at, scores, MASKED)


BLOCK = 256


def attention_forward(query, key, value, scale):
    tokens, heads, depth = query.shape
    groups = key.shape[1]
    repeat = heads // groups
    outs, logs = [], []
    for start in range(0, tokens, BLOCK):
        stop = start + BLOCK
        queries = query[start:stop].reshape(BLOCK, groups, repeat, depth)
        scores = block_scores(queries, key[:stop], start, scale)
        peak = jnp.max(scores, axis=-1, keepdims=True)
        weights = jnp.exp(scores - peak)
        totals = jnp.sum(weights, axis=-1, keepdims=True)
        probs = (weights / totals).astype(BF)
        mixed = jnp.einsum("grqk,kgd->qgrd", probs, value[:stop], preferred_element_type=F32)
        outs.append(mixed.astype(BF).reshape(BLOCK, heads * depth))
        logs.append(peak + jnp.log(totals))
    return (jnp.concatenate(outs, axis=0), logs)


def attention_backward(query, key, value, logs, grad_mixed, scale):
    tokens, heads, depth = query.shape
    groups = key.shape[1]
    repeat = heads // groups
    grad_key = jnp.zeros(key.shape, F32)
    grad_value = jnp.zeros(key.shape, F32)
    grad_queries = []
    for number, start in enumerate(range(0, tokens, BLOCK)):
        stop = start + BLOCK
        queries = query[start:stop].reshape(BLOCK, groups, repeat, depth)
        grads = grad_mixed[start:stop].reshape(BLOCK, groups, repeat, depth)
        keys = key[:stop]
        scores = block_scores(queries, keys, start, scale)
        probs = jnp.exp(scores - logs[number])
        grad_probs = jnp.einsum("qgrd,kgd->grqk", grads, value[:stop], preferred_element_type=F32)
        inner = jnp.sum(probs * grad_probs, axis=-1, keepdims=True)
        grad_scores = (probs * (grad_probs - inner)).astype(BF)
        grad_queries.append(
            jnp.einsum("grqk,kgd->qgrd", grad_scores, keys, preferred_element_type=F32).reshape(
                BLOCK, heads, depth
            )
            * scale
        )
        more_key = (
            jnp.einsum("grqk,qgrd->kgd", grad_scores, queries, preferred_element_type=F32) * scale
        )
        more_value = jnp.einsum(
            "grqk,qgrd->kgd", probs.astype(BF), grads, preferred_element_type=F32
        )
        grad_key = grad_key.at[:stop].add(more_key)
        grad_value = grad_value.at[:stop].add(more_value)
    return (jnp.concatenate(grad_queries, axis=0), grad_key, grad_value)


def swap(x, bit):
    return lax.ppermute(x, "ep", [(i, i ^ bit) for i in range(lax.axis_size("ep"))])


def gather_ep(x):
    n = lax.axis_size("ep")
    if n != 8:
        return lax.all_gather(x, "ep")
    first = [x] + [swap(x, k) for k in (2, 4, 6)]
    second = [swap(v, 1) for v in first]
    return jnp.stack([v for pair in zip(first, second) for v in pair])


def scatter_ep(x):
    n = lax.axis_size("ep")
    if n != 8:
        return lax.psum_scatter(x, "ep", scatter_dimension=0, tiled=False).astype(F32)
    other = swap(x[1::2], 1)
    mine = (x[0::2].astype(F32) + other.astype(F32)).astype(BF)
    got = [mine[0]] + [swap(mine[j], 2 * j) for j in (1, 2, 3)]
    return sum(v.astype(F32) for v in got)


def step_right(x, upto=None):
    n = lax.axis_size("tp")
    return lax.ppermute(x, "tp", [(i, i + 1) for i in range(n - 1 if upto is None else upto)])


def step_left(x, upto=None):
    n = lax.axis_size("tp")
    return lax.ppermute(x, "tp", [(n - 1 - i, n - 2 - i) for i in range(n - 1 if upto is None else upto)])


def gather_tp(x):
    n = lax.axis_size("tp")
    at = lax.axis_index("tp")
    right, left = [x], [x]
    for _ in range(1, n):
        right.append(step_right(right[-1]))
        left.append(step_left(left[-1]))
    return [x] + [jnp.where(at >= s, right[s], left[n - s]) for s in range(1, n)]


def scatter_tp(parts):
    n = lax.axis_size("tp")
    right = left = None
    for t in range(1, n):
        give_right = parts[t]
        give_left = parts[n - t]
        if right is not None:
            give_right = (give_right.astype(F32) + right.astype(F32)).astype(BF)
            give_left = (give_left.astype(F32) + left.astype(F32)).astype(BF)
        right = step_right(give_right, t)
        left = step_left(give_left, t)
    return parts[0].astype(F32) + right.astype(F32) + left.astype(F32)


def exchange_tp(pieces):
    n = lax.axis_size("tp")
    at = lax.axis_index("tp")
    out = jnp.zeros_like(pieces)
    own = lax.dynamic_index_in_dim(pieces, at, 0, False)
    out = lax.dynamic_update_index_in_dim(out, own, at, 0)
    for s in range(1, n):
        piece = lax.dynamic_index_in_dim(pieces, lax.rem(at + s, n), 0, False)
        got = lax.ppermute(piece, "tp", [(i, (i + s) % n) for i in range(n)])
        out = lax.dynamic_update_index_in_dim(out, got, lax.rem(at - s + n, n), 0)
    return out


def gather_tp_in_order(x):
    n = lax.axis_size("tp")
    at = lax.axis_index("tp")
    out = jnp.zeros((n,) + x.shape, x.dtype)
    for s, block in enumerate(gather_tp(x)):
        out = lax.dynamic_update_index_in_dim(out, block, lax.rem(at - s + n, n), 0)
    return out


def sum_all(x):
    for axis in ("ep", "tp"):
        n = lax.axis_size(axis)
        bit = 1
        while bit < n:
            x = x + lax.ppermute(x, axis, [(i, i ^ bit) for i in range(n)])
            bit *= 2
    return x


def body(
    inputs,
    routes,
    norm_gain,
    query_weight,
    key_weight,
    value_weight,
    output_weight,
    mixer_gain,
    router_weight,
    gate_weight,
    up_weight,
    down_weight,
    cotangent,
):
    tokens, width = inputs.shape
    experts = router_weight.shape[1]
    n_ep = lax.axis_size("ep")
    n_tp = lax.axis_size("tp")
    ep_at = lax.axis_index("ep")
    tp_at = lax.axis_index("tp")
    quarter = tokens // n_tp
    scale = HD ** (-0.5)
    heads_width = query_weight.shape[1]
    groups_width = key_weight.shape[1]
    heads_local = heads_width // HD
    groups_local = groups_width // HD

    def mine(x):
        return lax.dynamic_slice_in_dim(x, tp_at * quarter, quarter, 0)

    output_rows = output_weight.shape[0]
    part = output_rows // n_ep
    output_part = lax.dynamic_slice_in_dim(output_weight, ep_at * part, part, 0)
    output_whole = lax.all_gather(output_part, ("tp", "ep"), tiled=True)
    qkv_weight = jnp.concatenate([query_weight, key_weight, value_weight], axis=1)
    part_in = width // n_ep
    qkv_part = lax.dynamic_slice_in_dim(qkv_weight, ep_at * part_in, part_in, 0)
    qkv_whole = lax.all_gather(qkv_part, ("tp", "ep"), tiled=True).reshape(
        n_tp, width, heads_width + 2 * groups_width
    )
    gate_matrix = jnp.concatenate(gather_tp(gate_weight[0]), axis=1)
    up_matrix = jnp.concatenate(gather_tp(up_weight[0]), axis=1)
    down_matrix = jnp.concatenate(gather_tp(down_weight[0]), axis=0)
    routes_mine = mine(routes)
    grad_top_mine = mine(cotangent)
    routes_all = lax.all_gather(routes_mine, "ep")
    if n_ep == 8:
        slots = jnp.bitwise_xor(jnp.arange(n_ep), ep_at)
        routes_all = jnp.take(routes_all, slots, axis=0)
    grad_top_all = gather_ep(grad_top_mine)

    inputs32 = inputs.astype(F32)
    inverse_one = lax.rsqrt(jnp.mean(inputs32 * inputs32, axis=-1, keepdims=True) + EPS)
    unit_one = inputs32 * inverse_one
    normed = (unit_one * norm_gain).astype(BF)
    query_raw = jnp.dot(normed, query_weight, preferred_element_type=F32)
    key_raw = jnp.dot(normed, key_weight, preferred_element_type=F32)
    value_raw = jnp.dot(normed, value_weight, preferred_element_type=F32)
    positions = (jnp.arange(tokens) % LEN).astype(F32)
    cosine, sine = rotary_tables(positions, HD)
    query = rotate(query_raw.reshape(tokens, heads_local, HD), cosine, sine).astype(BF)
    key = rotate(key_raw.reshape(tokens, groups_local, HD), cosine, sine).astype(BF)
    value = value_raw.reshape(tokens, groups_local, HD).astype(BF)
    mixed, logs = attention_forward(query, key, value, scale)

    mixed_mine = exchange_tp(mixed.reshape(n_tp, quarter, heads_width))
    mixed_mine = mixed_mine.transpose(1, 0, 2).reshape(quarter, n_tp * heads_width)
    branch = jnp.dot(mixed_mine, output_whole, preferred_element_type=F32)
    inputs_mine = mine(inputs).astype(F32)
    attended = inputs_mine + branch
    inverse_two = lax.rsqrt(jnp.mean(attended * attended, axis=-1, keepdims=True) + EPS)
    unit_two = attended * inverse_two
    routed_in = (unit_two * mixer_gain).astype(BF)

    def gate_table(rows, chosen_routes):
        logits = jnp.dot(rows, router_weight, preferred_element_type=F32)
        ids = jnp.arange(experts, dtype=jnp.int32)
        chosen = jnp.any(chosen_routes[:, :, None] == ids[None, None, :], axis=1)
        logits = jnp.where(chosen, logits, MASKED)
        weights = jnp.exp(logits - jnp.max(logits, axis=-1, keepdims=True))
        weights = jnp.where(chosen, weights, 0.0)
        return weights / jnp.sum(weights, axis=-1, keepdims=True)

    routed_all = gather_ep(routed_in).reshape(-1, width)
    gates = gate_table(routed_in, routes_mine)
    gates_all = gate_table(routed_all, routes_all.reshape(-1, routes.shape[1]))
    own_gate = lax.dynamic_slice_in_dim(gates_all, ep_at, 1, 1)
    grad_rows = grad_top_all.reshape(-1, width)
    gate_vals = jnp.dot(routed_all, gate_matrix, preferred_element_type=F32)
    up_vals = jnp.dot(routed_all, up_matrix, preferred_element_type=F32)
    sigma = jax.nn.sigmoid(gate_vals)
    active = gate_vals * sigma
    hidden = (active * up_vals).astype(BF)
    expert_out = jnp.dot(hidden, down_matrix, preferred_element_type=F32)
    combined = (own_gate * expert_out).astype(BF)
    grad_gate_own = jnp.sum(grad_rows.astype(F32) * expert_out, axis=-1)
    grad_out = (own_gate * grad_rows.astype(F32)).astype(BF)
    grad_hidden = jnp.dot(grad_out, down_matrix.T, preferred_element_type=F32)
    grad_gate_vals = (grad_hidden * up_vals * sigma * (1.0 + gate_vals * (1.0 - sigma))).astype(BF)
    grad_up_vals = (grad_hidden * active).astype(BF)
    grad_gate_w = jnp.dot(routed_all.T, grad_gate_vals, preferred_element_type=F32).astype(BF)
    grad_up_w = jnp.dot(routed_all.T, grad_up_vals, preferred_element_type=F32).astype(BF)
    grad_down_w = jnp.dot(hidden.T, grad_out, preferred_element_type=F32).astype(BF)
    grad_in = (
        jnp.dot(grad_gate_vals, gate_matrix.T, preferred_element_type=F32)
        + jnp.dot(grad_up_vals, up_matrix.T, preferred_element_type=F32)
    ).astype(BF)

    combined_mine = scatter_ep(combined.reshape(n_ep, quarter, width))
    result_mine = (attended + combined_mine).astype(BF)
    result = gather_tp_in_order(result_mine).reshape(tokens, width)
    grad_gates = lax.all_to_all(
        grad_gate_own.reshape(n_ep, quarter), "ep", split_axis=0, concat_axis=0, tiled=True
    ) if n_ep != 8 else None
    if grad_gates is None:
        ordered = jnp.take(grad_gate_own.reshape(n_ep, quarter), slots, axis=0)
        grad_gates = lax.all_to_all(ordered, "ep", split_axis=0, concat_axis=0, tiled=True)
    grad_gates = grad_gates.T
    grad_routed_part = scatter_ep(grad_in.reshape(n_ep, quarter, width))
    inner_gate = jnp.sum(gates * grad_gates, axis=-1, keepdims=True)
    grad_logits = (gates * (grad_gates - inner_gate)).astype(BF)
    grad_router = jnp.dot(routed_in.T, grad_logits, preferred_element_type=F32)
    grad_routed = grad_routed_part + jnp.dot(
        grad_logits, router_weight.T, preferred_element_type=F32
    )
    grad_top = grad_top_mine.astype(F32)
    grad_mixer = jnp.sum(grad_routed * unit_two, axis=0)
    scaled_two = grad_routed * mixer_gain
    grad_attended = grad_top + inverse_two * (
        scaled_two - unit_two * jnp.mean(scaled_two * unit_two, axis=-1, keepdims=True)
    )
    grad_branch = grad_attended.astype(BF)
    grad_mixed_mine = jnp.dot(grad_branch, output_whole.T, preferred_element_type=F32).astype(BF)
    grad_mixed = exchange_tp(
        grad_mixed_mine.reshape(quarter, n_tp, heads_width).transpose(1, 0, 2)
    ).reshape(tokens, heads_local, HD)

    hidden_part = gate_weight.shape[2]

    def cut(x, axis):
        return [
            lax.slice_in_dim(x, s * hidden_part, (s + 1) * hidden_part, axis=axis)
            for s in range(n_tp)
        ]

    grad_gate_w = scatter_tp(cut(grad_gate_w, 1))
    grad_up_w = scatter_tp(cut(grad_up_w, 1))
    grad_down_w = scatter_tp(cut(grad_down_w, 0))

    grad_output = jnp.dot(mixed_mine.T, grad_branch, preferred_element_type=F32).astype(BF)
    grad_output = grad_output.reshape(n_tp, n_ep, part, width).transpose(1, 0, 2, 3)
    grad_output = lax.psum_scatter(
        grad_output.reshape(n_ep, n_tp * part, width), "ep", scatter_dimension=0, tiled=False
    )
    grad_output = lax.psum_scatter(
        grad_output.reshape(n_tp, part, width), "tp", scatter_dimension=0, tiled=False
    )
    grad_output = lax.all_gather(grad_output, "ep", tiled=True).astype(F32)

    grad_query_rot, grad_key_rot, grad_value_f = attention_backward(
        query, key, value, logs, grad_mixed, scale
    )
    grad_query = unrotate(grad_query_rot, cosine, sine).astype(BF).reshape(tokens, heads_width)
    grad_key = unrotate(grad_key_rot, cosine, sine).astype(BF).reshape(tokens, groups_width)
    grad_value = grad_value_f.astype(BF).reshape(tokens, groups_width)
    grad_qkv = jnp.concatenate([grad_query, grad_key, grad_value], axis=1)
    grad_qkv_w = jnp.dot(normed.T, grad_qkv, preferred_element_type=F32).astype(BF)
    grad_qkv_w = lax.psum(grad_qkv_w, "ep").astype(F32)

    grad_qkv_mine = exchange_tp(grad_qkv.reshape(n_tp, quarter, -1))
    grad_normed = jnp.einsum("jtc,jdc->td", grad_qkv_mine, qkv_whole, preferred_element_type=F32)
    inverse_mine = mine(inverse_one)
    unit_mine = inputs_mine * inverse_mine
    grad_norm = jnp.sum(grad_normed * unit_mine, axis=0)
    scaled_one = grad_normed * norm_gain
    grad_inputs_mine = grad_attended + inverse_mine * (
        scaled_one - unit_mine * jnp.mean(scaled_one * unit_mine, axis=-1, keepdims=True)
    )
    grad_inputs = gather_tp_in_order(grad_inputs_mine.astype(BF)).reshape(tokens, width)
    small = sum_all(jnp.concatenate([grad_mixer[None], grad_router.T], axis=0))
    grad_norm = sum_all(grad_norm[None])[0]
    return (
        result,
        grad_inputs,
        grad_norm,
        grad_qkv_w[:, :heads_width],
        grad_qkv_w[:, heads_width : heads_width + groups_width],
        grad_qkv_w[:, heads_width + groups_width :],
        grad_output,
        small[0],
        small[1:].T,
        grad_gate_w[None],
        grad_up_w[None],
        grad_down_w[None],
    )


def solution(mesh):
    placed = (
        P("ep", None),
        P("ep", None),
        P(),
        P(None, "tp"),
        P(None, "tp"),
        P(None, "tp"),
        P("tp", None),
        P(),
        P(),
        P("ep", None, "tp"),
        P("ep", None, "tp"),
        P("ep", "tp", None),
        P("ep", None),
    )
    return jax.shard_map(
        body,
        mesh=mesh,
        in_specs=placed,
        out_specs=(
            P("ep", None),
            P("ep", None),
            P(),
            P(None, "tp"),
            P(None, "tp"),
            P(None, "tp"),
            P("tp", None),
            P(),
            P(),
            P("ep", None, "tp"),
            P("ep", None, "tp"),
            P("ep", "tp", None),
        ),
        check_vma=False,
    )
```

```python
import functools

import jax
import jax.numpy as jnp
from jax import lax
from jax.experimental import pallas as pl
from jax.experimental.pallas import tpu as pltpu
from jax.sharding import PartitionSpec as P

HD = 64
LEN = 1024
EPS = 1e-06
MASKED = -1e30
BF = jnp.bfloat16
F32 = jnp.float32
BLOCK = 256
LANES = 128
NT = (((1,), (1,)), ((), ()))
TN = (((0,), (0,)), ((), ()))


def mul(a, b, dims=(((1,), (0,)), ((), ()))):
    return lax.dot_general(a, b, dims, preferred_element_type=F32)


def rotate_lanes(y, cos, sin_a, sin_b):
    return y * cos + pltpu.roll(y, 128 - HD // 2, 1) * sin_a + pltpu.roll(y, HD // 2, 1) * sin_b


def rotary_lanes(tokens):
    positions = (jnp.arange(tokens) % LEN).astype(F32)
    lane = jnp.arange(128)
    freqs = 10000.0 ** (-(lane % (HD // 2)).astype(F32) * 2.0 / HD)
    angles = positions[:, None] * freqs[None, :]
    cos, sin = jnp.cos(angles), jnp.sin(angles)
    first = (lane % HD < HD // 2)[None, :]
    return cos, jnp.where(first, -sin, 0.0), jnp.where(first, 0.0, sin)


def causal(block):
    key_at = lax.broadcasted_iota(jnp.int32, (block, block), 0)
    query_at = lax.broadcasted_iota(jnp.int32, (block, block), 1)
    return key_at <= query_at


def attend_kernel(at_ref, x_ref, gain_ref, w_ref, cos_ref, sin_a_ref, sin_b_ref, *refs):
    pieces, (normed_ref, q_ref, k_ref, v_ref, log_ref, vt_ref, out_ref) = refs[:-7], refs[-7:]
    tokens = x_ref.shape[0]
    heads, groups = q_ref.shape[0], k_ref.shape[0]
    repeat = heads // groups
    per = 128 // HD
    scale = HD ** (-0.5)

    @pl.loop(0, tokens // BLOCK)
    def _(i):
        at = pl.multiple_of(i * BLOCK, BLOCK)
        rows = pl.ds(at, BLOCK)
        x = x_ref[rows, :].astype(F32)
        inverse = lax.rsqrt(jnp.mean(x * x, axis=-1, keepdims=True) + EPS)
        normed = (x * inverse * gain_ref[...]).astype(BF)
        normed_ref[rows, :] = normed
        raw = mul(normed, w_ref[...])
        tables = (cos_ref[rows, :], sin_a_ref[rows, :], sin_b_ref[rows, :])
        for h in range(0, heads, per):
            turned = rotate_lanes(raw[:, h * HD : h * HD + 128], *tables) * scale
            for u in range(per):
                q_ref[h + u, rows, :] = turned[:, u * HD : (u + 1) * HD].astype(BF)
        for g in range(0, groups, per):
            lane = (heads + g) * HD
            turned = rotate_lanes(raw[:, lane : lane + 128], *tables)
            lane = (heads + groups + g) * HD
            value = raw[:, lane : lane + 128]
            turned_value = value.T
            for u in range(per):
                k_ref[g + u, rows, :] = turned[:, u * HD : (u + 1) * HD].astype(BF)
                v_ref[g + u, rows, :] = value[:, u * HD : (u + 1) * HD].astype(BF)
                vt_ref[g + u, :, rows] = turned_value[u * HD : (u + 1) * HD].astype(BF)

    keep = causal(BLOCK)

    @pl.loop(0, heads)
    def _(h):
        g = h // repeat
        for i in range(tokens // BLOCK):
            start, stop = i * BLOCK, (i + 1) * BLOCK
            query = q_ref[h, start:stop, :]
            parts = [jnp.where(keep, mul(k_ref[g, start:stop, :], query, NT), MASKED)]
            if i:
                parts.append(mul(k_ref[g, :start, :], query, NT))
            peak = jnp.max(parts[0], axis=0, keepdims=True)
            for part in parts[1:]:
                peak = jnp.maximum(peak, jnp.max(part, axis=0, keepdims=True))
            weights = [jnp.exp(part - peak) for part in parts]
            total = sum(jnp.sum(w, axis=0, keepdims=True) for w in weights)
            shrink = 1.0 / total
            mixed = mul(vt_ref[g, :, start:stop], (weights[0] * shrink).astype(BF))
            if i:
                mixed += mul(vt_ref[g, :, :start], (weights[1] * shrink).astype(BF))
            out_ref[h, :, start:stop] = mixed
            log_ref[h, :, start:stop] = peak + jnp.log(total)

    for s, piece_ref in enumerate(pieces):
        span = pl.ds(pl.multiple_of(lax.rem(at_ref[0] + s, len(pieces)) * BLOCK, BLOCK), BLOCK)
        for h in range(0, heads, per):
            pair = jnp.concatenate([out_ref[h + u, :, span] for u in range(per)], axis=0)
            piece_ref[:, h * HD : h * HD + 128] = pair.T.astype(BF)


VMEM = pl.BlockSpec(memory_space=pltpu.VMEM)
SMEM = pl.BlockSpec(memory_space=pltpu.SMEM)


def attend(x, gain, weight, tables, heads, groups, at):
    tokens, width = x.shape
    count = tokens // BLOCK
    return pl.pallas_call(
        attend_kernel,
        in_specs=[SMEM] + [VMEM] * 6,
        out_shape=[jax.ShapeDtypeStruct((BLOCK, heads * HD), BF)] * count
        + [
            jax.ShapeDtypeStruct((tokens, width), BF),
            jax.ShapeDtypeStruct((heads, tokens, HD), BF),
            jax.ShapeDtypeStruct((groups, tokens, HD), BF),
            jax.ShapeDtypeStruct((groups, tokens, HD), BF),
            jax.ShapeDtypeStruct((heads, 1, tokens), F32),
        ],
        scratch_shapes=[pltpu.VMEM((groups, HD, tokens), BF), pltpu.VMEM((heads, HD, tokens), F32)],
        compiler_params=pltpu.CompilerParams(vmem_limit_bytes=48 << 20),
        cost_estimate=pl.CostEstimate(
            flops=2 * tokens * width * weight.shape[1] + 3 * heads * tokens * tokens * HD,
            bytes_accessed=6 * tokens * width,
            transcendentals=heads * tokens * tokens // 2,
        ),
    )(at[None], x, gain[None], weight, *tables)


def attend_back_kernel(at_ref, q_ref, k_ref, v_ref, log_ref, cos_ref, sin_a_ref, sin_b_ref, *refs):
    do_ref, kt_ref, dq_ref, dk_ref, dv_ref = refs[-5:]
    out_ref = refs[-6]
    count = (len(refs) - 6) // 2
    grad_refs, pieces = refs[:count], refs[count : 2 * count]
    tokens = q_ref.shape[1]
    heads, groups = q_ref.shape[0], k_ref.shape[0]
    repeat = heads // groups
    per = 128 // HD
    scale = HD ** (-0.5)
    dk_ref[...] = jnp.zeros_like(dk_ref)
    dv_ref[...] = jnp.zeros_like(dv_ref)

    def span_of(s):
        return pl.ds(pl.multiple_of(lax.rem(at_ref[0] + s, count) * BLOCK, BLOCK), BLOCK)

    for s, grad_ref in enumerate(grad_refs):
        for h in range(heads):
            do_ref[h, span_of(s), :] = grad_ref[:, h * HD : (h + 1) * HD]

    @pl.loop(0, tokens // BLOCK)
    def _(i):
        rows = pl.ds(pl.multiple_of(i * BLOCK, BLOCK), BLOCK)
        for g in range(groups):
            kt_ref[g, :, rows] = k_ref[g, rows, :].astype(F32).T.astype(BF)

    keep = causal(BLOCK)

    @pl.loop(0, heads)
    def _(h):
        g = h // repeat
        for i in range(tokens // BLOCK):
            start, stop = i * BLOCK, (i + 1) * BLOCK
            query = q_ref[h, start:stop, :]
            grads = do_ref[h, start:stop, :]
            log_total = log_ref[h, :, start:stop]
            spans = [(start, stop)] + ([(0, start)] if i else [])
            probs, grad_probs = [], []
            for lo, hi in spans:
                scores = mul(k_ref[g, lo:hi, :], query, NT)
                if hi == stop:
                    scores = jnp.where(keep, scores, MASKED)
                probs.append(jnp.exp(scores - log_total))
                grad_probs.append(mul(v_ref[g, lo:hi, :], grads, NT))
            inner = sum(jnp.sum(p * d, axis=0, keepdims=True) for p, d in zip(probs, grad_probs))
            dq = None
            for (lo, hi), p, d in zip(spans, probs, grad_probs):
                ds = (p * (d - inner)).astype(BF)
                dk_ref[g, lo:hi, :] += mul(ds, query)
                dv_ref[g, lo:hi, :] += mul(p.astype(BF), grads)
                term = mul(kt_ref[g, :, lo:hi], ds)
                dq = term if dq is None else dq + term
            dq_ref[h, :, start:stop] = dq * scale

    @pl.loop(0, tokens // BLOCK)
    def _(i):
        rows = pl.ds(pl.multiple_of(i * BLOCK, BLOCK), BLOCK)
        tables = (cos_ref[rows, :], -sin_a_ref[rows, :], -sin_b_ref[rows, :])
        for h in range(0, heads, per):
            pair = jnp.concatenate([dq_ref[h + u, :, rows] for u in range(per)], axis=0).T
            out_ref[rows, h * HD : h * HD + 128] = rotate_lanes(pair, *tables).astype(BF)
        for g in range(0, groups, per):
            pair = jnp.concatenate([dk_ref[g + u, rows, :] for u in range(per)], axis=1)
            lane = (heads + g) * HD
            out_ref[rows, lane : lane + 128] = rotate_lanes(pair, *tables).astype(BF)
            pair = jnp.concatenate([dv_ref[g + u, rows, :] for u in range(per)], axis=1)
            lane = (heads + groups + g) * HD
            out_ref[rows, lane : lane + 128] = pair.astype(BF)

    for s, piece_ref in enumerate(pieces):
        piece_ref[...] = out_ref[span_of(s), :]


def attend_back(grad_pieces, q, k, v, logs, tables, at):
    heads, tokens, _ = q.shape
    groups = k.shape[0]
    count = len(grad_pieces)
    lanes = (heads + 2 * groups) * HD
    return pl.pallas_call(
        attend_back_kernel,
        in_specs=[SMEM] + [VMEM] * (7 + count),
        out_shape=[jax.ShapeDtypeStruct((BLOCK, lanes), BF)] * count + [jax.ShapeDtypeStruct((tokens, lanes), BF)],
        scratch_shapes=[
            pltpu.VMEM((heads, tokens, HD), BF),
            pltpu.VMEM((groups, HD, tokens), BF),
            pltpu.VMEM((heads, HD, tokens), F32),
            pltpu.VMEM((groups, tokens, HD), F32),
            pltpu.VMEM((groups, tokens, HD), F32),
        ],
        compiler_params=pltpu.CompilerParams(vmem_limit_bytes=48 << 20),
        cost_estimate=pl.CostEstimate(
            flops=6 * heads * tokens * tokens * HD,
            bytes_accessed=6 * tokens * heads * HD,
            transcendentals=heads * tokens * tokens // 2,
        ),
    )(at[None], q, k, v, logs, *tables, *grad_pieces)


def expert_kernel(order_ref, rows_ref, extra_ref, router_ref, gu_ref, down_ref, out_ref, gin_ref, wgu_ref, wdown_ref, agu, adown, *, top):
    step = pl.program_id(0)
    steps = pl.num_programs(0)
    hidden_width, width = down_ref.shape
    own = order_ref[steps]
    experts = order_ref[steps + 1]

    @pl.when(step == 0)
    def _():
        agu[...] = jnp.zeros_like(agu)
        adown[...] = jnp.zeros_like(adown)

    rows = rows_ref[...]
    grads32 = extra_ref[:, :width].astype(F32)
    named = extra_ref[:, width:].astype(F32)

    lane = lax.broadcasted_iota(jnp.int32, (rows.shape[0], LANES), 1)
    lane32 = lane.astype(F32)
    chosen = lane32 == named[:, 0:1]
    for k in range(1, top):
        chosen = chosen | (lane32 == named[:, k : k + 1])
    logits = jnp.where(chosen, mul(rows, router_ref[...]), MASKED)
    weights = jnp.where(chosen, jnp.exp(logits - jnp.max(logits, axis=-1, keepdims=True)), 0.0)
    mine = jnp.sum(jnp.where(lane == own, weights, 0.0), axis=-1, keepdims=True)
    gate = mine / jnp.sum(weights, axis=-1, keepdims=True)

    both = mul(rows, gu_ref[...], NT)
    gate_vals = both[:, :hidden_width]
    up_vals = both[:, hidden_width:]
    sigma = jax.nn.sigmoid(gate_vals)
    active = gate_vals * sigma
    hidden = (active * up_vals).astype(BF)
    grad_out = (gate * grads32).astype(BF)
    grad_hidden = mul(grad_out, down_ref[...], NT)
    expert_out = mul(hidden, down_ref[...])
    out_ref[...] = (gate * expert_out).astype(BF)
    score = jnp.sum(grads32 * expert_out, axis=-1, keepdims=True)
    high = score.astype(BF).astype(F32)
    scores = jnp.where(lane == own, high, jnp.where(lane == own + experts, score - high, 0.0))
    gin_ref[:, width:] = scores.astype(BF)
    grad_gate_vals = (grad_hidden * up_vals * sigma * (1.0 + gate_vals * (1.0 - sigma))).astype(BF)
    grad_up_vals = (grad_hidden * active).astype(BF)
    grad_both = jnp.concatenate([grad_gate_vals, grad_up_vals], axis=1)
    gin_ref[:, :width] = mul(grad_both, gu_ref[...]).astype(BF)
    agu[...] += mul(grad_both, rows, TN)
    adown[...] += mul(hidden, grad_out, TN)

    @pl.when(step == steps - 1)
    def _():
        wgu_ref[...] = agu[...].astype(BF)
        wdown_ref[...] = adown[...].astype(BF)


def run_experts(order, rows, extra, router, gate_up, down, top):
    count, width = rows.shape
    wide = extra.shape[1]
    hidden = down.shape[0]
    whole_gu = pl.BlockSpec((2 * hidden, width), lambda i, o: (0, 0))
    whole_down = pl.BlockSpec((hidden, width), lambda i, o: (0, 0))
    by_slot = pl.BlockSpec((BLOCK, width), lambda i, o: (i, 0))
    return pl.pallas_call(
        functools.partial(expert_kernel, top=top),
        grid_spec=pltpu.PrefetchScalarGridSpec(
            num_scalar_prefetch=1,
            grid=(count // BLOCK,),
            in_specs=[
                by_slot,
                pl.BlockSpec((BLOCK, wide), lambda i, o: (o[i], 0)),
                pl.BlockSpec((width, LANES), lambda i, o: (0, 0)),
                whole_gu,
                whole_down,
            ],
            out_specs=[by_slot, pl.BlockSpec((BLOCK, wide), lambda i, o: (i, 0)), whole_gu, whole_down],
            scratch_shapes=[pltpu.VMEM((2 * hidden, width), F32), pltpu.VMEM((hidden, width), F32)],
        ),
        out_shape=[
            jax.ShapeDtypeStruct((count, width), BF),
            jax.ShapeDtypeStruct((count, wide), BF),
            jax.ShapeDtypeStruct((2 * hidden, width), BF),
            jax.ShapeDtypeStruct((hidden, width), BF),
        ],
        compiler_params=pltpu.CompilerParams(vmem_limit_bytes=58 << 20),
        cost_estimate=pl.CostEstimate(
            flops=18 * count * width * hidden,
            bytes_accessed=8 * count * width + 18 * hidden * width,
            transcendentals=count * hidden,
        ),
    )(order, rows, extra, router, gate_up, down)


def after(x, *others):
    return lax.optimization_barrier((x, others))[0]


def swap(x, bit):
    return lax.ppermute(x, "ep", [(i, i ^ bit) for i in range(lax.axis_size("ep"))])


def turn(x, by):
    n = lax.axis_size("tp")
    return lax.ppermute(x, "tp", [(i, (i + by) % n) for i in range(n)])


def gather_ep(x):
    n = lax.axis_size("ep")
    if n != 8:
        whole = lax.all_gather(x, "ep")
        return [whole[k] for k in range(n)]
    first = [x] + [swap(x, k) for k in (2, 4, 6)]
    second = [swap(v, 1) for v in first]
    return [v for pair in zip(first, second) for v in pair]


def scatter_slots(x):
    if lax.axis_size("ep") != 8:
        return lax.psum_scatter(x, "ep", scatter_dimension=0, tiled=False).astype(F32)
    other = swap(x[1::2], 1)
    mine = (x[0::2].astype(F32) + other.astype(F32)).astype(BF)
    got = [mine[0]] + [swap(mine[j], 2 * j) for j in (1, 2, 3)]
    return sum(v.astype(F32) for v in got)


def scatter_devices(x):
    n = lax.axis_size("ep")
    if n != 8:
        return lax.psum_scatter(x, "ep", scatter_dimension=0, tiled=False).astype(F32)
    at = lax.axis_index("ep")
    core, chip = lax.rem(at, 2), lax.div(at, 2)
    x = x.reshape((n // 2, 2) + x.shape[1:])
    other = swap(lax.dynamic_index_in_dim(x, 1 - core, 1, False), 1)
    mine = lax.dynamic_index_in_dim(x, core, 1, False)
    mine = (mine.astype(F32) + other.astype(F32)).astype(BF)

    def of(j):
        return lax.dynamic_index_in_dim(mine, jnp.bitwise_xor(chip, j), 0, False)

    got = [of(0)] + [swap(of(j), 2 * j) for j in (1, 2, 3)]
    return sum(v.astype(F32) for v in got)


def slot_devices():
    n = lax.axis_size("ep")
    order = jnp.arange(n, dtype=jnp.int32)
    return jnp.bitwise_xor(order, lax.axis_index("ep")) if n == 8 else order


def in_device_order(blocks, shape, put):
    order = slot_devices()
    out = jnp.zeros(shape, blocks[0].dtype)
    for k, block in enumerate(blocks):
        out = put(out, block, order[k])
    return out


def step_right(x, upto=None):
    n = lax.axis_size("tp")
    return lax.ppermute(x, "tp", [(i, i + 1) for i in range(n - 1 if upto is None else upto)])


def step_left(x, upto=None):
    n = lax.axis_size("tp")
    return lax.ppermute(x, "tp", [(n - 1 - i, n - 2 - i) for i in range(n - 1 if upto is None else upto)])


def meet(at, right, left):
    n = lax.axis_size("tp")
    return [right[0]] + [jnp.where(at >= s, right[s], left[n - s]) for s in range(1, n)]


def body(
    inputs,
    routes,
    norm_gain,
    query_weight,
    key_weight,
    value_weight,
    output_weight,
    mixer_gain,
    router_weight,
    gate_weight,
    up_weight,
    down_weight,
    cotangent,
):
    tokens, width = inputs.shape
    experts = router_weight.shape[1]
    top = routes.shape[1]
    n_ep = lax.axis_size("ep")
    n_tp = lax.axis_size("tp")
    ep_at = lax.axis_index("ep").astype(jnp.int32)
    tp_at = lax.axis_index("tp").astype(jnp.int32)
    quarter = tokens // n_tp
    heads_width = query_weight.shape[1]
    groups_width = key_weight.shape[1]

    def mine(x):
        return lax.dynamic_slice_in_dim(x, tp_at * quarter, quarter, 0)

    hidden_part = gate_weight.shape[2]
    expert_part = jnp.concatenate([gate_weight[0].T, up_weight[0].T, down_weight[0]], axis=0)
    right, left = [expert_part], [expert_part]
    right.append(step_right(expert_part))
    left.append(step_left(expert_part))

    part = output_weight.shape[0] // n_ep
    output_part = lax.dynamic_slice_in_dim(output_weight, ep_at * part, part, 0)
    output_part = jnp.stack([output_part] + [turn(output_part, s) for s in range(1, n_tp)])

    routes_mine = mine(routes)
    grad_top_mine = mine(cotangent)
    named = jnp.pad(routes_mine.astype(BF), ((0, 0), (0, LANES - top)), constant_values=-1.0)
    extra = jnp.concatenate([grad_top_mine, named], axis=1)
    extra_all = lax.all_gather(extra, "ep", tiled=True)

    qkv_weight = jnp.concatenate([query_weight, key_weight, value_weight], axis=1)
    tables = rotary_lanes(tokens)
    *mixed, normed, query, key, value, logs = attend(
        inputs, norm_gain, qkv_weight, tables, heads_width // HD, groups_width // HD, tp_at
    )
    mixed = [mixed[0]] + [turn(mixed[s], s) for s in range(1, n_tp)]

    output_blocks = gather_ep(output_part)
    output_whole = in_device_order(
        output_blocks,
        (n_tp, n_ep, part, width),
        lambda out, block, at: lax.dynamic_update_slice(out, block[:, None], (0, at, 0, 0)),
    ).reshape(n_tp * heads_width, width)

    mixed_mine = jnp.concatenate(mixed, axis=1)
    branch = mul(mixed_mine, output_whole)
    inputs_mine = mine(inputs).astype(F32)
    attended = inputs_mine + branch
    inverse_two = lax.rsqrt(jnp.mean(attended * attended, axis=-1, keepdims=True) + EPS)
    unit_two = attended * inverse_two
    routed_in = (unit_two * mixer_gain).astype(BF)

    right[1], left[1] = after((right[1], left[1]), mixed)
    for _ in range(2, n_tp):
        right.append(step_right(right[-1]))
        left.append(step_left(left[-1]))
    expert_parts = meet(tp_at, right, left)
    gate_up = jnp.concatenate(
        [w[:hidden_part] for w in expert_parts] + [w[hidden_part : 2 * hidden_part] for w in expert_parts], axis=0
    )
    down = jnp.concatenate([w[2 * hidden_part :] for w in expert_parts], axis=0)

    routed_all = jnp.concatenate(gather_ep(routed_in), axis=0)
    router = jnp.pad(router_weight, ((0, 0), (0, LANES - experts)))
    order = jnp.concatenate([slot_devices(), ep_at[None], jnp.full((1,), experts, jnp.int32)])
    combined, grad_in, grad_gate_up, grad_down = run_experts(
        order, routed_all, extra_all, router, gate_up, down, top
    )
    logits = mul(routed_in, router_weight)
    ids = jnp.arange(experts, dtype=jnp.int32)
    chosen = jnp.any(routes_mine[:, :, None] == ids[None, None, :], axis=1)
    logits = jnp.where(chosen, logits, MASKED)
    weights = jnp.where(chosen, jnp.exp(logits - jnp.max(logits, axis=-1, keepdims=True)), 0.0)
    gates = weights / jnp.sum(weights, axis=-1, keepdims=True)

    grad_in = scatter_slots(grad_in.reshape(n_ep, quarter, -1))
    grad_gates = grad_in[:, width : width + experts] + grad_in[:, width + experts : width + 2 * experts]
    inner_gate = jnp.sum(gates * grad_gates, axis=-1, keepdims=True)
    grad_logits = (gates * (grad_gates - inner_gate)).astype(BF)
    grad_routed = grad_in[:, :width] + mul(grad_logits, router_weight, NT)
    grad_top = grad_top_mine.astype(F32)
    scaled_two = grad_routed * mixer_gain
    grad_attended = grad_top + inverse_two * (
        scaled_two - unit_two * jnp.mean(scaled_two * unit_two, axis=-1, keepdims=True)
    )
    grad_branch = grad_attended.astype(BF)
    grad_mixed = mul(grad_branch, output_whole, NT).astype(BF)
    grad_mixed = [grad_mixed[:, s * heads_width : (s + 1) * heads_width] for s in range(n_tp)]
    grad_mixed = [grad_mixed[0]] + [turn(grad_mixed[s], -s) for s in range(1, n_tp)]

    hidden_all = n_tp * hidden_part

    def term(s):
        at = s * hidden_part
        return jnp.concatenate(
            [
                grad_gate_up[at : at + hidden_part],
                grad_gate_up[hidden_all + at : hidden_all + at + hidden_part],
                grad_down[at : at + hidden_part],
            ],
            axis=0,
        )

    terms = [term(s) for s in range(n_tp)]
    go_right = go_left = None
    for t in range(1, n_tp):
        give_right, give_left = terms[t], terms[n_tp - t]
        if go_right is not None:
            give_right = (give_right.astype(F32) + go_right.astype(F32)).astype(BF)
            give_left = (give_left.astype(F32) + go_left.astype(F32)).astype(BF)
        if t == n_tp - 1:
            give_right, give_left = after((give_right, give_left), grad_mixed)
        go_right = step_right(give_right, t)
        go_left = step_left(give_left, t)
    grad_expert = terms[0].astype(F32) + go_right.astype(F32) + go_left.astype(F32)
    grad_gate_w = grad_expert[:hidden_part].T
    grad_up_w = grad_expert[hidden_part : 2 * hidden_part].T
    grad_down_w = grad_expert[2 * hidden_part :]

    combined = after(combined, grad_branch)
    combined_mine = scatter_slots(combined.reshape(n_ep, quarter, width))
    result_mine = (attended + combined_mine).astype(BF)
    result = lax.all_gather(result_mine, "tp", tiled=True)

    *grad_qkv, grad_qkv_all = attend_back(grad_mixed, query, key, value, logs, tables, tp_at)
    grad_qkv = [grad_qkv[0]] + [turn(grad_qkv[s], s) for s in range(1, n_tp)]
    grad_qkv_w = mul(normed, grad_qkv_all, TN).astype(BF)
    grad_qkv_w = lax.psum(grad_qkv_w, "ep").astype(F32)

    grad_router = mul(routed_in, grad_logits, TN)
    grad_mixer = jnp.sum(grad_routed * unit_two, axis=0)
    few = -(-(1 + experts) // n_ep)
    few_pad = -(-few // 16) * 16
    small = jnp.concatenate([grad_mixer[None], grad_router.T], axis=0).astype(BF)
    small = jnp.pad(small, ((0, few * n_ep - 1 - experts), (0, 0))).reshape(n_ep, few, width)
    small = jnp.pad(small, ((0, 0), (0, few_pad - few), (0, 0)))
    grad_output = mul(mixed_mine, grad_branch, TN).astype(BF)
    grad_output = grad_output.reshape(n_tp, n_ep, part, width).transpose(1, 0, 2, 3)
    grad_output = jnp.concatenate([grad_output.reshape(n_ep, n_tp * part, width), small], axis=1)
    grad_output = scatter_devices(grad_output).astype(BF)
    pieces = [
        jnp.concatenate([grad_output[s * part : (s + 1) * part], grad_output[n_tp * part :]], axis=0)
        for s in range(n_tp)
    ]
    pieces = [pieces[0]] + [turn(pieces[s], -s) for s in range(1, n_tp)]
    grad_output = sum(v.astype(F32) for v in pieces).astype(BF)
    grad_output = in_device_order(
        gather_ep(grad_output),
        (n_ep, part + few_pad, width),
        lambda out, block, at: lax.dynamic_update_index_in_dim(out, block, at, 0),
    )
    small = grad_output[:, part : part + few].reshape(n_ep * few, width)[: 1 + experts].astype(F32)
    grad_output = grad_output[:, :part].reshape(heads_width, width).astype(F32)

    part_in = width // n_ep
    qkv_part = lax.dynamic_slice_in_dim(qkv_weight, ep_at * part_in, part_in, 0)
    qkv_part = after(qkv_part, routed_in)
    qkv_whole = lax.all_gather(qkv_part, ("tp", "ep"), tiled=True).reshape(n_tp, width, -1)
    grad_normed = sum(
        mul(grad_qkv[s], lax.dynamic_index_in_dim(qkv_whole, lax.rem(tp_at - s + n_tp, n_tp), 0, False), NT)
        for s in range(n_tp)
    )
    inverse_one = lax.rsqrt(jnp.mean(inputs_mine * inputs_mine, axis=-1, keepdims=True) + EPS)
    unit_one = inputs_mine * inverse_one
    grad_norm = jnp.sum(grad_normed * unit_one, axis=0)
    scaled_one = grad_normed * norm_gain
    grad_inputs = grad_attended + inverse_one * (
        scaled_one - unit_one * jnp.mean(scaled_one * unit_one, axis=-1, keepdims=True)
    )
    grad_inputs = grad_inputs.astype(BF)
    right, left = [grad_inputs], [grad_inputs]
    for _ in range(1, n_tp):
        right.append(step_right(right[-1]))
        left.append(step_left(left[-1]))
    grad_inputs = jnp.zeros((tokens, width), BF)
    for s, block in enumerate(meet(tp_at, right, left)):
        grad_inputs = lax.dynamic_update_slice(
            grad_inputs, block, (lax.rem(tp_at - s + n_tp, n_tp) * quarter, 0)
        )
    grad_norm = grad_norm[None]
    for axis in ("ep", "tp"):
        n = lax.axis_size(axis)
        bit = 1
        while bit < n:
            grad_norm = grad_norm + lax.ppermute(grad_norm, axis, [(i, i ^ bit) for i in range(n)])
            bit *= 2
    return (
        result,
        grad_inputs,
        grad_norm[0],
        grad_qkv_w[:, :heads_width],
        grad_qkv_w[:, heads_width : heads_width + groups_width],
        grad_qkv_w[:, heads_width + groups_width :],
        grad_output,
        small[0],
        small[1:].T,
        grad_gate_w[None],
        grad_up_w[None],
        grad_down_w[None],
    )


def solution(mesh):
    placed = (
        P("ep", None),
        P("ep", None),
        P(),
        P(None, "tp"),
        P(None, "tp"),
        P(None, "tp"),
        P("tp", None),
        P(),
        P(),
        P("ep", None, "tp"),
        P("ep", None, "tp"),
        P("ep", "tp", None),
        P("ep", None),
    )
    return jax.shard_map(
        body,
        mesh=mesh,
        in_specs=placed,
        out_specs=(
            P("ep", None),
            P("ep", None),
            P(),
            P(None, "tp"),
            P(None, "tp"),
            P(None, "tp"),
            P("tp", None),
            P(),
            P(),
            P("ep", None, "tp"),
            P("ep", None, "tp"),
            P("ep", "tp", None),
        ),
        check_vma=False,
    )
```

```python
import functools

import jax
import jax.numpy as jnp
from jax import lax
from jax.experimental import pallas as pl
from jax.experimental.pallas import tpu as pltpu
from jax.sharding import PartitionSpec as P

HD = 64
LEN = 1024
EPS = 1e-06
MASKED = -1e30
BF = jnp.bfloat16
F32 = jnp.float32
BLOCK = 256
LANES = 128
NT = (((1,), (1,)), ((), ()))
TN = (((0,), (0,)), ((), ()))


def takes(us):
    return pl.CostEstimate(flops=int(us * 1.15e9), bytes_accessed=0, transcendentals=0)


def mul(a, b, dims=(((1,), (0,)), ((), ()))):
    return lax.dot_general(a, b, dims, preferred_element_type=F32)


def rotate_lanes(y, cos, sin_a, sin_b):
    return y * cos + pltpu.roll(y, 128 - HD // 2, 1) * sin_a + pltpu.roll(y, HD // 2, 1) * sin_b


def rotary_lanes(tokens):
    positions = (jnp.arange(tokens) % LEN).astype(F32)
    lane = jnp.arange(128)
    freqs = 10000.0 ** (-(lane % (HD // 2)).astype(F32) * 2.0 / HD)
    angles = positions[:, None] * freqs[None, :]
    cos, sin = jnp.cos(angles), jnp.sin(angles)
    first = (lane % HD < HD // 2)[None, :]
    return cos, jnp.where(first, -sin, 0.0), jnp.where(first, 0.0, sin)


def causal(block):
    key_at = lax.broadcasted_iota(jnp.int32, (block, block), 0)
    query_at = lax.broadcasted_iota(jnp.int32, (block, block), 1)
    return key_at <= query_at


def attend_kernel(x_ref, gain_ref, w_ref, cos_ref, sin_a_ref, sin_b_ref, mixed_ref, normed_ref, q_ref, k_ref, v_ref, log_ref, vt_ref, out_ref):
    tokens = x_ref.shape[0]
    heads, groups = q_ref.shape[0], k_ref.shape[0]
    repeat = heads // groups
    per = 128 // HD
    scale = HD ** (-0.5)

    @pl.loop(0, tokens // BLOCK)
    def _(i):
        at = pl.multiple_of(i * BLOCK, BLOCK)
        rows = pl.ds(at, BLOCK)
        x = x_ref[rows, :].astype(F32)
        inverse = lax.rsqrt(jnp.mean(x * x, axis=-1, keepdims=True) + EPS)
        normed = (x * inverse * gain_ref[...]).astype(BF)
        normed_ref[rows, :] = normed
        raw = mul(normed, w_ref[...])
        tables = (cos_ref[rows, :], sin_a_ref[rows, :], sin_b_ref[rows, :])
        for h in range(0, heads, per):
            turned = rotate_lanes(raw[:, h * HD : h * HD + 128], *tables) * scale
            for u in range(per):
                q_ref[h + u, rows, :] = turned[:, u * HD : (u + 1) * HD].astype(BF)
        for g in range(0, groups, per):
            lane = (heads + g) * HD
            turned = rotate_lanes(raw[:, lane : lane + 128], *tables)
            lane = (heads + groups + g) * HD
            value = raw[:, lane : lane + 128]
            turned_value = value.T
            for u in range(per):
                k_ref[g + u, rows, :] = turned[:, u * HD : (u + 1) * HD].astype(BF)
                v_ref[g + u, rows, :] = value[:, u * HD : (u + 1) * HD].astype(BF)
                vt_ref[g + u, :, rows] = turned_value[u * HD : (u + 1) * HD].astype(BF)

    keep = causal(BLOCK)

    @pl.loop(0, heads)
    def _(h):
        g = h // repeat
        for i in range(tokens // BLOCK):
            start, stop = i * BLOCK, (i + 1) * BLOCK
            query = q_ref[h, start:stop, :]
            parts = [jnp.where(keep, mul(k_ref[g, start:stop, :], query, NT), MASKED)]
            if i:
                parts.append(mul(k_ref[g, :start, :], query, NT))
            peak = jnp.max(parts[0], axis=0, keepdims=True)
            for part in parts[1:]:
                peak = jnp.maximum(peak, jnp.max(part, axis=0, keepdims=True))
            weights = [jnp.exp(part - peak) for part in parts]
            total = sum(jnp.sum(w, axis=0, keepdims=True) for w in weights)
            shrink = 1.0 / total
            mixed = mul(vt_ref[g, :, start:stop], (weights[0] * shrink).astype(BF))
            if i:
                mixed += mul(vt_ref[g, :, :start], (weights[1] * shrink).astype(BF))
            out_ref[h, :, start:stop] = mixed
            log_ref[h, :, start:stop] = peak + jnp.log(total)

    for i in range(tokens // BLOCK):
        start, stop = i * BLOCK, (i + 1) * BLOCK
        for h in range(0, heads, per):
            pair = jnp.concatenate([out_ref[h + u, :, start:stop] for u in range(per)], axis=0)
            mixed_ref[start:stop, h * HD : h * HD + 128] = pair.T.astype(BF)


def attend(x, gain, weight, tables, heads, groups):
    tokens, width = x.shape
    return pl.pallas_call(
        attend_kernel,
        out_shape=[
            jax.ShapeDtypeStruct((tokens, heads * HD), BF),
            jax.ShapeDtypeStruct((tokens, width), BF),
            jax.ShapeDtypeStruct((heads, tokens, HD), BF),
            jax.ShapeDtypeStruct((groups, tokens, HD), BF),
            jax.ShapeDtypeStruct((groups, tokens, HD), BF),
            jax.ShapeDtypeStruct((heads, 1, tokens), F32),
        ],
        scratch_shapes=[pltpu.VMEM((groups, HD, tokens), BF), pltpu.VMEM((heads, HD, tokens), F32)],
        compiler_params=pltpu.CompilerParams(vmem_limit_bytes=48 << 20),
        cost_estimate=takes(20),
    )(x, gain[None], weight, *tables)


def attend_back_kernel(grad_ref, q_ref, k_ref, v_ref, log_ref, cos_ref, sin_a_ref, sin_b_ref, out_ref, do_ref, kt_ref, dq_ref, dk_ref, dv_ref):
    tokens = grad_ref.shape[0]
    heads, groups = q_ref.shape[0], k_ref.shape[0]
    repeat = heads // groups
    per = 128 // HD
    scale = HD ** (-0.5)
    dk_ref[...] = jnp.zeros_like(dk_ref)
    dv_ref[...] = jnp.zeros_like(dv_ref)

    @pl.loop(0, tokens // BLOCK)
    def _(i):
        rows = pl.ds(pl.multiple_of(i * BLOCK, BLOCK), BLOCK)
        for h in range(heads):
            do_ref[h, rows, :] = grad_ref[rows, h * HD : (h + 1) * HD]
        for g in range(groups):
            kt_ref[g, :, rows] = k_ref[g, rows, :].astype(F32).T.astype(BF)

    keep = causal(BLOCK)

    @pl.loop(0, heads)
    def _(h):
        g = h // repeat
        for i in range(tokens // BLOCK):
            start, stop = i * BLOCK, (i + 1) * BLOCK
            query = q_ref[h, start:stop, :]
            grads = do_ref[h, start:stop, :]
            log_total = log_ref[h, :, start:stop]
            spans = [(start, stop)] + ([(0, start)] if i else [])
            probs, grad_probs = [], []
            for lo, hi in spans:
                scores = mul(k_ref[g, lo:hi, :], query, NT)
                if hi == stop:
                    scores = jnp.where(keep, scores, MASKED)
                probs.append(jnp.exp(scores - log_total))
                grad_probs.append(mul(v_ref[g, lo:hi, :], grads, NT))
            inner = sum(jnp.sum(p * d, axis=0, keepdims=True) for p, d in zip(probs, grad_probs))
            dq = None
            for (lo, hi), p, d in zip(spans, probs, grad_probs):
                ds = (p * (d - inner)).astype(BF)
                dk_ref[g, lo:hi, :] += mul(ds, query)
                dv_ref[g, lo:hi, :] += mul(p.astype(BF), grads)
                term = mul(kt_ref[g, :, lo:hi], ds)
                dq = term if dq is None else dq + term
            dq_ref[h, :, start:stop] = dq * scale

    @pl.loop(0, tokens // BLOCK)
    def _(i):
        rows = pl.ds(pl.multiple_of(i * BLOCK, BLOCK), BLOCK)
        tables = (cos_ref[rows, :], -sin_a_ref[rows, :], -sin_b_ref[rows, :])
        for h in range(0, heads, per):
            pair = jnp.concatenate([dq_ref[h + u, :, rows] for u in range(per)], axis=0).T
            out_ref[rows, h * HD : h * HD + 128] = rotate_lanes(pair, *tables).astype(BF)
        for g in range(0, groups, per):
            pair = jnp.concatenate([dk_ref[g + u, rows, :] for u in range(per)], axis=1)
            lane = (heads + g) * HD
            out_ref[rows, lane : lane + 128] = rotate_lanes(pair, *tables).astype(BF)
            pair = jnp.concatenate([dv_ref[g + u, rows, :] for u in range(per)], axis=1)
            lane = (heads + groups + g) * HD
            out_ref[rows, lane : lane + 128] = pair.astype(BF)


def attend_back(grad_mixed, q, k, v, logs, tables):
    heads, tokens, _ = q.shape
    groups = k.shape[0]
    return pl.pallas_call(
        attend_back_kernel,
        out_shape=jax.ShapeDtypeStruct((tokens, (heads + 2 * groups) * HD), BF),
        scratch_shapes=[
            pltpu.VMEM((heads, tokens, HD), BF),
            pltpu.VMEM((groups, HD, tokens), BF),
            pltpu.VMEM((heads, HD, tokens), F32),
            pltpu.VMEM((groups, tokens, HD), F32),
            pltpu.VMEM((groups, tokens, HD), F32),
        ],
        compiler_params=pltpu.CompilerParams(vmem_limit_bytes=48 << 20),
        cost_estimate=takes(20),
    )(grad_mixed, q, k, v, logs, *tables)


def place_rule(at, s, count, right, left, use):
    if s == 0:
        use(right[0])
        return

    @pl.when(at >= s)
    def _():
        use(right[s])

    @pl.when(at < s)
    def _():
        use(left[count - s])


def expert_kernel(order_ref, *refs, top, count):
    rows_refs, extra_refs, router_ref = refs[:2], refs[2:4], refs[4]
    own_ref = refs[5]
    right = [own_ref] + list(refs[6 : 5 + count])
    left = [own_ref] + list(refs[5 + count : 4 + 2 * count])
    outs = refs[4 + 2 * count :]
    out_refs, gin_refs, term_refs = outs[:2], outs[2:4], outs[4 : 4 + count]
    gu_ref, down_ref, agu, adown = outs[4 + count :]
    step = pl.program_id(0)
    steps = pl.num_programs(0)
    hidden_width, width = down_ref.shape
    part = hidden_width // count
    own = order_ref[2 * steps]
    experts = order_ref[2 * steps + 1]
    at = order_ref[2 * steps + 2]

    def spans(s):
        return (
            (gu_ref, agu, pl.ds(s * part, part)),
            (gu_ref, agu, pl.ds(hidden_width + s * part, part)),
            (down_ref, adown, pl.ds(s * part, part)),
        )

    @pl.when(step == 0)
    def _():
        agu[...] = jnp.zeros_like(agu)
        adown[...] = jnp.zeros_like(adown)
        for s in range(count):

            def keep(source, s=s):
                for j, (to_ref, _, span) in enumerate(spans(s)):
                    to_ref[span, :] = source[pl.ds(j * part, part), :]

            place_rule(at, s, count, right, left, keep)

    near = step < steps // 2
    rows = jnp.where(near, rows_refs[0][...], rows_refs[1][...])
    extra = jnp.concatenate([ref[...] for ref in extra_refs], axis=0)
    grads32 = extra[:, :width].astype(F32)
    named = extra[:, width:].astype(F32)

    lane = lax.broadcasted_iota(jnp.int32, (rows.shape[0], LANES), 1)
    lane32 = lane.astype(F32)
    chosen = lane32 == named[:, 0:1]
    for k in range(1, top):
        chosen = chosen | (lane32 == named[:, k : k + 1])
    logits = jnp.where(chosen, mul(rows, router_ref[...]), MASKED)
    weights = jnp.where(chosen, jnp.exp(logits - jnp.max(logits, axis=-1, keepdims=True)), 0.0)
    mine = jnp.sum(jnp.where(lane == own, weights, 0.0), axis=-1, keepdims=True)
    gate = mine / jnp.sum(weights, axis=-1, keepdims=True)

    both = mul(rows, gu_ref[...], NT)
    gate_vals = both[:, :hidden_width]
    up_vals = both[:, hidden_width:]
    sigma = jax.nn.sigmoid(gate_vals)
    active = gate_vals * sigma
    hidden = (active * up_vals).astype(BF)
    grad_out = (gate * grads32).astype(BF)
    grad_hidden = mul(grad_out, down_ref[...], NT)
    expert_out = mul(hidden, down_ref[...])
    combined = (gate * expert_out).astype(BF)
    score = jnp.sum(grads32 * expert_out, axis=-1, keepdims=True)
    high = score.astype(BF).astype(F32)
    scores = jnp.where(lane == own, high, jnp.where(lane == own + experts, score - high, 0.0)).astype(BF)
    grad_gate_vals = (grad_hidden * up_vals * sigma * (1.0 + gate_vals * (1.0 - sigma))).astype(BF)
    grad_up_vals = (grad_hidden * active).astype(BF)
    grad_both = jnp.concatenate([grad_gate_vals, grad_up_vals], axis=1)
    grad_in = mul(grad_both, gu_ref[...]).astype(BF)
    agu[...] += mul(grad_both, rows, TN)
    adown[...] += mul(hidden, grad_out, TN)
    for far in range(2):

        @pl.when(near if far == 0 else step >= steps // 2)
        def _():
            out_refs[far][...] = combined
            gin_refs[far][:, :width] = grad_in
            gin_refs[far][:, width:] = scores

    @pl.when(step == steps - 1)
    def _():
        for s in range(count):
            for j, (_, sums, span) in enumerate(spans(s)):
                term_refs[s][pl.ds(j * part, part), :] = sums[span, :].astype(BF)


def run_experts(order, near, far, extra, router, right, left, top):
    total, width = 2 * near.shape[0], near.shape[1]
    steps = total // BLOCK
    half_steps = steps // 2
    wide = extra.shape[1]
    count = len(right)
    part = right[0].shape[0] // 3
    hidden = count * part
    term = pl.BlockSpec((3 * part, width), lambda i, o: (0, 0))

    def by_set(lanes):
        return [
            pl.BlockSpec((BLOCK, lanes), lambda i, o: (jnp.minimum(i, half_steps - 1), 0)),
            pl.BlockSpec((BLOCK, lanes), lambda i, o: (jnp.maximum(i - half_steps, 0), 0)),
        ]

    half, half_wide = by_set(width), by_set(wide)
    weights = right + left[1:]
    return pl.pallas_call(
        functools.partial(expert_kernel, top=top, count=count),
        grid_spec=pltpu.PrefetchScalarGridSpec(
            num_scalar_prefetch=1,
            grid=(steps,),
            in_specs=[
                *by_set(width),
                pl.BlockSpec((BLOCK // 2, wide), lambda i, o: (o[2 * i], 0)),
                pl.BlockSpec((BLOCK // 2, wide), lambda i, o: (o[2 * i + 1], 0)),
                pl.BlockSpec((width, LANES), lambda i, o: (0, 0)),
            ]
            + [term] * len(weights),
            out_specs=half + half_wide + [term] * count,
            scratch_shapes=[
                pltpu.VMEM((2 * hidden, width), BF),
                pltpu.VMEM((hidden, width), BF),
                pltpu.VMEM((2 * hidden, width), F32),
                pltpu.VMEM((hidden, width), F32),
            ],
        ),
        out_shape=[jax.ShapeDtypeStruct((total // 2, width), BF)] * 2
        + [jax.ShapeDtypeStruct((total // 2, wide), BF)] * 2
        + [jax.ShapeDtypeStruct((3 * part, width), BF)] * count,
        compiler_params=pltpu.CompilerParams(vmem_limit_bytes=58 << 20),
        cost_estimate=takes(5 * steps),
    )(order, near, far, extra, extra, router, *weights)


def join(*values):
    return lax.optimization_barrier(values)


def swap(x, bit):
    return lax.ppermute(x, "ep", [(i, i ^ bit) for i in range(lax.axis_size("ep"))])


def turn(x, by):
    n = lax.axis_size("tp")
    return lax.ppermute(x, "tp", [(i, (i + by) % n) for i in range(n)])


def gather_slots(x):
    n = lax.axis_size("ep")
    if n != 8:
        whole = lax.all_gather(x, "ep")
        return [whole[k] for k in range(n)]
    first = [x] + [swap(x, k) for k in (2, 4, 6)]
    second = [swap(v, 1) for v in first]
    return [v for pair in zip(first, second) for v in pair]


def set_halves():
    n = lax.axis_size("ep")
    if n != 8:
        return jnp.arange(2 * n, dtype=jnp.int32)
    near = jnp.array([0, 2, 4, 6, 0, 4, 2, 6], jnp.int32)
    device = jnp.bitwise_xor(lax.axis_index("ep").astype(jnp.int32), jnp.concatenate([near, near + 1]))
    return 2 * device + jnp.array([0, 0, 0, 0, 1, 1, 1, 1] * 2, jnp.int32)


def gather_near(x):
    half = x.shape[0] // 2
    return swap(x[:half], 2), swap(x[half:], 4)


def gather_more(x, got):
    half = x.shape[0] // 2
    first, second = join(
        jnp.concatenate([x[:half], got[0]], axis=0), jnp.concatenate([x[half:], got[1]], axis=0)
    )
    return (first, second), (swap(first, 4), swap(second, 2))


def gather_last(sums, got):
    return jnp.concatenate([sums[0], got[0], sums[1], got[1]], axis=0)


def gather_whole(x):
    whole = lax.all_gather(x, "ep", tiled=True)
    return whole[: whole.shape[0] // 2], whole[whole.shape[0] // 2 :]


def add(a, b):
    return (a.astype(F32) + b.astype(F32)).astype(BF)


def sum_cores(near, far, other):
    rows = near.shape[0] // 4
    return join(*[add(near[j * rows : (j + 1) * rows], other[j * rows : (j + 1) * rows]) for j in range(4)])


def halves_home(sums):
    half = sums[0].shape[0] // 2
    return swap(sums[0][half:], 2), swap(sums[1][half:], 4)


def whole_home(sums, got):
    half = sums[0].shape[0] // 2
    return jnp.concatenate([s[:half].astype(F32) + g.astype(F32) for s, g in zip(sums, got)], axis=0)


def scatter_whole(near, far):
    n = lax.axis_size("ep")
    terms = jnp.concatenate([near, far], axis=0).reshape(n, -1, near.shape[1])
    return lax.psum_scatter(terms, "ep", scatter_dimension=0, tiled=False)


def slot_devices():
    n = lax.axis_size("ep")
    order = jnp.arange(n, dtype=jnp.int32)
    return jnp.bitwise_xor(order, lax.axis_index("ep")) if n == 8 else order


def in_device_order(blocks, shape, put):
    order = slot_devices()
    out = jnp.zeros(shape, blocks[0].dtype)
    for k, block in enumerate(blocks):
        out = put(out, block, order[k])
    return out


def step_both(right, left, low=0, high=None):
    n = lax.axis_size("tp")
    pairs = [(i, i + 1) for i in range(low, n - 1 if high is None else high)]
    return (
        lax.ppermute(right, "tp", pairs),
        lax.ppermute(left, "tp", [(n - 1 - i, n - 1 - j) for i, j in pairs]),
    )


def body(
    inputs,
    routes,
    norm_gain,
    query_weight,
    key_weight,
    value_weight,
    output_weight,
    mixer_gain,
    router_weight,
    gate_weight,
    up_weight,
    down_weight,
    cotangent,
):
    tokens, width = inputs.shape
    experts = router_weight.shape[1]
    top = routes.shape[1]
    n_ep = lax.axis_size("ep")
    n_tp = lax.axis_size("tp")
    ep_at = lax.axis_index("ep").astype(jnp.int32)
    tp_at = lax.axis_index("tp").astype(jnp.int32)
    quarter = tokens // n_tp
    heads_width = query_weight.shape[1]
    groups_width = key_weight.shape[1]

    def mine(x):
        return lax.dynamic_slice_in_dim(x, tp_at * quarter, quarter, 0)

    part = output_weight.shape[0] // n_ep
    output_part = lax.dynamic_slice_in_dim(output_weight, ep_at * part, part, 0)
    output_parts = [output_part] + [turn(output_part, -s) for s in range(1, n_tp)]

    routes_mine = mine(routes)
    grad_top_mine = mine(cotangent)
    named = jnp.pad(routes_mine.astype(BF), ((0, 0), (0, LANES - top)), constant_values=-1.0)
    extra = jnp.concatenate([grad_top_mine, named], axis=1)
    extra_all = lax.all_gather(extra, "ep", tiled=True)

    expert_part = jnp.concatenate([gate_weight[0].T, up_weight[0].T, down_weight[0]], axis=0)
    qkv_weight = jnp.concatenate([query_weight, key_weight, value_weight], axis=1)
    tables = rotary_lanes(tokens)
    expert_part, output_parts, qkv_weight, tables = join(expert_part, output_parts, qkv_weight, tables)
    output_part = jnp.concatenate(output_parts, axis=0)
    step = step_both(expert_part, expert_part)
    if n_ep == 8:
        got = gather_near(output_part)
    mixed, normed, query, key, value, logs = attend(
        inputs, norm_gain, qkv_weight, tables, heads_width // HD, groups_width // HD
    )
    if n_ep == 8:
        mixed, got, step = join(mixed, got, step)
    else:
        mixed, step = join(mixed, step)
    steps = [step]

    mixed_mine = lax.all_to_all(mixed, "tp", split_axis=0, concat_axis=1, tiled=True)
    if n_ep == 8:
        held, got = gather_more(output_part, got)
        mixed_mine, held, got, extra_all = join(mixed_mine, held, got, extra_all)
        near = gather_last(held, got)
        far = swap(near, 1)
    else:
        near, far = gather_whole(output_part)
    steps[0], mixed_mine = join(steps[0], mixed_mine)
    steps.append(step_both(*steps[0], 1))
    halves = set_halves()
    output_whole = jnp.zeros((n_tp, n_ep, part, width), BF)
    for blocks, first in ((near, 0), (far, n_ep)):
        blocks = blocks.reshape(n_ep, n_tp // 2, part, width)
        for k in range(n_ep):
            device, half = lax.div(halves[first + k], 2), lax.rem(halves[first + k], 2)
            for u in range(n_tp // 2):
                place = lax.rem(tp_at + half * (n_tp // 2) + u, n_tp)
                output_whole = lax.dynamic_update_slice(
                    output_whole, blocks[k, u][None, None], (place, device, 0, 0)
                )
    output_whole = output_whole.reshape(n_tp * heads_width, width)

    branch = mul(mixed_mine, output_whole)
    inputs_mine = mine(inputs).astype(F32)
    attended = inputs_mine + branch
    inverse_two = lax.rsqrt(jnp.mean(attended * attended, axis=-1, keepdims=True) + EPS)
    unit_two = attended * inverse_two
    routed_in = (unit_two * mixer_gain).astype(BF)
    logits = mul(routed_in, router_weight)
    ids = jnp.arange(experts, dtype=jnp.int32)
    chosen = jnp.any(routes_mine[:, :, None] == ids[None, None, :], axis=1)
    logits = jnp.where(chosen, logits, MASKED)
    weights = jnp.where(chosen, jnp.exp(logits - jnp.max(logits, axis=-1, keepdims=True)), 0.0)
    gates = weights / jnp.sum(weights, axis=-1, keepdims=True)

    if n_ep == 8:
        got = gather_near(routed_in)
        got, steps[-1], gates = join(got, steps[-1], gates)
        for t in range(2, n_tp - 1):
            steps.append(step_both(*steps[-1], t))
        held, got = gather_more(routed_in, got)
        held, got = join(held, got)
        near = gather_last(held, got)
        far = swap(near, 1)
    else:
        near, far = gather_whole(routed_in)
        for t in range(2, n_tp - 1):
            steps.append(step_both(*steps[-1], t))
    near, far, steps[-1] = join(near, far, steps[-1])
    right = [expert_part] + [v[0] for v in steps]
    left = [expert_part] + [v[1] for v in steps]
    router = jnp.pad(router_weight, ((0, 0), (0, LANES - experts)))
    order = jnp.concatenate(
        [halves, ep_at[None], jnp.full((1,), experts, jnp.int32), tp_at[None]]
    )
    out_near, out_far, gin_near, gin_far, *terms = run_experts(
        order, near, far, extra_all, router, right, left, top
    )
    if n_ep == 8:
        gin = sum_cores(gin_near, gin_far, swap(gin_far, 1))
        gin, terms, out_far = join(gin, terms, out_far)
        go = step_both(terms[1], terms[n_tp - 1], 0, 1)
        got = (swap(gin[1], 4), swap(gin[3], 2))
        out = swap(out_far, 1)
        got, out = join(got, out)
        gin = add(gin[0], got[0]), add(gin[2], got[1])
        out = sum_cores(out_near, out_far, out)
        gin, out = join(gin, out)
        got = halves_home(gin)
        out_got = (swap(out[1], 4), swap(out[3], 2))
        got, go = join(got, go)
        grad_in = whole_home(gin, got)
    else:
        go = step_both(terms[1], terms[n_tp - 1], 0, 1)
        grad_in = scatter_whole(gin_near, gin_far).astype(F32)
    grad_gates = grad_in[:, width : width + experts] + grad_in[:, width + experts : width + 2 * experts]
    inner_gate = jnp.sum(gates * grad_gates, axis=-1, keepdims=True)
    grad_logits = (gates * (grad_gates - inner_gate)).astype(BF)
    grad_routed = grad_in[:, :width] + mul(grad_logits, router_weight, NT)
    grad_top = grad_top_mine.astype(F32)
    scaled_two = grad_routed * mixer_gain
    grad_attended = grad_top + inverse_two * (
        scaled_two - unit_two * jnp.mean(scaled_two * unit_two, axis=-1, keepdims=True)
    )
    grad_branch = grad_attended.astype(BF)
    grad_mixed = mul(grad_branch, output_whole, NT).astype(BF)
    for t in range(2, n_tp - 1):
        go = step_both(add(terms[t], go[0]), add(terms[n_tp - t], go[1]), 0, t)

    if n_ep == 8:
        grad_mixed, out_got = join(grad_mixed, out_got)
    grad_mixed = lax.all_to_all(grad_mixed, "tp", split_axis=1, concat_axis=0, tiled=True)
    if n_ep == 8:
        out = join(add(out[0], out_got[0]), add(out[2], out_got[1]))
        out_got = halves_home(out)
    grad_router = mul(routed_in, grad_logits, TN)
    grad_mixer = jnp.sum(grad_routed * unit_two, axis=0)
    few = -(-(1 + experts) // n_ep)
    pad = 16 * (few // 16 + 1)
    small = jnp.concatenate([grad_mixer[None], grad_router.T], axis=0).astype(BF)
    small = jnp.pad(small, ((0, few * n_ep - 1 - experts), (0, 0))).reshape(n_ep, few, width)
    small = jnp.pad(small, ((0, 0), (0, pad - few), (0, 0)))
    grad_output = mul(mixed_mine, grad_branch, TN).astype(BF)
    grad_output = grad_output.reshape(n_tp, n_ep, part, width).transpose(1, 0, 2, 3)
    grad_output = jnp.concatenate([grad_output.reshape(n_ep, n_tp * part, width), small], axis=1)
    if n_ep == 8:
        core, chip = lax.rem(ep_at, 2), lax.div(ep_at, 2)
        grad_output = grad_output.reshape((n_ep // 2, 2) + grad_output.shape[1:])
        other_output = lax.dynamic_index_in_dim(grad_output, 1 - core, 1, False)
        grad_output = lax.dynamic_index_in_dim(grad_output, core, 1, False)
        grad_mixed, out_got, go, other_output, grad_output = join(
            grad_mixed, out_got, go, other_output, grad_output
        )
        out = whole_home(out, out_got)
        other_output = swap(other_output, 1)
    else:
        out = scatter_whole(out_near, out_far).astype(F32)
    result_mine = (attended + out).astype(BF)

    result_mine, grad_mixed = join(result_mine, grad_mixed)
    result_steps = [step_both(result_mine, result_mine)]
    grad_qkv = attend_back(grad_mixed, query, key, value, logs, tables)
    if n_ep == 8:
        grad_qkv, result_steps[0], other_output = join(grad_qkv, result_steps[0], other_output)
    else:
        grad_qkv, result_steps[0] = join(grad_qkv, result_steps[0])

    grad_normed = mul(grad_qkv, qkv_weight, NT).astype(BF).reshape(n_tp, quarter, width)
    grad_qkv_w = mul(normed, grad_qkv, TN).astype(BF)

    def block(j):
        return lax.dynamic_index_in_dim(grad_normed, lax.rem(tp_at + j + n_tp, n_tp), 0, False)

    sent = None
    for t in range(1, n_tp):
        give = [block(n_tp - t), block(t - n_tp)]
        if sent is not None:
            give = [add(give[0], sent[0]), add(give[1], sent[1])]
        sent = step_both(*give, 0, t)
        if t < n_tp - 1:
            result_steps.append(step_both(*result_steps[-1], t))
            if t == 1:
                sent, result_steps[-1], grad_qkv_w = join(sent, result_steps[-1], grad_qkv_w)
                grad_qkv_w = lax.psum(grad_qkv_w, "ep")
                if n_ep == 8:
                    grad_output = add(grad_output, other_output)
            else:
                last = add(terms[n_tp - 1], go[0]), add(terms[1], go[1])
                sent, result_steps[-1], grad_output, last = join(sent, result_steps[-1], grad_output, last)
    if n_ep == 8:

        def chip_block(j):
            return lax.dynamic_index_in_dim(grad_output, jnp.bitwise_xor(chip, j), 0, False)

        got = [swap(chip_block(j), 2 * j) for j in (1, 2, 3)]
        grad_output = chip_block(0)
    else:
        got = []
        grad_output = lax.psum_scatter(grad_output, "ep", scatter_dimension=0, tiled=False)
    sent, last = join(sent, last)
    go = step_both(*last, 0, n_tp - 1)
    grad_normed = block(0).astype(F32) + sent[0].astype(F32) + sent[1].astype(F32)
    inverse_one = lax.rsqrt(jnp.mean(inputs_mine * inputs_mine, axis=-1, keepdims=True) + EPS)
    unit_one = inputs_mine * inverse_one
    scaled_one = grad_normed * norm_gain
    grad_inputs = grad_attended + inverse_one * (
        scaled_one - unit_one * jnp.mean(scaled_one * unit_one, axis=-1, keepdims=True)
    )
    grad_inputs = grad_inputs.astype(BF)
    grad_norm = jnp.sum(grad_normed * unit_one, axis=0)

    input_steps = [step_both(grad_inputs, grad_inputs)]
    got, input_steps[0] = join(got, input_steps[0])
    grad_output = sum([grad_output.astype(F32)] + [v.astype(F32) for v in got])
    grad_output = grad_output.at[-1].set(grad_norm).astype(BF)
    pieces = [
        jnp.concatenate([grad_output[j * part : (j + 1) * part], grad_output[n_tp * part :]], axis=0)
        for j in range(n_tp)
    ]
    pieces = jnp.stack(pieces)

    def piece(j):
        return lax.dynamic_index_in_dim(pieces, lax.rem(tp_at + j, n_tp), 0, False)

    got = [turn(piece(s), s) for s in range(1, n_tp)]
    input_steps.append(step_both(*input_steps[-1], 1))
    got, input_steps[-1] = join(got, input_steps[-1])
    grad_output = (piece(0).astype(F32) + sum(v.astype(F32) for v in got)).astype(BF)
    got = gather_slots(grad_output)
    for t in range(2, n_tp - 1):
        input_steps.append(step_both(*input_steps[-1], t))
    input_steps[-1], grad_qkv_w = join(input_steps[-1], grad_qkv_w)
    grad_output = in_device_order(
        got,
        (n_ep, part + pad, width),
        lambda out, block, at: lax.dynamic_update_index_in_dim(out, block, at, 0),
    )
    small = grad_output[:, part : part + few].reshape(n_ep * few, width)[: 1 + experts].astype(F32)
    grad_norm = jnp.sum(grad_output[:, -1].astype(F32), axis=0)
    grad_output = grad_output[:, :part].reshape(heads_width, width).astype(F32)
    grad_qkv_w = grad_qkv_w.astype(F32)
    grad_expert = terms[0].astype(F32) + go[0].astype(F32) + go[1].astype(F32)
    hidden_part = gate_weight.shape[2]
    grad_gate_w = grad_expert[:hidden_part].T
    grad_up_w = grad_expert[hidden_part : 2 * hidden_part].T
    grad_down_w = grad_expert[2 * hidden_part :]

    def spread(own, steps):
        out = jnp.zeros((tokens, width), BF)
        for t, step in enumerate(steps):
            for got, place in zip(step, (tp_at - t - 1, tp_at + t + 1)):
                place = jnp.where((place >= 0) & (place < n_tp), place, tp_at)
                out = lax.dynamic_update_slice(out, got, (place * quarter, 0))
        return lax.dynamic_update_slice(out, own, (tp_at * quarter, 0))

    result = spread(result_mine, result_steps)
    grad_inputs = spread(grad_inputs, input_steps)
    return (
        result,
        grad_inputs,
        grad_norm,
        grad_qkv_w[:, :heads_width],
        grad_qkv_w[:, heads_width : heads_width + groups_width],
        grad_qkv_w[:, heads_width + groups_width :],
        grad_output,
        small[0],
        small[1:].T,
        grad_gate_w[None],
        grad_up_w[None],
        grad_down_w[None],
    )


def solution(mesh):
    placed = (
        P("ep", None),
        P("ep", None),
        P(),
        P(None, "tp"),
        P(None, "tp"),
        P(None, "tp"),
        P("tp", None),
        P(),
        P(),
        P("ep", None, "tp"),
        P("ep", None, "tp"),
        P("ep", "tp", None),
        P("ep", None),
    )
    return jax.shard_map(
        body,
        mesh=mesh,
        in_specs=placed,
        out_specs=(
            P("ep", None),
            P("ep", None),
            P(),
            P(None, "tp"),
            P(None, "tp"),
            P(None, "tp"),
            P("tp", None),
            P(),
            P(),
            P("ep", None, "tp"),
            P("ep", None, "tp"),
            P("ep", "tp", None),
        ),
        check_vma=False,
    )
```

```python
import functools

import jax
import jax.numpy as jnp
from jax import lax
from jax.experimental import pallas as pl
from jax.experimental.pallas import tpu as pltpu
from jax.sharding import PartitionSpec as P

HD = 64
LEN = 1024
EPS = 1e-06
MASKED = -1e30
BF = jnp.bfloat16
F32 = jnp.float32
BLOCK = 256
LANES = 128
NT = (((1,), (1,)), ((), ()))
TN = (((0,), (0,)), ((), ()))


def takes(us):
    return pl.CostEstimate(flops=int(us * 1.15e9), bytes_accessed=0, transcendentals=0)


def mul(a, b, dims=(((1,), (0,)), ((), ()))):
    return lax.dot_general(a, b, dims, preferred_element_type=F32)


def rotate_lanes(y, cos, sin_a, sin_b):
    return y * cos + pltpu.roll(y, 128 - HD // 2, 1) * sin_a + pltpu.roll(y, HD // 2, 1) * sin_b


def rotary_lanes(tokens):
    positions = (jnp.arange(tokens) % LEN).astype(F32)
    lane = jnp.arange(128)
    freqs = 10000.0 ** (-(lane % (HD // 2)).astype(F32) * 2.0 / HD)
    angles = positions[:, None] * freqs[None, :]
    cos, sin = jnp.cos(angles), jnp.sin(angles)
    first = (lane % HD < HD // 2)[None, :]
    return cos, jnp.where(first, -sin, 0.0), jnp.where(first, 0.0, sin)


def causal(block):
    key_at = lax.broadcasted_iota(jnp.int32, (block, block), 0)
    query_at = lax.broadcasted_iota(jnp.int32, (block, block), 1)
    return key_at <= query_at


def attend_kernel(at_ref, x_ref, gain_ref, wq_ref, wk_ref, wv_ref, cos_ref, sin_a_ref, sin_b_ref, *refs):
    pieces, (normed_ref, q_ref, k_ref, v_ref, w_ref, log_ref, vt_ref, out_ref) = refs[:-8], refs[-8:]
    tokens = x_ref.shape[0]
    heads, groups = q_ref.shape[0], k_ref.shape[0]
    repeat = heads // groups
    per = 128 // HD
    scale = HD ** (-0.5)
    w_ref[...] = jnp.concatenate([wq_ref[...], wk_ref[...], wv_ref[...]], axis=1)

    @pl.loop(0, tokens // BLOCK)
    def _(i):
        at = pl.multiple_of(i * BLOCK, BLOCK)
        rows = pl.ds(at, BLOCK)
        x = x_ref[rows, :].astype(F32)
        inverse = lax.rsqrt(jnp.mean(x * x, axis=-1, keepdims=True) + EPS)
        normed = (x * inverse * gain_ref[...]).astype(BF)
        normed_ref[rows, :] = normed
        raw = mul(normed, w_ref[...])
        tables = (cos_ref[rows, :], sin_a_ref[rows, :], sin_b_ref[rows, :])
        for h in range(0, heads, per):
            turned = rotate_lanes(raw[:, h * HD : h * HD + 128], *tables) * scale
            for u in range(per):
                q_ref[h + u, rows, :] = turned[:, u * HD : (u + 1) * HD].astype(BF)
        for g in range(0, groups, per):
            lane = (heads + g) * HD
            turned = rotate_lanes(raw[:, lane : lane + 128], *tables)
            lane = (heads + groups + g) * HD
            value = raw[:, lane : lane + 128]
            turned_value = value.T
            for u in range(per):
                k_ref[g + u, rows, :] = turned[:, u * HD : (u + 1) * HD].astype(BF)
                v_ref[g + u, rows, :] = value[:, u * HD : (u + 1) * HD].astype(BF)
                vt_ref[g + u, :, rows] = turned_value[u * HD : (u + 1) * HD].astype(BF)

    keep = causal(BLOCK)

    @pl.loop(0, heads)
    def _(h):
        g = h // repeat
        for i in range(tokens // BLOCK):
            start, stop = i * BLOCK, (i + 1) * BLOCK
            query = q_ref[h, start:stop, :]
            parts = [jnp.where(keep, mul(k_ref[g, start:stop, :], query, NT), MASKED)]
            if i:
                parts.append(mul(k_ref[g, :start, :], query, NT))
            peak = jnp.max(parts[0], axis=0, keepdims=True)
            for part in parts[1:]:
                peak = jnp.maximum(peak, jnp.max(part, axis=0, keepdims=True))
            weights = [jnp.exp(part - peak) for part in parts]
            total = sum(jnp.sum(w, axis=0, keepdims=True) for w in weights)
            shrink = 1.0 / total
            mixed = mul(vt_ref[g, :, start:stop], (weights[0] * shrink).astype(BF))
            if i:
                mixed += mul(vt_ref[g, :, :start], (weights[1] * shrink).astype(BF))
            out_ref[h, :, start:stop] = mixed
            log_ref[h, :, start:stop] = peak + jnp.log(total)

    for s, piece_ref in enumerate(pieces):
        span = pl.ds(pl.multiple_of(lax.rem(at_ref[0] + s, len(pieces)) * BLOCK, BLOCK), BLOCK)
        for h in range(0, heads, per):
            pair = jnp.concatenate([out_ref[h + u, :, span] for u in range(per)], axis=0)
            piece_ref[:, h * HD : h * HD + 128] = pair.T.astype(BF)


VMEM = pl.BlockSpec(memory_space=pltpu.VMEM)
SMEM = pl.BlockSpec(memory_space=pltpu.SMEM)


def attend(x, gain, weights, tables, heads, groups, at):
    tokens, width = x.shape
    count = tokens // BLOCK
    return pl.pallas_call(
        attend_kernel,
        in_specs=[SMEM] + [VMEM] * 8,
        out_shape=[jax.ShapeDtypeStruct((BLOCK, heads * HD), BF)] * count
        + [
            jax.ShapeDtypeStruct((tokens, width), BF),
            jax.ShapeDtypeStruct((heads, tokens, HD), BF),
            jax.ShapeDtypeStruct((groups, tokens, HD), BF),
            jax.ShapeDtypeStruct((groups, tokens, HD), BF),
            jax.ShapeDtypeStruct((width, (heads + 2 * groups) * HD), BF),
            jax.ShapeDtypeStruct((heads, 1, tokens), F32),
        ],
        scratch_shapes=[pltpu.VMEM((groups, HD, tokens), BF), pltpu.VMEM((heads, HD, tokens), F32)],
        compiler_params=pltpu.CompilerParams(vmem_limit_bytes=48 << 20),
        cost_estimate=takes(20),
    )(at[None], x, gain[None], *weights, *tables)


def attend_back_kernel(at_ref, q_ref, k_ref, v_ref, log_ref, cos_ref, sin_a_ref, sin_b_ref, *refs):
    do_ref, kt_ref, dq_ref, dk_ref, dv_ref = refs[-5:]
    out_ref = refs[-6]
    grad_refs = refs[:-6]
    count = len(grad_refs)
    tokens = q_ref.shape[1]
    heads, groups = q_ref.shape[0], k_ref.shape[0]
    repeat = heads // groups
    per = 128 // HD
    scale = HD ** (-0.5)
    dk_ref[...] = jnp.zeros_like(dk_ref)
    dv_ref[...] = jnp.zeros_like(dv_ref)

    def span_of(s):
        return pl.ds(pl.multiple_of(lax.rem(at_ref[0] + s, count) * BLOCK, BLOCK), BLOCK)

    for s, grad_ref in enumerate(grad_refs):
        for h in range(heads):
            do_ref[h, span_of(s), :] = grad_ref[:, h * HD : (h + 1) * HD]

    @pl.loop(0, tokens // BLOCK)
    def _(i):
        rows = pl.ds(pl.multiple_of(i * BLOCK, BLOCK), BLOCK)
        for g in range(groups):
            kt_ref[g, :, rows] = k_ref[g, rows, :].astype(F32).T.astype(BF)

    keep = causal(BLOCK)

    @pl.loop(0, heads)
    def _(h):
        g = h // repeat
        for i in range(tokens // BLOCK):
            start, stop = i * BLOCK, (i + 1) * BLOCK
            query = q_ref[h, start:stop, :]
            grads = do_ref[h, start:stop, :]
            log_total = log_ref[h, :, start:stop]
            spans = [(start, stop)] + ([(0, start)] if i else [])
            probs, grad_probs = [], []
            for lo, hi in spans:
                scores = mul(k_ref[g, lo:hi, :], query, NT)
                if hi == stop:
                    scores = jnp.where(keep, scores, MASKED)
                probs.append(jnp.exp(scores - log_total))
                grad_probs.append(mul(v_ref[g, lo:hi, :], grads, NT))
            inner = sum(jnp.sum(p * d, axis=0, keepdims=True) for p, d in zip(probs, grad_probs))
            dq = None
            for (lo, hi), p, d in zip(spans, probs, grad_probs):
                ds = (p * (d - inner)).astype(BF)
                dk_ref[g, lo:hi, :] += mul(ds, query)
                dv_ref[g, lo:hi, :] += mul(p.astype(BF), grads)
                term = mul(kt_ref[g, :, lo:hi], ds)
                dq = term if dq is None else dq + term
            dq_ref[h, :, start:stop] = dq * scale

    @pl.loop(0, tokens // BLOCK)
    def _(i):
        rows = pl.ds(pl.multiple_of(i * BLOCK, BLOCK), BLOCK)
        tables = (cos_ref[rows, :], -sin_a_ref[rows, :], -sin_b_ref[rows, :])
        for h in range(0, heads, per):
            pair = jnp.concatenate([dq_ref[h + u, :, rows] for u in range(per)], axis=0).T
            out_ref[rows, h * HD : h * HD + 128] = rotate_lanes(pair, *tables).astype(BF)
        for g in range(0, groups, per):
            pair = jnp.concatenate([dk_ref[g + u, rows, :] for u in range(per)], axis=1)
            lane = (heads + g) * HD
            out_ref[rows, lane : lane + 128] = rotate_lanes(pair, *tables).astype(BF)
            pair = jnp.concatenate([dv_ref[g + u, rows, :] for u in range(per)], axis=1)
            lane = (heads + groups + g) * HD
            out_ref[rows, lane : lane + 128] = pair.astype(BF)


def attend_back(grad_pieces, q, k, v, logs, tables, at):
    heads, tokens, _ = q.shape
    groups = k.shape[0]
    count = len(grad_pieces)
    lanes = (heads + 2 * groups) * HD
    return pl.pallas_call(
        attend_back_kernel,
        in_specs=[SMEM] + [VMEM] * (7 + count),
        out_shape=jax.ShapeDtypeStruct((tokens, lanes), BF),
        scratch_shapes=[
            pltpu.VMEM((heads, tokens, HD), BF),
            pltpu.VMEM((groups, HD, tokens), BF),
            pltpu.VMEM((heads, HD, tokens), F32),
            pltpu.VMEM((groups, tokens, HD), F32),
            pltpu.VMEM((groups, tokens, HD), F32),
        ],
        compiler_params=pltpu.CompilerParams(vmem_limit_bytes=48 << 20),
        cost_estimate=takes(20),
    )(at[None], q, k, v, logs, *tables, *grad_pieces)


def expert_kernel(order_ref, near_ref, far_ref, extra_near_ref, extra_far_ref, router_ref, parts_ref, *refs, top, count):
    out_refs, gin_refs, terms_ref = refs[:2], refs[2:4], refs[4]
    weights_ref, sums_ref = refs[5:]
    step = pl.program_id(0)
    steps = pl.num_programs(0)
    hidden_width, width = weights_ref.shape[0] // 3, weights_ref.shape[1]
    gate_up = slice(0, 2 * hidden_width)
    down = slice(2 * hidden_width, 3 * hidden_width)
    own = order_ref[0]
    experts = order_ref[1]
    part = hidden_width // count
    spans = [
        (pl.ds((3 * s + j) * part, part), pl.ds(j * hidden_width + s * part, part))
        for s in range(count)
        for j in range(3)
    ]

    @pl.when(step == 0)
    def _():
        sums_ref[...] = jnp.zeros_like(sums_ref)
        for there, here in spans:
            weights_ref[here, :] = parts_ref[there, :]

    near = step < steps // 2
    rows = jnp.where(near, near_ref[...], far_ref[...])
    extra = jnp.where(near, extra_near_ref[...], extra_far_ref[...])
    grads32 = extra[:, :width].astype(F32)
    named = extra[:, width:].astype(F32)

    lane = lax.broadcasted_iota(jnp.int32, (rows.shape[0], LANES), 1)
    lane32 = lane.astype(F32)
    chosen = lane32 == named[:, 0:1]
    for k in range(1, top):
        chosen = chosen | (lane32 == named[:, k : k + 1])
    logits = jnp.where(chosen, mul(rows, router_ref[...]), MASKED)
    weights = jnp.where(chosen, jnp.exp(logits - jnp.max(logits, axis=-1, keepdims=True)), 0.0)
    mine = jnp.sum(jnp.where(lane == own, weights, 0.0), axis=-1, keepdims=True)
    gate = mine / jnp.sum(weights, axis=-1, keepdims=True)

    both = mul(rows, weights_ref[gate_up, :], NT)
    gate_vals = both[:, :hidden_width]
    up_vals = both[:, hidden_width:]
    sigma = jax.nn.sigmoid(gate_vals)
    active = gate_vals * sigma
    hidden = (active * up_vals).astype(BF)
    grad_out = (gate * grads32).astype(BF)
    grad_hidden = mul(grad_out, weights_ref[down, :], NT)
    expert_out = mul(hidden, weights_ref[down, :])
    combined = (gate * expert_out).astype(BF)
    score = jnp.sum(grads32 * expert_out, axis=-1, keepdims=True)
    high = score.astype(BF).astype(F32)
    scores = jnp.where(lane == own, high, jnp.where(lane == own + experts, score - high, 0.0)).astype(BF)
    grad_gate_vals = (grad_hidden * up_vals * sigma * (1.0 + gate_vals * (1.0 - sigma))).astype(BF)
    grad_up_vals = (grad_hidden * active).astype(BF)
    grad_both = jnp.concatenate([grad_gate_vals, grad_up_vals], axis=1)
    grad_in = mul(grad_both, weights_ref[gate_up, :]).astype(BF)
    sums_ref[gate_up, :] += mul(grad_both, rows, TN)
    sums_ref[down, :] += mul(hidden, grad_out, TN)
    for far in range(2):

        @pl.when(near if far == 0 else step >= steps // 2)
        def _():
            out_refs[far][...] = combined
            gin_refs[far][:, :width] = grad_in
            gin_refs[far][:, width:] = scores

    @pl.when(step == steps - 1)
    def _():
        for there, here in spans:
            terms_ref[there, :] = sums_ref[here, :].astype(BF)


def run_experts(order, near, far, extra_near, extra_far, router, parts, top, count):
    total, width = 2 * near.shape[0], near.shape[1]
    steps = total // BLOCK
    half_steps = steps // 2
    wide = extra_near.shape[1]
    hidden = parts.shape[0] // 3

    def by_set(lanes):
        return [
            pl.BlockSpec((BLOCK, lanes), lambda i, o: (jnp.minimum(i, half_steps - 1), 0)),
            pl.BlockSpec((BLOCK, lanes), lambda i, o: (jnp.maximum(i - half_steps, 0), 0)),
        ]

    half, half_wide = by_set(width), by_set(wide)
    whole = pl.BlockSpec((3 * hidden, width), lambda i, o: (0, 0), pipeline_mode=pl.Buffered(1))
    return pl.pallas_call(
        functools.partial(expert_kernel, top=top, count=count),
        grid_spec=pltpu.PrefetchScalarGridSpec(
            num_scalar_prefetch=1,
            grid=(steps,),
            in_specs=[
                *by_set(width),
                *by_set(wide),
                pl.BlockSpec((width, LANES), lambda i, o: (0, 0)),
                whole,
            ],
            out_specs=half + half_wide + [whole],
            scratch_shapes=[
                pltpu.VMEM((3 * hidden, width), BF),
                pltpu.VMEM((3 * hidden, width), F32),
            ],
        ),
        out_shape=[jax.ShapeDtypeStruct((total // 2, width), BF)] * 2
        + [jax.ShapeDtypeStruct((total // 2, wide), BF)] * 2
        + [jax.ShapeDtypeStruct((3 * hidden, width), BF)],
        compiler_params=pltpu.CompilerParams(vmem_limit_bytes=58 << 20),
        cost_estimate=takes(5 * steps),
    )(order, near, far, extra_near, extra_far, router, parts)


def set_rows_kernel(order_ref, near_ref, far_ref, out_ref, small_ref, norm_ref, *, part, few_rows):
    rows, width = near_ref.shape[0] // 4, near_ref.shape[1]
    norm = jnp.zeros((1, width), F32)
    for k in range(8):
        source = near_ref if k < 4 else far_ref
        block = source[(k % 4) * rows : (k % 4 + 1) * rows, :].astype(F32)
        device = order_ref[k]
        out_ref[pl.ds(pl.multiple_of(device * part, 8), part), :] = block[:part]
        small_ref[pl.ds(pl.multiple_of(device * few_rows, 8), few_rows), :] = block[part : part + few_rows]
        norm += block[rows - 1 :]
    norm_ref[...] = norm


def set_rows(order, near, far, part, few_rows):
    width = near.shape[1]
    return pl.pallas_call(
        functools.partial(set_rows_kernel, part=part, few_rows=few_rows),
        in_specs=[SMEM, VMEM, VMEM],
        out_shape=[
            jax.ShapeDtypeStruct((8 * part, width), F32),
            jax.ShapeDtypeStruct((8 * few_rows, width), F32),
            jax.ShapeDtypeStruct((1, width), F32),
        ],
        compiler_params=pltpu.CompilerParams(vmem_limit_bytes=32 << 20),
        cost_estimate=takes(3),
    )(order, near, far)


def join(*values):
    return lax.optimization_barrier(values)


def add(a, b):
    return (a.astype(F32) + b.astype(F32)).astype(BF)


def swap(x, bit):
    return lax.ppermute(x, "ep", [(i, i ^ bit) for i in range(lax.axis_size("ep"))])


def turn(x, by):
    n = lax.axis_size("tp")
    return lax.ppermute(x, "tp", [(i, (i + by) % n) for i in range(n)])


def step_both(right, left, low=0, high=None):
    n = lax.axis_size("tp")
    pairs = [(i, i + 1) for i in range(low, n - 1 if high is None else high)]
    mirror = [(n - 1 - i, n - 1 - j) for i, j in pairs]
    return lax.ppermute(right, "tp", pairs), lax.ppermute(left, "tp", mirror)


def step_ends(right, left, low, high):
    n = lax.axis_size("tp")
    at = lax.axis_index("tp")
    pairs = [(i, i + 1) for i in range(low, high)]
    give = jnp.where((at >= low) & (at < high), right, left)
    return lax.ppermute(give, "tp", pairs + [(n - 1 - i, n - 1 - j) for i, j in pairs])


def by_side(got, low, high):
    at = lax.axis_index("tp")
    ahead = (at > low) & (at <= high)
    return jnp.where(ahead, got, 0), jnp.where(ahead, 0, got)


def gather_first(x):
    half = x.shape[0] // 2
    return swap(x[:half], 2), swap(x[half:], 4)


def gather_second(x, got):
    half = x.shape[0] // 2
    first, second = join(
        jnp.concatenate([x[:half], got[0]], axis=0), jnp.concatenate([x[half:], got[1]], axis=0)
    )
    return (first, second), (swap(first, 4), swap(second, 2))


def gather_near(held, got):
    return jnp.concatenate([held[0], got[0], held[1], got[1]], axis=0)


def gather_halves():
    n = lax.axis_size("ep")
    if n != 8:
        return [(jnp.int32(k // 2), k % 2) for k in range(2 * n)]
    at = lax.axis_index("ep").astype(jnp.int32)
    near = [(0, 0), (2, 0), (4, 0), (6, 0), (0, 1), (4, 1), (2, 1), (6, 1)]
    return [(jnp.bitwise_xor(at, k + core), half) for core in (0, 1) for k, half in near]


def gather_whole(x):
    whole = lax.all_gather(x, "ep", tiled=True)
    return whole[: whole.shape[0] // 2], whole[whole.shape[0] // 2 :]


def sum_cores(near, far):
    rows = near.shape[0] // 4
    return join(*[add(near[j * rows : (j + 1) * rows], far[j * rows : (j + 1) * rows]) for j in range(4)])


def sum_first(sums):
    return swap(sums[1], 4), swap(sums[3], 2)


def sum_second(sums, got):
    first, second = join(add(sums[0], got[0]), add(sums[2], got[1]))
    half = first.shape[0] // 2
    return (first, second), (swap(first[half:], 2), swap(second[half:], 4))


def sum_last(sums, got):
    half = sums[0].shape[0] // 2
    return jnp.concatenate([s[:half].astype(F32) + g.astype(F32) for s, g in zip(sums, got)], axis=0)


def sum_whole(near, far):
    n = lax.axis_size("ep")
    terms = jnp.concatenate([near, far], axis=0).reshape(n, -1, near.shape[1])
    return lax.psum_scatter(terms, "ep", scatter_dimension=0, tiled=False).astype(F32)


def spread(own, steps, last):
    n = lax.axis_size("tp")
    at = lax.axis_index("tp").astype(jnp.int32)
    rows, width = own.shape
    out = jnp.zeros((n * rows, width), BF)
    for t, step in enumerate(steps):
        for got, place in zip(step, (at - t - 1, at + t + 1)):
            place = jnp.where((place >= 0) & (place < n), place, at)
            out = lax.dynamic_update_slice(out, got, (place * rows, 0))
    place = jnp.where(at == n - 1, 0, jnp.where(at == 0, n - 1, at))
    out = lax.dynamic_update_slice(out, last, (place * rows, 0))
    return lax.dynamic_update_slice(out, own, (at * rows, 0))


def body(
    inputs,
    routes,
    norm_gain,
    query_weight,
    key_weight,
    value_weight,
    output_weight,
    mixer_gain,
    router_weight,
    gate_weight,
    up_weight,
    down_weight,
    cotangent,
):
    tokens, width = inputs.shape
    experts = router_weight.shape[1]
    top = routes.shape[1]
    n_ep = lax.axis_size("ep")
    n_tp = lax.axis_size("tp")
    fine = n_ep == 8
    ep_at = lax.axis_index("ep").astype(jnp.int32)
    tp_at = lax.axis_index("tp").astype(jnp.int32)
    quarter = tokens // n_tp
    heads_width = query_weight.shape[1]
    groups_width = key_weight.shape[1]

    def mine(x):
        return lax.dynamic_slice_in_dim(x, tp_at * quarter, quarter, 0)

    part = output_weight.shape[0] // n_ep
    output_part = lax.dynamic_slice_in_dim(output_weight, ep_at * part, part, 0)
    output_parts = [output_part] + [turn(output_part, -s) for s in range(1, n_tp)]

    hidden_part = gate_weight.shape[2]
    expert_part = jnp.concatenate([gate_weight[0].T, up_weight[0].T, down_weight[0]], axis=0)
    expert_parts = lax.all_gather(expert_part, "tp", tiled=True)

    routes_mine = mine(routes)
    grad_top_mine = mine(cotangent)
    named = jnp.pad(routes_mine.astype(BF), ((0, 0), (0, LANES - top)), constant_values=-1.0)
    extra = jnp.concatenate([grad_top_mine, named], axis=1)
    tables = rotary_lanes(tokens)
    if fine:
        extra_got = gather_first(extra)
        output_parts, extra_got, tables = join(output_parts, extra_got, tables)
        output_part = jnp.concatenate(output_parts, axis=0)
        output_got = gather_first(output_part)
        extra_held, extra_got = gather_second(extra, extra_got)
    else:
        output_part = jnp.concatenate(output_parts, axis=0)
        extra_near, extra_far = gather_whole(extra)

    *mixed, normed, query, key, value, qkv_weight, logs = attend(
        inputs,
        norm_gain,
        (query_weight, key_weight, value_weight),
        tables,
        heads_width // HD,
        groups_width // HD,
        tp_at,
    )
    if fine:
        mixed, output_got, extra_held, extra_got = join(mixed, output_got, extra_held, extra_got)

    mixed = [mixed[0]] + [turn(mixed[s], s) for s in range(1, n_tp)]
    if fine:
        output_held, output_got = gather_second(output_part, output_got)
        extra_near = gather_near(extra_held, extra_got)
        mixed, output_held, output_got, extra_near = join(mixed, output_held, output_got, extra_near)
        near = gather_near(output_held, output_got)
        far = swap(near, 1)
        extra_far = swap(extra_near, 1)
    else:
        near, far = gather_whole(output_part)
    halves = gather_halves()
    output_whole = jnp.zeros((n_tp, n_ep, part, width), BF)
    for j, blocks in enumerate((near, far)):
        blocks = blocks.reshape(n_ep, n_tp // 2, part, width)
        for k in range(n_ep):
            device, half = halves[j * n_ep + k]
            for u in range(n_tp // 2):
                place = (n_tp - half * (n_tp // 2) - u) % n_tp
                output_whole = lax.dynamic_update_slice(
                    output_whole, blocks[k, u][None, None], (place, device, 0, 0)
                )
    output_whole = output_whole.reshape(n_tp * heads_width, width)

    mixed_mine = jnp.concatenate(mixed, axis=1)
    branch = mul(mixed_mine, output_whole)
    inputs_mine = mine(inputs).astype(F32)
    attended = inputs_mine + branch
    inverse_two = lax.rsqrt(jnp.mean(attended * attended, axis=-1, keepdims=True) + EPS)
    unit_two = attended * inverse_two
    routed_in = (unit_two * mixer_gain).astype(BF)
    logits = mul(routed_in, router_weight)
    ids = jnp.arange(experts, dtype=jnp.int32)
    chosen = jnp.any(routes_mine[:, :, None] == ids[None, None, :], axis=1)
    logits = jnp.where(chosen, logits, MASKED)
    weights = jnp.where(chosen, jnp.exp(logits - jnp.max(logits, axis=-1, keepdims=True)), 0.0)
    gates = weights / jnp.sum(weights, axis=-1, keepdims=True)

    router = jnp.pad(router_weight, ((0, 0), (0, LANES - experts)))
    order = jnp.concatenate([ep_at[None], jnp.full((1,), experts, jnp.int32)])
    if fine:
        got = gather_first(routed_in)
        got, gates, router, order = join(got, gates, router, order)
        held, got = gather_second(routed_in, got)
        held, got = join(held, got)
        near = gather_near(held, got)
        far = swap(near, 1)
    else:
        near, far = gather_whole(routed_in)
    out_near, out_far, gin_near, gin_far, terms = run_experts(
        order, near, far, extra_near, extra_far, router, expert_parts, top, n_tp
    )

    grad_expert = lax.psum_scatter(terms, "tp", scatter_dimension=0, tiled=True)

    if fine:
        gin = sum_cores(gin_near, swap(gin_far, 1))
        got = sum_first(gin)
        out_far, gin = join(out_far, gin)
        out_far = swap(out_far, 1)
        got, out_far = join(got, out_far)
        gin, got = sum_second(gin, got)
        out = sum_cores(out_near, out_far)
        out_got = sum_first(out)
        gin, got = join(gin, got)
        grad_in = sum_last(gin, got)
    else:
        grad_in = sum_whole(gin_near, gin_far)
    grad_gates = grad_in[:, width : width + experts] + grad_in[:, width + experts : width + 2 * experts]
    inner_gate = jnp.sum(gates * grad_gates, axis=-1, keepdims=True)
    grad_logits = (gates * (grad_gates - inner_gate)).astype(BF)
    grad_routed = grad_in[:, :width] + mul(grad_logits, router_weight, NT)
    grad_top = grad_top_mine.astype(F32)
    scaled_two = grad_routed * mixer_gain
    grad_attended = grad_top + inverse_two * (
        scaled_two - unit_two * jnp.mean(scaled_two * unit_two, axis=-1, keepdims=True)
    )
    grad_branch = grad_attended.astype(BF)
    grad_mixed = mul(grad_branch, output_whole, NT).astype(BF)
    grad_mixed = [grad_mixed[:, s * heads_width : (s + 1) * heads_width] for s in range(n_tp)]

    if fine:
        grad_mixed, out_got = join(grad_mixed, out_got)
    grad_mixed = [grad_mixed[0]] + [turn(grad_mixed[s], -s) for s in range(1, n_tp)]
    if fine:
        out, out_got = sum_second(out, out_got)

    few = -(-(1 + experts) // n_ep)
    pad = 16 * (few // 16 + 1)
    small_rows = -(-few // 8) * 8
    grad_router = mul(routed_in, grad_logits, TN)
    grad_mixer = jnp.sum(grad_routed * unit_two, axis=0)
    small = jnp.concatenate([grad_mixer[None], grad_router.T], axis=0).astype(BF)
    small = jnp.pad(small, ((0, few * n_ep - 1 - experts), (0, 0))).reshape(n_ep, few, width)
    small = jnp.pad(small, ((0, 0), (0, pad - few), (0, 0)))
    grad_output = mul(mixed_mine, grad_branch, TN).astype(BF)
    grad_output = grad_output.reshape(n_tp, n_ep, part, width).transpose(1, 0, 2, 3)
    grad_output = jnp.concatenate([grad_output.reshape(n_ep, n_tp * part, width), small], axis=1)
    if fine:
        core, chip = lax.rem(ep_at, 2), lax.div(ep_at, 2)
        grad_output = grad_output.reshape((n_ep // 2, 2) + grad_output.shape[1:])
        other_output = lax.dynamic_index_in_dim(grad_output, 1 - core, 1, False)
        grad_output = lax.dynamic_index_in_dim(grad_output, core, 1, False)
        grad_mixed, out, out_got, other_output, grad_output = join(
            grad_mixed, out, out_got, other_output, grad_output
        )
        out = sum_last(out, out_got)
        other_output = swap(other_output, 1)
    else:
        out = sum_whole(out_near, out_far)
    result_mine = (attended + out).astype(BF)

    result_mine, grad_mixed = join(result_mine, grad_mixed)
    result_steps = [step_both(result_mine, result_mine)]
    grad_qkv = attend_back(grad_mixed, query, key, value, logs, tables, tp_at)
    if fine:
        grad_qkv, result_steps[0], other_output = join(grad_qkv, result_steps[0], other_output)
    else:
        grad_qkv, result_steps[0] = join(grad_qkv, result_steps[0])

    grad_normed = mul(grad_qkv, qkv_weight, NT).astype(BF).reshape(n_tp, quarter, width)
    grad_qkv_w = mul(normed, grad_qkv, TN).astype(BF)
    if fine:
        grad_output = add(grad_output, other_output)

    def block(j):
        return lax.dynamic_index_in_dim(grad_normed, lax.rem(tp_at + j + n_tp, n_tp), 0, False)

    def chip_half(j, half):
        rows = grad_output.shape[1] // 2
        chip_rows = lax.dynamic_index_in_dim(grad_output, jnp.bitwise_xor(chip, j), 0, False)
        return chip_rows[half * rows : (half + 1) * rows]

    if fine:
        sums = join(
            *[
                jnp.concatenate([chip_half(a, half), chip_half(c, half)], axis=0)
                for half, places in ((0, ((0, 1), (2, 3))), (1, ((0, 2), (1, 3))))
                for a, c in places
            ]
        )
        got = sum_first(sums)
    result_steps.append(step_both(*result_steps[-1], 1))
    sent = step_ends(block(n_tp - 1), block(1 - n_tp), 0, 1)
    if fine:
        sent, result_steps[-1], got, grad_qkv_w, grad_expert = join(
            sent, result_steps[-1], got, grad_qkv_w, grad_expert
        )
        sums, got = sum_second(sums, got)
    else:
        sent, result_steps[-1], grad_qkv_w, grad_expert = join(
            sent, result_steps[-1], grad_qkv_w, grad_expert
        )
    grad_qkv_w = lax.psum(grad_qkv_w, "ep")
    sent = by_side(sent, 0, 1)
    result_last = None
    for t in range(2, n_tp):
        sent = step_both(add(block(n_tp - t), sent[0]), add(block(t - n_tp), sent[1]), 0, t)
        if t < n_tp - 1:
            result_last = step_ends(*result_steps[-1], t, n_tp - 1)
            if fine:
                sent, result_last, got, sums = join(sent, result_last, got, sums)
                grad_output = sum_last(sums, got).astype(BF)
            else:
                sent, result_last = join(sent, result_last)
                grad_output = lax.psum_scatter(grad_output, "ep", scatter_dimension=0, tiled=False)
            pieces = [
                jnp.concatenate([grad_output[s * part : (s + 1) * part], grad_output[n_tp * part :][:small_rows]], axis=0)
                for s in range(n_tp)
            ]
    got = [turn(pieces[s], -s) for s in range(1, n_tp)]
    sent, result_steps, result_last = join(sent, result_steps, result_last)
    grad_normed = block(0).astype(F32) + sent[0].astype(F32) + sent[1].astype(F32)
    inverse_one = lax.rsqrt(jnp.mean(inputs_mine * inputs_mine, axis=-1, keepdims=True) + EPS)
    unit_one = inputs_mine * inverse_one
    scaled_one = grad_normed * norm_gain
    grad_inputs = grad_attended + inverse_one * (
        scaled_one - unit_one * jnp.mean(scaled_one * unit_one, axis=-1, keepdims=True)
    )
    grad_inputs = grad_inputs.astype(BF)
    grad_norm = jnp.sum(grad_normed * unit_one, axis=0)
    used = -(-(part + small_rows + 1) // 32) * 32

    grad_inputs, grad_norm = join(grad_inputs, grad_norm)
    input_steps = [step_both(grad_inputs, grad_inputs)]
    grad_norm = grad_norm[None]
    norm_got = [turn(grad_norm, s) for s in range(1, n_tp)]
    got, norm_got, input_steps[0] = join(got, norm_got, input_steps[0])
    grad_norm = (grad_norm + sum(norm_got))[0]
    grad_output = (pieces[0].astype(F32) + sum(v.astype(F32) for v in got)).astype(BF)
    grad_output = jnp.pad(grad_output, ((0, used - grad_output.shape[0]), (0, 0)))
    grad_output = grad_output.at[used - 1].set(grad_norm.astype(BF))
    if fine:
        got = [swap(grad_output, k) for k in (2, 4, 6)]
    grad_expert = grad_expert.reshape(3, -1, width).astype(F32)
    grad_gate_w, grad_up_w, grad_down_w = grad_expert[0].T, grad_expert[1].T, grad_expert[2]
    for t in range(1, n_tp - 2):
        input_steps.append(step_both(*input_steps[-1], t))
    if fine:
        got, input_steps[-1], grad_gate_w, grad_up_w, grad_down_w = join(
            got, input_steps[-1], grad_gate_w, grad_up_w, grad_down_w
        )
        near = jnp.concatenate([grad_output] + got, axis=0)
        far = swap(near, 1)
        far, grad_qkv_w = join(far, grad_qkv_w)
        devices = jnp.stack([jnp.bitwise_xor(ep_at, jnp.int32(k)) for k in (0, 2, 4, 6, 1, 3, 5, 7)])
        grad_output, small, grad_norm = set_rows(devices, near, far, part, small_rows)
        small = small.reshape(n_ep, small_rows, width)
        grad_norm = grad_norm[0]
    else:
        gathered = lax.all_gather(grad_output, "ep")
        small = gathered[:, part : part + small_rows].astype(F32)
        grad_norm = jnp.sum(gathered[:, used - 1].astype(F32), axis=0)
        grad_output = gathered[:, :part].reshape(heads_width, width).astype(F32)
    small = small[:, :few].reshape(n_ep * few, width)[: 1 + experts]
    result = spread(result_mine, result_steps, result_last)
    input_last = step_ends(*input_steps[-1], n_tp - 2, n_tp - 1)
    grad_qkv_w = grad_qkv_w.astype(F32)
    qkv_grads = (
        grad_qkv_w[:, :heads_width],
        grad_qkv_w[:, heads_width : heads_width + groups_width],
        grad_qkv_w[:, heads_width + groups_width :],
    )
    grad_norm, small, grad_output, input_last, qkv_grads, result = join(
        grad_norm, small, grad_output, input_last, qkv_grads, result
    )
    grad_inputs = spread(grad_inputs, input_steps, input_last)
    return (
        result,
        grad_inputs,
        grad_norm,
        *qkv_grads,
        grad_output,
        small[0],
        small[1:].T,
        grad_gate_w[None],
        grad_up_w[None],
        grad_down_w[None],
    )


def solution(mesh):
    placed = (
        P("ep", None),
        P("ep", None),
        P(),
        P(None, "tp"),
        P(None, "tp"),
        P(None, "tp"),
        P("tp", None),
        P(),
        P(),
        P("ep", None, "tp"),
        P("ep", None, "tp"),
        P("ep", "tp", None),
        P("ep", None),
    )
    return jax.shard_map(
        body,
        mesh=mesh,
        in_specs=placed,
        out_specs=(
            P("ep", None),
            P("ep", None),
            P(),
            P(None, "tp"),
            P(None, "tp"),
            P(None, "tp"),
            P("tp", None),
            P(),
            P(),
            P("ep", None, "tp"),
            P("ep", None, "tp"),
            P("ep", "tp", None),
        ),
        check_vma=False,
    )
```

```python
import functools

import jax
import jax.numpy as jnp
import numpy as np
from jax import lax
from jax.experimental import pallas as pl
from jax.experimental.pallas import tpu as pltpu
from jax.sharding import PartitionSpec as P

HD = 64
LEN = 1024
EPS = 1e-06
MASKED = -1e30
BF = jnp.bfloat16
F32 = jnp.float32
BLOCK = 256
LANES = 128
NT = (((1,), (1,)), ((), ()))
TN = (((0,), (0,)), ((), ()))


def takes(us):
    return pl.CostEstimate(flops=int(us * 1.15e9), bytes_accessed=0, transcendentals=0)


def mul(a, b, dims=(((1,), (0,)), ((), ()))):
    return lax.dot_general(a, b, dims, preferred_element_type=F32)


def rotate_lanes(y, cos, sin):
    half = HD // 2
    first = lax.broadcasted_iota(jnp.int32, y.shape, 1) % HD < half
    return y * cos + jnp.where(first, pltpu.roll(y, 128 - half, 1), pltpu.roll(y, half, 1)) * sin


def rotary_lanes(tokens):
    lane = np.arange(128)
    freqs = np.float32(10000.0) ** (-(lane % (HD // 2)).astype(np.float32) * np.float32(2.0 / HD))
    angles = (np.arange(tokens) % LEN).astype(np.float32)[:, None] * freqs[None, :].astype(np.float32)
    sign = np.where(lane % HD < HD // 2, np.float32(-1.0), np.float32(1.0))
    return jnp.asarray(np.cos(angles), F32), jnp.asarray(np.sin(angles) * sign, F32)


def causal(block):
    key_at = lax.broadcasted_iota(jnp.int32, (block, block), 0)
    query_at = lax.broadcasted_iota(jnp.int32, (block, block), 1)
    return key_at <= query_at


def attend_kernel(at_ref, x_ref, gain_ref, wq_ref, wk_ref, wv_ref, cos_ref, sin_ref, *refs):
    pieces, (q_ref, k_ref, v_ref, log_ref, w_ref, vt_ref, out_ref) = refs[:-7], refs[-7:]
    tokens = x_ref.shape[0]
    heads, groups = q_ref.shape[0], k_ref.shape[0]
    repeat = heads // groups
    per = 128 // HD
    scale = HD ** (-0.5)
    w_ref[...] = jnp.concatenate([wq_ref[...], wk_ref[...], wv_ref[...]], axis=1)

    @pl.loop(0, tokens // BLOCK)
    def _(i):
        at = pl.multiple_of(i * BLOCK, BLOCK)
        rows = pl.ds(at, BLOCK)
        x = x_ref[rows, :].astype(F32)
        inverse = lax.rsqrt(jnp.mean(x * x, axis=-1, keepdims=True) + EPS)
        normed = (x * inverse * gain_ref[...]).astype(BF)
        raw = mul(normed, w_ref[...])
        tables = (cos_ref[rows, :], sin_ref[rows, :])
        for h in range(0, heads, per):
            turned = rotate_lanes(raw[:, h * HD : h * HD + 128], *tables) * scale
            for u in range(per):
                q_ref[h + u, rows, :] = turned[:, u * HD : (u + 1) * HD].astype(BF)
        for g in range(0, groups, per):
            lane = (heads + g) * HD
            turned = rotate_lanes(raw[:, lane : lane + 128], *tables)
            lane = (heads + groups + g) * HD
            value = raw[:, lane : lane + 128]
            turned_value = value.T
            for u in range(per):
                k_ref[g + u, rows, :] = turned[:, u * HD : (u + 1) * HD].astype(BF)
                v_ref[g + u, rows, :] = value[:, u * HD : (u + 1) * HD].astype(BF)
                vt_ref[g + u, :, rows] = turned_value[u * HD : (u + 1) * HD].astype(BF)

    keep = causal(BLOCK)

    @pl.loop(0, heads)
    def _(h):
        g = h // repeat
        for i in range(tokens // BLOCK):
            start, stop = i * BLOCK, (i + 1) * BLOCK
            query = q_ref[h, start:stop, :]
            parts = [jnp.where(keep, mul(k_ref[g, start:stop, :], query, NT), MASKED)]
            if i:
                parts.append(mul(k_ref[g, :start, :], query, NT))
            peak = jnp.max(parts[0], axis=0, keepdims=True)
            for part in parts[1:]:
                peak = jnp.maximum(peak, jnp.max(part, axis=0, keepdims=True))
            weights = [jnp.exp(part - peak) for part in parts]
            total = sum(jnp.sum(w, axis=0, keepdims=True) for w in weights)
            shrink = 1.0 / total
            mixed = mul(vt_ref[g, :, start:stop], (weights[0] * shrink).astype(BF))
            if i:
                mixed += mul(vt_ref[g, :, :start], (weights[1] * shrink).astype(BF))
            out_ref[h, :, start:stop] = mixed
            log_ref[h, :, start:stop] = peak + jnp.log(total)

    for s, piece_ref in enumerate(pieces):
        span = pl.ds(pl.multiple_of(lax.rem(at_ref[0] + s, len(pieces)) * BLOCK, BLOCK), BLOCK)
        for h in range(0, heads, per):
            pair = jnp.concatenate([out_ref[h + u, :, span] for u in range(per)], axis=0)
            piece_ref[:, h * HD : h * HD + 128] = pair.T.astype(BF)


VMEM = pl.BlockSpec(memory_space=pltpu.VMEM)
SMEM = pl.BlockSpec(memory_space=pltpu.SMEM)


def attend(x, gain, weights, tables, heads, groups, at):
    tokens, width = x.shape
    count = tokens // BLOCK
    return pl.pallas_call(
        attend_kernel,
        in_specs=[SMEM] + [VMEM] * 7,
        out_shape=[jax.ShapeDtypeStruct((BLOCK, heads * HD), BF)] * count
        + [
            jax.ShapeDtypeStruct((heads, tokens, HD), BF),
            jax.ShapeDtypeStruct((groups, tokens, HD), BF),
            jax.ShapeDtypeStruct((groups, tokens, HD), BF),
            jax.ShapeDtypeStruct((heads, 1, tokens), F32),
        ],
        scratch_shapes=[
            pltpu.VMEM((width, (heads + 2 * groups) * HD), BF),
            pltpu.VMEM((groups, HD, tokens), BF),
            pltpu.VMEM((heads, HD, tokens), F32),
        ],
        compiler_params=pltpu.CompilerParams(vmem_limit_bytes=48 << 20),
        cost_estimate=takes(20),
    )(at[None], x, gain[None], *weights, *tables)


def attend_back_kernel(at_ref, q_ref, k_ref, v_ref, log_ref, cos_ref, sin_ref, wq_ref, wk_ref, wv_ref, *refs):
    w_ref, do_ref, kt_ref, dq_ref, dk_ref, dv_ref = refs[-6:]
    out_ref, end_ref = refs[-8:-6]
    count = (len(refs) - 8) // 2
    grad_refs, block_refs = refs[:count], refs[count:-8]
    tokens = q_ref.shape[1]
    heads, groups = q_ref.shape[0], k_ref.shape[0]
    repeat = heads // groups
    per = 128 // HD
    scale = HD ** (-0.5)
    w_ref[...] = jnp.concatenate([wq_ref[...], wk_ref[...], wv_ref[...]], axis=1)
    dk_ref[...] = jnp.zeros_like(dk_ref)
    dv_ref[...] = jnp.zeros_like(dv_ref)

    def span_of(s):
        return pl.ds(pl.multiple_of(lax.rem(at_ref[0] + s, count) * BLOCK, BLOCK), BLOCK)

    for s, grad_ref in enumerate(grad_refs):
        for h in range(heads):
            do_ref[h, span_of(s), :] = grad_ref[:, h * HD : (h + 1) * HD]

    @pl.loop(0, tokens // BLOCK)
    def _(i):
        rows = pl.ds(pl.multiple_of(i * BLOCK, BLOCK), BLOCK)
        for g in range(groups):
            kt_ref[g, :, rows] = k_ref[g, rows, :].astype(F32).T.astype(BF)

    keep = causal(BLOCK)

    @pl.loop(0, heads)
    def _(h):
        g = h // repeat
        for i in range(tokens // BLOCK):
            start, stop = i * BLOCK, (i + 1) * BLOCK
            query = q_ref[h, start:stop, :]
            grads = do_ref[h, start:stop, :]
            log_total = log_ref[h, :, start:stop]
            spans = [(start, stop)] + ([(0, start)] if i else [])
            probs, grad_probs = [], []
            for lo, hi in spans:
                scores = mul(k_ref[g, lo:hi, :], query, NT)
                if hi == stop:
                    scores = jnp.where(keep, scores, MASKED)
                probs.append(jnp.exp(scores - log_total))
                grad_probs.append(mul(v_ref[g, lo:hi, :], grads, NT))
            inner = sum(jnp.sum(p * d, axis=0, keepdims=True) for p, d in zip(probs, grad_probs))
            dq = None
            for (lo, hi), p, d in zip(spans, probs, grad_probs):
                ds = (p * (d - inner)).astype(BF)
                dk_ref[g, lo:hi, :] += mul(ds, query)
                dv_ref[g, lo:hi, :] += mul(p.astype(BF), grads)
                term = mul(kt_ref[g, :, lo:hi], ds)
                dq = term if dq is None else dq + term
            dq_ref[h, :, start:stop] = dq * scale

    @pl.loop(0, tokens // BLOCK)
    def _(i):
        rows = pl.ds(pl.multiple_of(i * BLOCK, BLOCK), BLOCK)
        tables = (cos_ref[rows, :], -sin_ref[rows, :])
        for h in range(0, heads, per):
            pair = jnp.concatenate([dq_ref[h + u, :, rows] for u in range(per)], axis=0).T
            out_ref[rows, h * HD : h * HD + 128] = rotate_lanes(pair, *tables).astype(BF)
        for g in range(0, groups, per):
            pair = jnp.concatenate([dk_ref[g + u, rows, :] for u in range(per)], axis=1)
            lane = (heads + g) * HD
            out_ref[rows, lane : lane + 128] = rotate_lanes(pair, *tables).astype(BF)
            pair = jnp.concatenate([dv_ref[g + u, rows, :] for u in range(per)], axis=1)
            lane = (heads + groups + g) * HD
            out_ref[rows, lane : lane + 128] = pair.astype(BF)


    for s, block_ref in enumerate(block_refs):
        block_ref[...] = mul(out_ref[span_of(s), :], w_ref[...], NT).astype(BF)

    @pl.when(at_ref[0] < count // 2)
    def _():
        end_ref[...] = block_refs[count - 1][...]

    @pl.when(at_ref[0] >= count // 2)
    def _():
        end_ref[...] = block_refs[1][...]


def attend_back(grad_pieces, q, k, v, logs, tables, weights, at):
    heads, tokens, _ = q.shape
    groups = k.shape[0]
    count = len(grad_pieces)
    lanes = (heads + 2 * groups) * HD
    width = weights[0].shape[0]
    block = jax.ShapeDtypeStruct((BLOCK, width), BF)
    return pl.pallas_call(
        attend_back_kernel,
        in_specs=[SMEM] + [VMEM] * (9 + count),
        out_shape=[block] * count + [jax.ShapeDtypeStruct((tokens, lanes), BF), block],
        scratch_shapes=[
            pltpu.VMEM((width, lanes), BF),
            pltpu.VMEM((heads, tokens, HD), BF),
            pltpu.VMEM((groups, HD, tokens), BF),
            pltpu.VMEM((heads, HD, tokens), F32),
            pltpu.VMEM((groups, tokens, HD), F32),
            pltpu.VMEM((groups, tokens, HD), F32),
        ],
        compiler_params=pltpu.CompilerParams(vmem_limit_bytes=48 << 20),
        cost_estimate=takes(20),
    )(at[None], q, k, v, logs, *tables, *weights, *grad_pieces)


def pack_kernel(gate_ref, up_ref, down_ref, out_ref):
    part = down_ref.shape[0]
    out_ref[:part, :] = gate_ref[...].astype(F32).T.astype(BF)
    out_ref[part : 2 * part, :] = up_ref[...].astype(F32).T.astype(BF)
    out_ref[2 * part :, :] = down_ref[...]


def pack(gate, up, down):
    return pl.pallas_call(
        pack_kernel,
        out_shape=jax.ShapeDtypeStruct((3 * down.shape[0], down.shape[1]), BF),
        compiler_params=pltpu.CompilerParams(vmem_limit_bytes=32 << 20),
        cost_estimate=takes(3),
    )(gate, up, down)


def expert_kernel(order_ref, near_ref, far_ref, extra_near_ref, extra_far_ref, router_ref, parts_ref, *refs, top, count):
    out_refs, gin_refs, terms_ref = refs[:2], refs[2:4], refs[4]
    weights_ref, sums_ref = refs[5:]
    step = pl.program_id(0)
    steps = pl.num_programs(0)
    hidden_width, width = weights_ref.shape[0] // 3, weights_ref.shape[1]
    gate_up = slice(0, 2 * hidden_width)
    down = slice(2 * hidden_width, 3 * hidden_width)
    own = order_ref[0]
    experts = order_ref[1]
    part = hidden_width // count
    spans = [
        (pl.ds((3 * s + j) * part, part), pl.ds(j * hidden_width + s * part, part))
        for s in range(count)
        for j in range(3)
    ]

    @pl.when(step == 0)
    def _():
        sums_ref[...] = jnp.zeros_like(sums_ref)
        for there, here in spans:
            weights_ref[here, :] = parts_ref[there, :]

    near = step < steps // 2
    rows = jnp.where(near, near_ref[...], far_ref[...])
    extra = jnp.where(near, extra_near_ref[...], extra_far_ref[...])
    grads32 = extra[:, :width].astype(F32)
    named = extra[:, width:].astype(F32)

    lane = lax.broadcasted_iota(jnp.int32, (rows.shape[0], LANES), 1)
    lane32 = lane.astype(F32)
    chosen = lane32 == named[:, 0:1]
    for k in range(1, top):
        chosen = chosen | (lane32 == named[:, k : k + 1])
    logits = jnp.where(chosen, mul(rows, router_ref[...]), MASKED)
    weights = jnp.where(chosen, jnp.exp(logits - jnp.max(logits, axis=-1, keepdims=True)), 0.0)
    mine = jnp.sum(jnp.where(lane == own, weights, 0.0), axis=-1, keepdims=True)
    gate = mine / jnp.sum(weights, axis=-1, keepdims=True)

    both = mul(rows, weights_ref[gate_up, :], NT)
    gate_vals = both[:, :hidden_width]
    up_vals = both[:, hidden_width:]
    sigma = jax.nn.sigmoid(gate_vals)
    active = gate_vals * sigma
    hidden = (active * up_vals).astype(BF)
    grad_out = (gate * grads32).astype(BF)
    grad_hidden = mul(grad_out, weights_ref[down, :], NT)
    expert_out = mul(hidden, weights_ref[down, :])
    combined = (gate * expert_out).astype(BF)
    score = jnp.sum(grads32 * expert_out, axis=-1, keepdims=True)
    high = score.astype(BF).astype(F32)
    scores = jnp.where(lane == own, high, jnp.where(lane == own + experts, score - high, 0.0)).astype(BF)
    grad_gate_vals = (grad_hidden * up_vals * sigma * (1.0 + gate_vals * (1.0 - sigma))).astype(BF)
    grad_up_vals = (grad_hidden * active).astype(BF)
    grad_both = jnp.concatenate([grad_gate_vals, grad_up_vals], axis=1)
    grad_in = mul(grad_both, weights_ref[gate_up, :]).astype(BF)
    sums_ref[gate_up, :] += mul(grad_both, rows, TN)
    sums_ref[down, :] += mul(hidden, grad_out, TN)
    for far in range(2):

        @pl.when(near if far == 0 else step >= steps // 2)
        def _():
            out_refs[far][...] = combined
            gin_refs[far][:, :width] = grad_in
            gin_refs[far][:, width:] = scores

    @pl.when(step == steps - 1)
    def _():
        for there, here in spans:
            terms_ref[there, :] = sums_ref[here, :].astype(BF)


def run_experts(order, near, far, extra_near, extra_far, router, parts, top, count):
    total, width = 2 * near.shape[0], near.shape[1]
    steps = total // BLOCK
    half_steps = steps // 2
    wide = extra_near.shape[1]
    hidden = parts.shape[0] // 3

    def by_set(lanes):
        return [
            pl.BlockSpec((BLOCK, lanes), lambda i, o: (jnp.minimum(i, half_steps - 1), 0)),
            pl.BlockSpec((BLOCK, lanes), lambda i, o: (jnp.maximum(i - half_steps, 0), 0)),
        ]

    half, half_wide = by_set(width), by_set(wide)
    whole = pl.BlockSpec((3 * hidden, width), lambda i, o: (0, 0), pipeline_mode=pl.Buffered(1))
    return pl.pallas_call(
        functools.partial(expert_kernel, top=top, count=count),
        grid_spec=pltpu.PrefetchScalarGridSpec(
            num_scalar_prefetch=1,
            grid=(steps,),
            in_specs=[
                *by_set(width),
                *by_set(wide),
                pl.BlockSpec((width, LANES), lambda i, o: (0, 0)),
                whole,
            ],
            out_specs=half + half_wide + [whole],
            scratch_shapes=[
                pltpu.VMEM((3 * hidden, width), BF),
                pltpu.VMEM((3 * hidden, width), F32),
            ],
        ),
        out_shape=[jax.ShapeDtypeStruct((total // 2, width), BF)] * 2
        + [jax.ShapeDtypeStruct((total // 2, wide), BF)] * 2
        + [jax.ShapeDtypeStruct((3 * hidden, width), BF)],
        compiler_params=pltpu.CompilerParams(vmem_limit_bytes=58 << 20),
        cost_estimate=takes(5 * steps),
    )(order, near, far, extra_near, extra_far, router, parts)


def set_rows_kernel(order_ref, near_ref, far_ref, out_ref, small_ref, norm_ref, *, part, few_rows):
    rows, width = near_ref.shape[0] // 4, near_ref.shape[1]
    norm = jnp.zeros((1, width), F32)
    for k in range(8):
        source = near_ref if k < 4 else far_ref
        block = source[(k % 4) * rows : (k % 4 + 1) * rows, :].astype(F32)
        device = order_ref[k]
        out_ref[pl.ds(pl.multiple_of(device * part, 8), part), :] = block[:part]
        small_ref[pl.ds(pl.multiple_of(device * few_rows, 8), few_rows), :] = block[part : part + few_rows]
        norm += block[rows - 1 :]
    norm_ref[...] = norm


def set_rows(order, near, far, part, few_rows):
    width = near.shape[1]
    return pl.pallas_call(
        functools.partial(set_rows_kernel, part=part, few_rows=few_rows),
        in_specs=[SMEM, VMEM, VMEM],
        out_shape=[
            jax.ShapeDtypeStruct((8 * part, width), F32),
            jax.ShapeDtypeStruct((8 * few_rows, width), F32),
            jax.ShapeDtypeStruct((1, width), F32),
        ],
        compiler_params=pltpu.CompilerParams(vmem_limit_bytes=32 << 20),
        cost_estimate=takes(3),
    )(order, near, far)


def join(*values):
    return lax.optimization_barrier(values)


def add(a, b):
    return (a.astype(F32) + b.astype(F32)).astype(BF)


def swap(x, bit):
    return lax.ppermute(x, "ep", [(i, i ^ bit) for i in range(lax.axis_size("ep"))])


def turn(x, by):
    n = lax.axis_size("tp")
    return lax.ppermute(x, "tp", [(i, (i + by) % n) for i in range(n)])


def step_both(right, left, low=0, high=None):
    n = lax.axis_size("tp")
    pairs = [(i, i + 1) for i in range(low, n - 1 if high is None else high)]
    mirror = [(n - 1 - i, n - 1 - j) for i, j in pairs]
    return lax.ppermute(right, "tp", pairs), lax.ppermute(left, "tp", mirror)


def step_ends(right, left, low, high):
    n = lax.axis_size("tp")
    at = lax.axis_index("tp")
    pairs = [(i, i + 1) for i in range(low, high)]
    give = right if right is left else jnp.where((at >= low) & (at < high), right, left)
    return lax.ppermute(give, "tp", pairs + [(n - 1 - i, n - 1 - j) for i, j in pairs])


def by_side(got, low, high):
    at = lax.axis_index("tp")
    ahead = (at > low) & (at <= high)
    return jnp.where(ahead, got, 0), jnp.where(ahead, 0, got)


def gather_first(x):
    half = x.shape[0] // 2
    return swap(x[:half], 2), swap(x[half:], 4)


def gather_second(x, got):
    half = x.shape[0] // 2
    first, second = join(
        jnp.concatenate([x[:half], got[0]], axis=0), jnp.concatenate([x[half:], got[1]], axis=0)
    )
    return (first, second), (swap(first, 4), swap(second, 2))


def gather_near(held, got):
    return jnp.concatenate([held[0], got[0], held[1], got[1]], axis=0)


def gather_halves():
    n = lax.axis_size("ep")
    if n != 8:
        return [(jnp.int32(k // 2), k % 2) for k in range(2 * n)]
    at = lax.axis_index("ep").astype(jnp.int32)
    near = [(0, 0), (2, 0), (4, 0), (6, 0), (0, 1), (4, 1), (2, 1), (6, 1)]
    return [(jnp.bitwise_xor(at, k + core), half) for core in (0, 1) for k, half in near]


def gather_whole(x):
    whole = lax.all_gather(x, "ep", tiled=True)
    return whole[: whole.shape[0] // 2], whole[whole.shape[0] // 2 :]


def sum_cores(near, far):
    rows = near.shape[0] // 4
    return join(*[add(near[j * rows : (j + 1) * rows], far[j * rows : (j + 1) * rows]) for j in range(4)])


def sum_first(sums):
    return swap(sums[1], 4), swap(sums[3], 2)


def sum_second(sums, got):
    first, second = join(add(sums[0], got[0]), add(sums[2], got[1]))
    half = first.shape[0] // 2
    return (first, second), (swap(first[half:], 2), swap(second[half:], 4))


def sum_last(sums, got):
    half = sums[0].shape[0] // 2
    return jnp.concatenate([s[:half].astype(F32) + g.astype(F32) for s, g in zip(sums, got)], axis=0)


def sum_whole(near, far):
    n = lax.axis_size("ep")
    terms = jnp.concatenate([near, far], axis=0).reshape(n, -1, near.shape[1])
    return lax.psum_scatter(terms, "ep", scatter_dimension=0, tiled=False).astype(F32)


def spread(own, steps, last):
    n = lax.axis_size("tp")
    at = lax.axis_index("tp").astype(jnp.int32)
    rows, width = own.shape
    out = jnp.zeros((n * rows, width), BF)
    for t, step in enumerate(steps):
        for got, place in zip(step, (at - t - 1, at + t + 1)):
            place = jnp.where((place >= 0) & (place < n), place, at)
            out = lax.dynamic_update_slice(out, got, (place * rows, 0))
    place = jnp.where(at == n - 1, 0, jnp.where(at == 0, n - 1, at))
    out = lax.dynamic_update_slice(out, last, (place * rows, 0))
    return lax.dynamic_update_slice(out, own, (at * rows, 0))


def body(
    inputs,
    routes,
    norm_gain,
    query_weight,
    key_weight,
    value_weight,
    output_weight,
    mixer_gain,
    router_weight,
    gate_weight,
    up_weight,
    down_weight,
    cotangent,
):
    tokens, width = inputs.shape
    experts = router_weight.shape[1]
    top = routes.shape[1]
    n_ep = lax.axis_size("ep")
    n_tp = lax.axis_size("tp")
    fine = n_ep == 8
    ep_at = lax.axis_index("ep").astype(jnp.int32)
    tp_at = lax.axis_index("tp").astype(jnp.int32)
    quarter = tokens // n_tp
    heads_width = query_weight.shape[1]
    groups_width = key_weight.shape[1]

    def mine(x):
        return lax.dynamic_slice_in_dim(x, tp_at * quarter, quarter, 0)

    part = output_weight.shape[0] // n_ep
    output_part = lax.dynamic_slice_in_dim(output_weight, ep_at * part, part, 0)
    output_parts = [output_part] + [turn(output_part, -s) for s in range(1, n_tp)]

    hidden_part = gate_weight.shape[2]
    expert_part = pack(gate_weight[0], up_weight[0], down_weight[0])
    expert_parts = lax.all_gather(expert_part, "tp", tiled=True)

    routes_mine = mine(routes)
    grad_top_mine = mine(cotangent)
    named = jnp.pad(routes_mine.astype(BF), ((0, 0), (0, LANES - top)), constant_values=-1.0)
    extra = jnp.concatenate([grad_top_mine, named], axis=1)
    tables = rotary_lanes(tokens)
    qkv_weights = (query_weight, key_weight, value_weight)
    if fine:
        extra_got = gather_first(extra)
        output_parts, qkv_weights, expert_part = join(output_parts, qkv_weights, expert_part)
        output_part = jnp.concatenate(output_parts, axis=0)
        output_got = gather_first(output_part)
    else:
        output_part = jnp.concatenate(output_parts, axis=0)
        extra_near, extra_far = gather_whole(extra)

    *mixed, query, key, value, logs = attend(
        inputs,
        norm_gain,
        qkv_weights,
        tables,
        heads_width // HD,
        groups_width // HD,
        tp_at,
    )
    if fine:
        mixed, output_got, extra_got = join(mixed, output_got, extra_got)

    mixed = [mixed[0]] + [turn(mixed[s], s) for s in range(1, n_tp)]
    if fine:
        output_held, output_got = gather_second(output_part, output_got)
        mixed, output_held, output_got = join(mixed, output_held, output_got)
        near = gather_near(output_held, output_got)
        far = swap(near, 1)
        extra_held, extra_got = gather_second(extra, extra_got)
    else:
        near, far = gather_whole(output_part)
    halves = gather_halves()
    output_whole = jnp.zeros((n_tp, n_ep, part, width), BF)
    for j, blocks in enumerate((near, far)):
        blocks = blocks.reshape(n_ep, n_tp // 2, part, width)
        for k in range(n_ep):
            device, half = halves[j * n_ep + k]
            for u in range(n_tp // 2):
                place = (n_tp - half * (n_tp // 2) - u) % n_tp
                output_whole = lax.dynamic_update_slice(
                    output_whole, blocks[k, u][None, None], (place, device, 0, 0)
                )
    output_whole = output_whole.reshape(n_tp * heads_width, width)

    mixed_mine = jnp.concatenate(mixed, axis=1)
    branch = mul(mixed_mine, output_whole)
    inputs_mine = mine(inputs).astype(F32)
    attended = inputs_mine + branch
    inverse_two = lax.rsqrt(jnp.mean(attended * attended, axis=-1, keepdims=True) + EPS)
    unit_two = attended * inverse_two
    routed_in = (unit_two * mixer_gain).astype(BF)
    logits = mul(routed_in, router_weight)
    ids = jnp.arange(experts, dtype=jnp.int32)
    chosen = jnp.any(routes_mine[:, :, None] == ids[None, None, :], axis=1)
    logits = jnp.where(chosen, logits, MASKED)
    weights = jnp.where(chosen, jnp.exp(logits - jnp.max(logits, axis=-1, keepdims=True)), 0.0)
    gates = weights / jnp.sum(weights, axis=-1, keepdims=True)

    router = jnp.pad(router_weight, ((0, 0), (0, LANES - experts)))
    order = jnp.concatenate([ep_at[None], jnp.full((1,), experts, jnp.int32)])
    if fine:
        got = gather_first(routed_in)
        got, gates, router, order, extra_held, extra_got = join(
            got, gates, router, order, extra_held, extra_got
        )
        extra_near = gather_near(extra_held, extra_got)
        extra_far = swap(extra_near, 1)
        held, got = gather_second(routed_in, got)
        held, got = join(held, got)
        near = gather_near(held, got)
        far = swap(near, 1)
    else:
        near, far = gather_whole(routed_in)
    out_near, out_far, gin_near, gin_far, terms = run_experts(
        order, near, far, extra_near, extra_far, router, expert_parts, top, n_tp
    )

    grad_expert = lax.psum_scatter(terms, "tp", scatter_dimension=0, tiled=True)

    if fine:
        gin = sum_cores(gin_near, swap(gin_far, 1))
        got = sum_first(gin)
        out_far, gin = join(out_far, gin)
        out_far = swap(out_far, 1)
        got, out_far = join(got, out_far)
        gin, got = sum_second(gin, got)
        out = sum_cores(out_near, out_far)
        out_got = sum_first(out)
        gin, got = join(gin, got)
        grad_in = sum_last(gin, got)
    else:
        grad_in = sum_whole(gin_near, gin_far)
    grad_gates = grad_in[:, width : width + experts] + grad_in[:, width + experts : width + 2 * experts]
    inner_gate = jnp.sum(gates * grad_gates, axis=-1, keepdims=True)
    grad_logits = (gates * (grad_gates - inner_gate)).astype(BF)
    grad_routed = grad_in[:, :width] + mul(grad_logits, router_weight, NT)
    grad_top = grad_top_mine.astype(F32)
    scaled_two = grad_routed * mixer_gain
    grad_attended = grad_top + inverse_two * (
        scaled_two - unit_two * jnp.mean(scaled_two * unit_two, axis=-1, keepdims=True)
    )
    grad_branch = grad_attended.astype(BF)
    grad_mixed = mul(grad_branch, output_whole, NT).astype(BF)
    grad_mixed = [grad_mixed[:, s * heads_width : (s + 1) * heads_width] for s in range(n_tp)]

    if fine:
        grad_mixed, out_got = join(grad_mixed, out_got)
    grad_mixed = [grad_mixed[0]] + [turn(grad_mixed[s], -s) for s in range(1, n_tp)]
    if fine:
        out, out_got = sum_second(out, out_got)

    few = -(-(1 + experts) // n_ep)
    pad = 16 * (few // 16 + 1)
    small_rows = -(-few // 8) * 8
    grad_router = mul(routed_in, grad_logits, TN)
    grad_mixer = jnp.sum(grad_routed * unit_two, axis=0)
    small = jnp.concatenate([grad_mixer[None], grad_router.T], axis=0).astype(BF)
    small = jnp.pad(small, ((0, few * n_ep - 1 - experts), (0, 0))).reshape(n_ep, few, width)
    small = jnp.pad(small, ((0, 0), (0, pad - few), (0, 0)))
    grad_output = mul(mixed_mine, grad_branch, TN).astype(BF)
    grad_output = grad_output.reshape(n_tp, n_ep, part, width).transpose(1, 0, 2, 3)
    grad_output = jnp.concatenate([grad_output.reshape(n_ep, n_tp * part, width), small], axis=1)
    if fine:
        core, chip = lax.rem(ep_at, 2), lax.div(ep_at, 2)
        grad_output = grad_output.reshape((n_ep // 2, 2) + grad_output.shape[1:])
        other_output = lax.dynamic_index_in_dim(grad_output, 1 - core, 1, False)
        grad_output = lax.dynamic_index_in_dim(grad_output, core, 1, False)
        grad_mixed, out, out_got, other_output, grad_output = join(
            grad_mixed, out, out_got, other_output, grad_output
        )
        out = sum_last(out, out_got)
        other_output = swap(other_output, 1)
    else:
        out = sum_whole(out_near, out_far)
    result_mine = (attended + out).astype(BF)

    result_mine, grad_mixed = join(result_mine, grad_mixed)
    result_steps = [step_both(result_mine, result_mine)]
    *blocks, grad_qkv, end_block = attend_back(grad_mixed, query, key, value, logs, tables, qkv_weights, tp_at)
    if fine:
        blocks, grad_qkv, end_block, result_steps[0], other_output = join(
            blocks, grad_qkv, end_block, result_steps[0], other_output
        )
    else:
        blocks, grad_qkv, end_block, result_steps[0] = join(blocks, grad_qkv, end_block, result_steps[0])

    inputs32 = inputs.astype(F32)
    normed = inputs32 * lax.rsqrt(jnp.mean(inputs32 * inputs32, axis=-1, keepdims=True) + EPS)
    normed = (normed * norm_gain).astype(BF)
    grad_qkv_w = mul(normed, grad_qkv, TN).astype(BF)
    if fine:
        grad_output = add(grad_output, other_output)

    def chip_half(j, half):
        rows = grad_output.shape[1] // 2
        chip_rows = lax.dynamic_index_in_dim(grad_output, jnp.bitwise_xor(chip, j), 0, False)
        return chip_rows[half * rows : (half + 1) * rows]

    if fine:
        sums = join(
            *[
                jnp.concatenate([chip_half(a, half), chip_half(c, half)], axis=0)
                for half, places in ((0, ((0, 1), (2, 3))), (1, ((0, 2), (1, 3))))
                for a, c in places
            ]
        )
        got = sum_first(sums)
    result_steps.append(step_both(*result_steps[-1], 1))
    sent = step_ends(end_block, end_block, 0, 1)
    if fine:
        sent, result_steps[-1], got, grad_qkv_w, grad_expert = join(
            sent, result_steps[-1], got, grad_qkv_w, grad_expert
        )
        sums, got = sum_second(sums, got)
    else:
        sent, result_steps[-1], grad_qkv_w, grad_expert = join(
            sent, result_steps[-1], grad_qkv_w, grad_expert
        )
    grad_qkv_w = lax.psum(grad_qkv_w, "ep")
    sent = by_side(sent, 0, 1)
    result_last = None
    for t in range(2, n_tp):
        sent = step_both(add(blocks[n_tp - t], sent[0]), add(blocks[t], sent[1]), 0, t)
        if t < n_tp - 1:
            result_last = step_ends(*result_steps[-1], t, n_tp - 1)
            if fine:
                sent, result_last, got, sums = join(sent, result_last, got, sums)
                grad_output = sum_last(sums, got).astype(BF)
            else:
                sent, result_last = join(sent, result_last)
                grad_output = lax.psum_scatter(grad_output, "ep", scatter_dimension=0, tiled=False)
            pieces = [
                jnp.concatenate([grad_output[s * part : (s + 1) * part], grad_output[n_tp * part :][:small_rows]], axis=0)
                for s in range(n_tp)
            ]
    got = [turn(pieces[s], -s) for s in range(1, n_tp)]
    sent, result_steps, result_last = join(sent, result_steps, result_last)
    grad_normed = blocks[0].astype(F32) + sent[0].astype(F32) + sent[1].astype(F32)
    inverse_one = lax.rsqrt(jnp.mean(inputs_mine * inputs_mine, axis=-1, keepdims=True) + EPS)
    unit_one = inputs_mine * inverse_one
    scaled_one = grad_normed * norm_gain
    grad_inputs = grad_attended + inverse_one * (
        scaled_one - unit_one * jnp.mean(scaled_one * unit_one, axis=-1, keepdims=True)
    )
    grad_inputs = grad_inputs.astype(BF)
    grad_norm = jnp.sum(grad_normed * unit_one, axis=0)
    used = -(-(part + small_rows + 1) // 32) * 32

    grad_inputs, grad_norm = join(grad_inputs, grad_norm)
    input_steps = [step_both(grad_inputs, grad_inputs)]
    grad_norm = grad_norm[None]
    norm_got = [turn(grad_norm, s) for s in range(1, n_tp)]
    got, norm_got, input_steps[0] = join(got, norm_got, input_steps[0])
    grad_norm = (grad_norm + sum(norm_got))[0]
    grad_output = (pieces[0].astype(F32) + sum(v.astype(F32) for v in got)).astype(BF)
    grad_output = jnp.pad(grad_output, ((0, used - grad_output.shape[0]), (0, 0)))
    grad_output = grad_output.at[used - 1].set(grad_norm.astype(BF))
    if fine:
        got = [swap(grad_output, k) for k in (2, 4, 6)]
    grad_expert = grad_expert.reshape(3, -1, width).astype(F32)
    grad_gate_w, grad_up_w, grad_down_w = grad_expert[0].T, grad_expert[1].T, grad_expert[2]
    for t in range(1, n_tp - 2):
        input_steps.append(step_both(*input_steps[-1], t))
    if fine:
        got, input_steps[-1], grad_gate_w, grad_up_w, grad_down_w = join(
            got, input_steps[-1], grad_gate_w, grad_up_w, grad_down_w
        )
        near = jnp.concatenate([grad_output] + got, axis=0)
        far = swap(near, 1)
        far, grad_qkv_w = join(far, grad_qkv_w)
        devices = jnp.stack([jnp.bitwise_xor(ep_at, jnp.int32(k)) for k in (0, 2, 4, 6, 1, 3, 5, 7)])
        grad_output, small, grad_norm = set_rows(devices, near, far, part, small_rows)
        small = small.reshape(n_ep, small_rows, width)
        grad_norm = grad_norm[0]
    else:
        gathered = lax.all_gather(grad_output, "ep")
        small = gathered[:, part : part + small_rows].astype(F32)
        grad_norm = jnp.sum(gathered[:, used - 1].astype(F32), axis=0)
        grad_output = gathered[:, :part].reshape(heads_width, width).astype(F32)
    small = small[:, :few].reshape(n_ep * few, width)[: 1 + experts]
    result = spread(result_mine, result_steps, result_last)
    input_last = step_ends(*input_steps[-1], n_tp - 2, n_tp - 1)
    grad_qkv_w = grad_qkv_w.astype(F32)
    qkv_grads = (
        grad_qkv_w[:, :heads_width],
        grad_qkv_w[:, heads_width : heads_width + groups_width],
        grad_qkv_w[:, heads_width + groups_width :],
    )
    grad_norm, small, grad_output, input_last, qkv_grads, result = join(
        grad_norm, small, grad_output, input_last, qkv_grads, result
    )
    grad_inputs = spread(grad_inputs, input_steps, input_last)
    return (
        result,
        grad_inputs,
        grad_norm,
        *qkv_grads,
        grad_output,
        small[0],
        small[1:].T,
        grad_gate_w[None],
        grad_up_w[None],
        grad_down_w[None],
    )


def solution(mesh):
    placed = (
        P("ep", None),
        P("ep", None),
        P(),
        P(None, "tp"),
        P(None, "tp"),
        P(None, "tp"),
        P("tp", None),
        P(),
        P(),
        P("ep", None, "tp"),
        P("ep", None, "tp"),
        P("ep", "tp", None),
        P("ep", None),
    )
    return jax.shard_map(
        body,
        mesh=mesh,
        in_specs=placed,
        out_specs=(
            P("ep", None),
            P("ep", None),
            P(),
            P(None, "tp"),
            P(None, "tp"),
            P(None, "tp"),
            P("tp", None),
            P(),
            P(),
            P("ep", None, "tp"),
            P("ep", None, "tp"),
            P("ep", "tp", None),
        ),
        check_vma=False,
    )
```

```python
import functools

import jax
import jax.numpy as jnp
import numpy as np
from jax import lax
from jax.experimental import pallas as pl
from jax.experimental.pallas import tpu as pltpu
from jax.sharding import PartitionSpec as P

HD = 64
LEN = 1024
EPS = 1e-06
MASKED = -1e30
BF = jnp.bfloat16
F32 = jnp.float32
BLOCK = 256
LANES = 128
NT = (((1,), (1,)), ((), ()))
TN = (((0,), (0,)), ((), ()))


def takes(us):
    return pl.CostEstimate(flops=int(us * 1.15e9), bytes_accessed=0, transcendentals=0)


def mul(a, b, dims=(((1,), (0,)), ((), ()))):
    return lax.dot_general(a, b, dims, preferred_element_type=F32)


def rotate_lanes(y, cos, sin):
    half = HD // 2
    first = lax.broadcasted_iota(jnp.int32, y.shape, 1) % HD < half
    return y * cos + jnp.where(first, pltpu.roll(y, 128 - half, 1), pltpu.roll(y, half, 1)) * sin


def rotary_lanes(tokens):
    lane = np.arange(128)
    freqs = np.float32(10000.0) ** (-(lane % (HD // 2)).astype(np.float32) * np.float32(2.0 / HD))
    angles = (np.arange(tokens) % LEN).astype(np.float32)[:, None] * freqs[None, :].astype(np.float32)
    sign = np.where(lane % HD < HD // 2, np.float32(-1.0), np.float32(1.0))
    return jnp.asarray(np.cos(angles), F32), jnp.asarray(np.sin(angles) * sign, F32)


def causal(block):
    key_at = lax.broadcasted_iota(jnp.int32, (block, block), 0)
    query_at = lax.broadcasted_iota(jnp.int32, (block, block), 1)
    return key_at <= query_at


def attend_kernel(at_ref, x_ref, gain_ref, wq_ref, wk_ref, wv_ref, cos_ref, sin_ref, *refs):
    pieces, (q_ref, k_ref, v_ref, log_ref, w_ref, vt_ref, out_ref) = refs[:-7], refs[-7:]
    tokens = x_ref.shape[0]
    heads, groups = q_ref.shape[0], k_ref.shape[0]
    repeat = heads // groups
    per = 128 // HD
    scale = HD ** (-0.5)
    w_ref[...] = jnp.concatenate([wq_ref[...], wk_ref[...], wv_ref[...]], axis=1)

    @pl.loop(0, tokens // BLOCK)
    def _(i):
        at = pl.multiple_of(i * BLOCK, BLOCK)
        rows = pl.ds(at, BLOCK)
        x = x_ref[rows, :].astype(F32)
        inverse = lax.rsqrt(jnp.mean(x * x, axis=-1, keepdims=True) + EPS)
        normed = (x * inverse * gain_ref[...]).astype(BF)
        raw = mul(normed, w_ref[...])
        tables = (cos_ref[rows, :], sin_ref[rows, :])
        for h in range(0, heads, per):
            turned = rotate_lanes(raw[:, h * HD : h * HD + 128], *tables) * scale
            for u in range(per):
                q_ref[h + u, rows, :] = turned[:, u * HD : (u + 1) * HD].astype(BF)
        for g in range(0, groups, per):
            lane = (heads + g) * HD
            turned = rotate_lanes(raw[:, lane : lane + 128], *tables)
            lane = (heads + groups + g) * HD
            value = raw[:, lane : lane + 128]
            turned_value = value.T
            for u in range(per):
                k_ref[g + u, rows, :] = turned[:, u * HD : (u + 1) * HD].astype(BF)
                v_ref[g + u, rows, :] = value[:, u * HD : (u + 1) * HD].astype(BF)
                vt_ref[g + u, :, rows] = turned_value[u * HD : (u + 1) * HD].astype(BF)

    keep = causal(BLOCK)

    @pl.loop(0, heads)
    def _(h):
        g = h // repeat
        for i in range(tokens // BLOCK):
            start, stop = i * BLOCK, (i + 1) * BLOCK
            query = q_ref[h, start:stop, :]
            parts = [jnp.where(keep, mul(k_ref[g, start:stop, :], query, NT), MASKED)]
            if i:
                parts.append(mul(k_ref[g, :start, :], query, NT))
            peak = jnp.max(parts[0], axis=0, keepdims=True)
            for part in parts[1:]:
                peak = jnp.maximum(peak, jnp.max(part, axis=0, keepdims=True))
            weights = [jnp.exp(part - peak) for part in parts]
            total = sum(jnp.sum(w, axis=0, keepdims=True) for w in weights)
            shrink = 1.0 / total
            mixed = mul(vt_ref[g, :, start:stop], (weights[0] * shrink).astype(BF))
            if i:
                mixed += mul(vt_ref[g, :, :start], (weights[1] * shrink).astype(BF))
            out_ref[h, :, start:stop] = mixed
            log_ref[h, :, start:stop] = peak + jnp.log(total)

    for s, piece_ref in enumerate(pieces):
        span = pl.ds(pl.multiple_of(lax.rem(at_ref[0] + s, len(pieces)) * BLOCK, BLOCK), BLOCK)
        for h in range(0, heads, per):
            pair = jnp.concatenate([out_ref[h + u, :, span] for u in range(per)], axis=0)
            piece_ref[:, h * HD : h * HD + 128] = pair.T.astype(BF)


VMEM = pl.BlockSpec(memory_space=pltpu.VMEM)
SMEM = pl.BlockSpec(memory_space=pltpu.SMEM)


def attend(x, gain, weights, tables, heads, groups, at):
    tokens, width = x.shape
    count = tokens // BLOCK
    return pl.pallas_call(
        attend_kernel,
        in_specs=[SMEM] + [VMEM] * 7,
        out_shape=[jax.ShapeDtypeStruct((BLOCK, heads * HD), BF)] * count
        + [
            jax.ShapeDtypeStruct((heads, tokens, HD), BF),
            jax.ShapeDtypeStruct((groups, tokens, HD), BF),
            jax.ShapeDtypeStruct((groups, tokens, HD), BF),
            jax.ShapeDtypeStruct((heads, 1, tokens), F32),
        ],
        scratch_shapes=[
            pltpu.VMEM((width, (heads + 2 * groups) * HD), BF),
            pltpu.VMEM((groups, HD, tokens), BF),
            pltpu.VMEM((heads, HD, tokens), F32),
        ],
        compiler_params=pltpu.CompilerParams(vmem_limit_bytes=48 << 20),
        cost_estimate=takes(20),
    )(at[None], x, gain[None], *weights, *tables)


def attend_back_kernel(at_ref, q_ref, k_ref, v_ref, log_ref, cos_ref, sin_ref, wq_ref, wk_ref, wv_ref, *refs):
    w_ref, do_ref, kt_ref, dq_ref, dk_ref, dv_ref = refs[-6:]
    out_ref, end_ref = refs[-8:-6]
    count = (len(refs) - 8) // 2
    grad_refs, block_refs = refs[:count], refs[count:-8]
    tokens = q_ref.shape[1]
    heads, groups = q_ref.shape[0], k_ref.shape[0]
    repeat = heads // groups
    per = 128 // HD
    scale = HD ** (-0.5)
    w_ref[...] = jnp.concatenate([wq_ref[...], wk_ref[...], wv_ref[...]], axis=1)
    dk_ref[...] = jnp.zeros_like(dk_ref)
    dv_ref[...] = jnp.zeros_like(dv_ref)

    def span_of(s):
        return pl.ds(pl.multiple_of(lax.rem(at_ref[0] + s, count) * BLOCK, BLOCK), BLOCK)

    for s, grad_ref in enumerate(grad_refs):
        for h in range(heads):
            do_ref[h, span_of(s), :] = grad_ref[:, h * HD : (h + 1) * HD]

    @pl.loop(0, tokens // BLOCK)
    def _(i):
        rows = pl.ds(pl.multiple_of(i * BLOCK, BLOCK), BLOCK)
        for g in range(groups):
            kt_ref[g, :, rows] = k_ref[g, rows, :].astype(F32).T.astype(BF)

    keep = causal(BLOCK)

    @pl.loop(0, heads)
    def _(h):
        g = h // repeat
        for i in range(tokens // BLOCK):
            start, stop = i * BLOCK, (i + 1) * BLOCK
            query = q_ref[h, start:stop, :]
            grads = do_ref[h, start:stop, :]
            log_total = log_ref[h, :, start:stop]
            spans = [(start, stop)] + ([(0, start)] if i else [])
            probs, grad_probs = [], []
            for lo, hi in spans:
                scores = mul(k_ref[g, lo:hi, :], query, NT)
                if hi == stop:
                    scores = jnp.where(keep, scores, MASKED)
                probs.append(jnp.exp(scores - log_total))
                grad_probs.append(mul(v_ref[g, lo:hi, :], grads, NT))
            inner = sum(jnp.sum(p * d, axis=0, keepdims=True) for p, d in zip(probs, grad_probs))
            dq = None
            for (lo, hi), p, d in zip(spans, probs, grad_probs):
                ds = (p * (d - inner)).astype(BF)
                dk_ref[g, lo:hi, :] += mul(ds, query)
                dv_ref[g, lo:hi, :] += mul(p.astype(BF), grads)
                term = mul(kt_ref[g, :, lo:hi], ds)
                dq = term if dq is None else dq + term
            dq_ref[h, :, start:stop] = dq * scale

    @pl.loop(0, tokens // BLOCK)
    def _(i):
        rows = pl.ds(pl.multiple_of(i * BLOCK, BLOCK), BLOCK)
        tables = (cos_ref[rows, :], -sin_ref[rows, :])
        for h in range(0, heads, per):
            pair = jnp.concatenate([dq_ref[h + u, :, rows] for u in range(per)], axis=0).T
            out_ref[rows, h * HD : h * HD + 128] = rotate_lanes(pair, *tables).astype(BF)
        for g in range(0, groups, per):
            pair = jnp.concatenate([dk_ref[g + u, rows, :] for u in range(per)], axis=1)
            lane = (heads + g) * HD
            out_ref[rows, lane : lane + 128] = rotate_lanes(pair, *tables).astype(BF)
            pair = jnp.concatenate([dv_ref[g + u, rows, :] for u in range(per)], axis=1)
            lane = (heads + groups + g) * HD
            out_ref[rows, lane : lane + 128] = pair.astype(BF)


    for s, block_ref in enumerate(block_refs):
        block_ref[...] = mul(out_ref[span_of(s), :], w_ref[...], NT).astype(BF)

    @pl.when(at_ref[0] < count // 2)
    def _():
        end_ref[...] = block_refs[count - 1][...]

    @pl.when(at_ref[0] >= count // 2)
    def _():
        end_ref[...] = block_refs[1][...]


def attend_back(grad_pieces, q, k, v, logs, tables, weights, at):
    heads, tokens, _ = q.shape
    groups = k.shape[0]
    count = len(grad_pieces)
    lanes = (heads + 2 * groups) * HD
    width = weights[0].shape[0]
    block = jax.ShapeDtypeStruct((BLOCK, width), BF)
    return pl.pallas_call(
        attend_back_kernel,
        in_specs=[SMEM] + [VMEM] * (9 + count),
        out_shape=[block] * count + [jax.ShapeDtypeStruct((tokens, lanes), BF), block],
        scratch_shapes=[
            pltpu.VMEM((width, lanes), BF),
            pltpu.VMEM((heads, tokens, HD), BF),
            pltpu.VMEM((groups, HD, tokens), BF),
            pltpu.VMEM((heads, HD, tokens), F32),
            pltpu.VMEM((groups, tokens, HD), F32),
            pltpu.VMEM((groups, tokens, HD), F32),
        ],
        compiler_params=pltpu.CompilerParams(vmem_limit_bytes=48 << 20),
        cost_estimate=takes(20),
    )(at[None], q, k, v, logs, *tables, *weights, *grad_pieces)


def pack_kernel(gate_ref, up_ref, down_ref, out_ref):
    part = down_ref.shape[0]
    out_ref[:part, :] = gate_ref[...].astype(F32).T.astype(BF)
    out_ref[part : 2 * part, :] = up_ref[...].astype(F32).T.astype(BF)
    out_ref[2 * part :, :] = down_ref[...]


def pack(gate, up, down):
    return pl.pallas_call(
        pack_kernel,
        out_shape=jax.ShapeDtypeStruct((3 * down.shape[0], down.shape[1]), BF),
        compiler_params=pltpu.CompilerParams(vmem_limit_bytes=32 << 20),
        cost_estimate=takes(3),
    )(gate, up, down)


def expert_kernel(order_ref, near_ref, far_ref, extra_near_ref, extra_far_ref, router_ref, parts_ref, *refs, top, count):
    out_refs, gin_refs, terms_ref = refs[:2], refs[2:5], refs[5]
    weights_ref, sums_ref = refs[6:]
    step = pl.program_id(0)
    steps = pl.num_programs(0)
    hidden_width, width = weights_ref.shape[0] // 3, weights_ref.shape[1]
    gate_up = slice(0, 2 * hidden_width)
    down = slice(2 * hidden_width, 3 * hidden_width)
    own = order_ref[0]
    experts = order_ref[1]
    part = hidden_width // count
    spans = [
        (pl.ds((3 * s + j) * part, part), pl.ds(j * hidden_width + s * part, part))
        for s in range(count)
        for j in range(3)
    ]

    @pl.when(step == 0)
    def _():
        sums_ref[...] = jnp.zeros_like(sums_ref)
        for there, here in spans:
            weights_ref[here, :] = parts_ref[there, :]

    near = step < steps // 2
    rows = jnp.where(near, near_ref[...], far_ref[...])
    extra = jnp.where(near, extra_near_ref[...], extra_far_ref[...])
    grads32 = extra[:, :width].astype(F32)
    named = extra[:, width:].astype(F32)

    lane = lax.broadcasted_iota(jnp.int32, (rows.shape[0], LANES), 1)
    lane32 = lane.astype(F32)
    chosen = lane32 == named[:, 0:1]
    for k in range(1, top):
        chosen = chosen | (lane32 == named[:, k : k + 1])
    logits = jnp.where(chosen, mul(rows, router_ref[...]), MASKED)
    weights = jnp.where(chosen, jnp.exp(logits - jnp.max(logits, axis=-1, keepdims=True)), 0.0)
    mine = jnp.sum(jnp.where(lane == own, weights, 0.0), axis=-1, keepdims=True)
    gate = mine / jnp.sum(weights, axis=-1, keepdims=True)

    both = mul(rows, weights_ref[gate_up, :], NT)
    gate_vals = both[:, :hidden_width]
    up_vals = both[:, hidden_width:]
    sigma = jax.nn.sigmoid(gate_vals)
    active = gate_vals * sigma
    hidden = (active * up_vals).astype(BF)
    grad_out = (gate * grads32).astype(BF)
    grad_hidden = mul(grad_out, weights_ref[down, :], NT)
    expert_out = mul(hidden, weights_ref[down, :])
    combined = (gate * expert_out).astype(BF)
    score = jnp.sum(grads32 * expert_out, axis=-1, keepdims=True)
    high = score.astype(BF).astype(F32)
    scores = jnp.where(lane == own, high, jnp.where(lane == own + experts, score - high, 0.0)).astype(BF)
    grad_gate_vals = (grad_hidden * up_vals * sigma * (1.0 + gate_vals * (1.0 - sigma))).astype(BF)
    grad_up_vals = (grad_hidden * active).astype(BF)
    grad_both = jnp.concatenate([grad_gate_vals, grad_up_vals], axis=1)
    grad_in = mul(grad_both, weights_ref[gate_up, :]).astype(BF)
    sums_ref[gate_up, :] += mul(grad_both, rows, TN)
    sums_ref[down, :] += mul(hidden, grad_out, TN)
    far_step = step - steps // 2
    for k, now in enumerate((near, jnp.logical_not(near))):

        @pl.when(now)
        def _():
            out_refs[k][...] = combined

    even = lax.rem(step, 2) == 0
    for k, now in enumerate((near, (far_step >= 0) & even, (far_step >= 0) & jnp.logical_not(even))):

        @pl.when(now)
        def _():
            gin_refs[k][:, :width] = grad_in
            gin_refs[k][:, width:] = scores

    @pl.when(step == steps - 1)
    def _():
        for there, here in spans:
            terms_ref[there, :] = sums_ref[here, :].astype(BF)


def run_experts(order, near, far, extra_near, extra_far, router, parts, top, count):
    total, width = 2 * near.shape[0], near.shape[1]
    steps = total // BLOCK
    half_steps = steps // 2
    wide = extra_near.shape[1]
    hidden = parts.shape[0] // 3

    def by_set(lanes):
        return [
            pl.BlockSpec((BLOCK, lanes), lambda i, o: (jnp.minimum(i, half_steps - 1), 0)),
            pl.BlockSpec((BLOCK, lanes), lambda i, o: (jnp.maximum(i - half_steps, 0), 0)),
        ]

    half = by_set(width)
    far_pair = pl.BlockSpec((BLOCK, wide), lambda i, o: (jnp.maximum(i - half_steps, 0) // 2, 0))
    half_wide = [by_set(wide)[0], far_pair, far_pair]
    whole = pl.BlockSpec((3 * hidden, width), lambda i, o: (0, 0), pipeline_mode=pl.Buffered(1))
    return pl.pallas_call(
        functools.partial(expert_kernel, top=top, count=count),
        grid_spec=pltpu.PrefetchScalarGridSpec(
            num_scalar_prefetch=1,
            grid=(steps,),
            in_specs=[
                *by_set(width),
                *by_set(wide),
                pl.BlockSpec((width, LANES), lambda i, o: (0, 0)),
                whole,
            ],
            out_specs=half + half_wide + [whole],
            scratch_shapes=[
                pltpu.VMEM((3 * hidden, width), BF),
                pltpu.VMEM((3 * hidden, width), F32),
            ],
        ),
        out_shape=[jax.ShapeDtypeStruct((total // 2, width), BF)] * 2
        + [jax.ShapeDtypeStruct((total // 2, wide), BF)]
        + [jax.ShapeDtypeStruct((total // 4, wide), BF)] * 2
        + [jax.ShapeDtypeStruct((3 * hidden, width), BF)],
        compiler_params=pltpu.CompilerParams(vmem_limit_bytes=58 << 20),
        cost_estimate=takes(5 * steps),
    )(order, near, far, extra_near, extra_far, router, parts)


def set_rows_kernel(order_ref, near_ref, far_ref, out_ref, small_ref, norm_ref, *, part, few_rows):
    rows, width = near_ref.shape[0] // 4, near_ref.shape[1]
    norm = jnp.zeros((1, width), F32)
    for k in range(8):
        source = near_ref if k < 4 else far_ref
        block = source[(k % 4) * rows : (k % 4 + 1) * rows, :].astype(F32)
        device = order_ref[k]
        out_ref[pl.ds(pl.multiple_of(device * part, 8), part), :] = block[:part]
        small_ref[pl.ds(pl.multiple_of(device * few_rows, 8), few_rows), :] = block[part : part + few_rows]
        norm += block[rows - 1 :]
    norm_ref[...] = norm


def set_rows(order, near, far, part, few_rows):
    width = near.shape[1]
    return pl.pallas_call(
        functools.partial(set_rows_kernel, part=part, few_rows=few_rows),
        in_specs=[SMEM, VMEM, VMEM],
        out_shape=[
            jax.ShapeDtypeStruct((8 * part, width), F32),
            jax.ShapeDtypeStruct((8 * few_rows, width), F32),
            jax.ShapeDtypeStruct((1, width), F32),
        ],
        compiler_params=pltpu.CompilerParams(vmem_limit_bytes=32 << 20),
        cost_estimate=takes(3),
    )(order, near, far)


def join(*values):
    return lax.optimization_barrier(values)


def add(a, b):
    return (a.astype(F32) + b.astype(F32)).astype(BF)


def swap(x, bit):
    return lax.ppermute(x, "ep", [(i, i ^ bit) for i in range(lax.axis_size("ep"))])


def turn(x, by):
    n = lax.axis_size("tp")
    return lax.ppermute(x, "tp", [(i, (i + by) % n) for i in range(n)])


def step_both(right, left, low=0, high=None):
    n = lax.axis_size("tp")
    pairs = [(i, i + 1) for i in range(low, n - 1 if high is None else high)]
    mirror = [(n - 1 - i, n - 1 - j) for i, j in pairs]
    return lax.ppermute(right, "tp", pairs), lax.ppermute(left, "tp", mirror)


def step_ends(right, left, low, high):
    n = lax.axis_size("tp")
    at = lax.axis_index("tp")
    pairs = [(i, i + 1) for i in range(low, high)]
    give = right if right is left else jnp.where((at >= low) & (at < high), right, left)
    return lax.ppermute(give, "tp", pairs + [(n - 1 - i, n - 1 - j) for i, j in pairs])


def by_side(got, low, high):
    at = lax.axis_index("tp")
    ahead = (at > low) & (at <= high)
    return jnp.where(ahead, got, 0), jnp.where(ahead, 0, got)


def gather_first(x):
    half = x.shape[0] // 2
    return swap(x[:half], 2), swap(x[half:], 4)


def gather_second(x, got):
    half = x.shape[0] // 2
    first, second = join(
        jnp.concatenate([x[:half], got[0]], axis=0), jnp.concatenate([x[half:], got[1]], axis=0)
    )
    return (first, second), (swap(first, 4), swap(second, 2))


def gather_near(held, got):
    return jnp.concatenate([held[0], got[0], held[1], got[1]], axis=0)


def gather_halves():
    n = lax.axis_size("ep")
    if n != 8:
        return [(jnp.int32(k // 2), k % 2) for k in range(2 * n)]
    at = lax.axis_index("ep").astype(jnp.int32)
    near = [(0, 0), (2, 0), (4, 0), (6, 0), (0, 1), (4, 1), (2, 1), (6, 1)]
    return [(jnp.bitwise_xor(at, k + core), half) for core in (0, 1) for k, half in near]


def gather_whole(x):
    whole = lax.all_gather(x, "ep", tiled=True)
    return whole[: whole.shape[0] // 2], whole[whole.shape[0] // 2 :]


def sum_cores(near, far):
    rows = near.shape[0] // 4
    return join(*[add(near[j * rows : (j + 1) * rows], far[j * rows : (j + 1) * rows]) for j in range(4)])


def sum_first(sums):
    return swap(sums[1], 4), swap(sums[3], 2)


def sum_second(sums, got):
    first, second = join(add(sums[0], got[0]), add(sums[2], got[1]))
    half = first.shape[0] // 2
    return (first, second), (swap(first[half:], 2), swap(second[half:], 4))


def sum_last(sums, got):
    half = sums[0].shape[0] // 2
    return jnp.concatenate([s[:half].astype(F32) + g.astype(F32) for s, g in zip(sums, got)], axis=0)


def sum_whole(near, far):
    n = lax.axis_size("ep")
    terms = jnp.concatenate([near, far], axis=0).reshape(n, -1, near.shape[1])
    return lax.psum_scatter(terms, "ep", scatter_dimension=0, tiled=False).astype(F32)


def spread(own, steps, last):
    n = lax.axis_size("tp")
    at = lax.axis_index("tp").astype(jnp.int32)
    rows, width = own.shape
    out = jnp.zeros((n * rows, width), BF)
    for t, step in enumerate(steps):
        for got, place in zip(step, (at - t - 1, at + t + 1)):
            place = jnp.where((place >= 0) & (place < n), place, at)
            out = lax.dynamic_update_slice(out, got, (place * rows, 0))
    place = jnp.where(at == n - 1, 0, jnp.where(at == 0, n - 1, at))
    out = lax.dynamic_update_slice(out, last, (place * rows, 0))
    return lax.dynamic_update_slice(out, own, (at * rows, 0))


def body(
    inputs,
    routes,
    norm_gain,
    query_weight,
    key_weight,
    value_weight,
    output_weight,
    mixer_gain,
    router_weight,
    gate_weight,
    up_weight,
    down_weight,
    cotangent,
):
    tokens, width = inputs.shape
    experts = router_weight.shape[1]
    top = routes.shape[1]
    n_ep = lax.axis_size("ep")
    n_tp = lax.axis_size("tp")
    fine = n_ep == 8
    ep_at = lax.axis_index("ep").astype(jnp.int32)
    tp_at = lax.axis_index("tp").astype(jnp.int32)
    quarter = tokens // n_tp
    heads_width = query_weight.shape[1]
    groups_width = key_weight.shape[1]

    def mine(x):
        return lax.dynamic_slice_in_dim(x, tp_at * quarter, quarter, 0)

    part = output_weight.shape[0] // n_ep
    output_part = lax.dynamic_slice_in_dim(output_weight, ep_at * part, part, 0)
    output_parts = [output_part] + [turn(output_part, -s) for s in range(1, n_tp)]

    hidden_part = gate_weight.shape[2]
    expert_part = pack(gate_weight[0], up_weight[0], down_weight[0])
    expert_parts = lax.all_gather(expert_part, "tp", tiled=True)

    routes_mine = mine(routes)
    grad_top_mine = mine(cotangent)
    named = jnp.pad(routes_mine.astype(BF), ((0, 0), (0, LANES - top)), constant_values=-1.0)
    extra = jnp.concatenate([grad_top_mine, named], axis=1)
    tables = rotary_lanes(tokens)
    qkv_weights = (query_weight, key_weight, value_weight)
    if fine:
        extra_got = gather_first(extra)
        output_parts, qkv_weights, expert_part = join(output_parts, qkv_weights, expert_part)
        output_part = jnp.concatenate(output_parts, axis=0)
        output_got = gather_first(output_part)
    else:
        output_part = jnp.concatenate(output_parts, axis=0)
        extra_near, extra_far = gather_whole(extra)

    *mixed, query, key, value, logs = attend(
        inputs,
        norm_gain,
        qkv_weights,
        tables,
        heads_width // HD,
        groups_width // HD,
        tp_at,
    )
    if fine:
        mixed, output_got, extra_got = join(mixed, output_got, extra_got)

    mixed = [mixed[0]] + [turn(mixed[s], s) for s in range(1, n_tp)]
    if fine:
        output_held, output_got = gather_second(output_part, output_got)
        mixed, output_held, output_got = join(mixed, output_held, output_got)
        near = gather_near(output_held, output_got)
        far = swap(near, 1)
        extra_held, extra_got = gather_second(extra, extra_got)
    else:
        near, far = gather_whole(output_part)
    halves = gather_halves()
    output_whole = jnp.zeros((n_tp, n_ep, part, width), BF)
    for j, blocks in enumerate((near, far)):
        blocks = blocks.reshape(n_ep, n_tp // 2, part, width)
        for k in range(n_ep):
            device, half = halves[j * n_ep + k]
            for u in range(n_tp // 2):
                place = (n_tp - half * (n_tp // 2) - u) % n_tp
                output_whole = lax.dynamic_update_slice(
                    output_whole, blocks[k, u][None, None], (place, device, 0, 0)
                )
    output_whole = output_whole.reshape(n_tp * heads_width, width)

    mixed_mine = jnp.concatenate(mixed, axis=1)
    branch = mul(mixed_mine, output_whole)
    inputs_mine = mine(inputs).astype(F32)
    attended = inputs_mine + branch
    inverse_two = lax.rsqrt(jnp.mean(attended * attended, axis=-1, keepdims=True) + EPS)
    unit_two = attended * inverse_two
    routed_in = (unit_two * mixer_gain).astype(BF)
    logits = mul(routed_in, router_weight)
    ids = jnp.arange(experts, dtype=jnp.int32)
    chosen = jnp.any(routes_mine[:, :, None] == ids[None, None, :], axis=1)
    logits = jnp.where(chosen, logits, MASKED)
    weights = jnp.where(chosen, jnp.exp(logits - jnp.max(logits, axis=-1, keepdims=True)), 0.0)
    gates = weights / jnp.sum(weights, axis=-1, keepdims=True)

    router = jnp.pad(router_weight, ((0, 0), (0, LANES - experts)))
    order = jnp.concatenate([ep_at[None], jnp.full((1,), experts, jnp.int32)])
    if fine:
        got = gather_first(routed_in)
        got, gates, router, order, extra_held, extra_got = join(
            got, gates, router, order, extra_held, extra_got
        )
        extra_near = gather_near(extra_held, extra_got)
        extra_far = swap(extra_near, 1)
        held, got = gather_second(routed_in, got)
        held, got = join(held, got)
        near = gather_near(held, got)
        far = swap(near, 1)
    else:
        near, far = gather_whole(routed_in)
    out_near, out_far, gin_near, gin_even, gin_odd, terms = run_experts(
        order, near, far, extra_near, extra_far, router, expert_parts, top, n_tp
    )

    grad_expert = lax.psum_scatter(terms, "tp", scatter_dimension=0, tiled=True)

    if fine:
        gin_near = [gin_near[j * quarter : (j + 1) * quarter] for j in range(4)]
        other = swap(gin_odd, 1)
        gin = join(add(gin_near[1], other[:quarter]), add(gin_near[3], other[quarter:]))
        got = (swap(gin[0], 4), swap(gin[1], 2))
        out_far, gin_even, gin = join(out_far, gin_even, gin)
        gin_even = swap(gin_even, 1)
        out_far = swap(out_far, 1)
        got, out_far, gin_even = join(got, out_far, gin_even)
        gin = join(
            add(gin_near[0].astype(F32) + gin_even[:quarter].astype(F32), got[0]),
            add(gin_near[2].astype(F32) + gin_even[quarter:].astype(F32), got[1]),
        )
        got = [swap(g[quarter // 2 :], bit) for g, bit in zip(gin, (2, 4))]
        out = sum_cores(out_near, out_far)
        out_got = sum_first(out)
        gin, got = join(gin, got)
        grad_in = sum_last(gin, got)
    else:
        gin_far = jnp.stack([v.reshape(-1, quarter, v.shape[1]) for v in (gin_even, gin_odd)], axis=1)
        grad_in = sum_whole(gin_near, gin_far.reshape(gin_near.shape))
    grad_gates = grad_in[:, width : width + experts] + grad_in[:, width + experts : width + 2 * experts]
    inner_gate = jnp.sum(gates * grad_gates, axis=-1, keepdims=True)
    grad_logits = (gates * (grad_gates - inner_gate)).astype(BF)
    grad_routed = grad_in[:, :width] + mul(grad_logits, router_weight, NT)
    grad_top = grad_top_mine.astype(F32)
    scaled_two = grad_routed * mixer_gain
    grad_attended = grad_top + inverse_two * (
        scaled_two - unit_two * jnp.mean(scaled_two * unit_two, axis=-1, keepdims=True)
    )
    grad_branch = grad_attended.astype(BF)
    grad_mixed = mul(grad_branch, output_whole, NT).astype(BF)
    grad_mixed = [grad_mixed[:, s * heads_width : (s + 1) * heads_width] for s in range(n_tp)]

    grad_mixed, grad_branch = join(grad_mixed, grad_branch)
    grad_mixed = [grad_mixed[0]] + [turn(grad_mixed[s], -s) for s in range(1, n_tp)]
    if fine:
        out, out_got = sum_second(out, out_got)

    few = -(-(1 + experts) // n_ep)
    pad = 16 * (few // 16 + 1)
    small_rows = -(-few // 8) * 8
    grad_router = mul(routed_in, grad_logits, TN)
    grad_mixer = jnp.sum(grad_routed * unit_two, axis=0)
    small = jnp.concatenate([grad_mixer[None], grad_router.T], axis=0).astype(BF)
    small = jnp.pad(small, ((0, few * n_ep - 1 - experts), (0, 0))).reshape(n_ep, few, width)
    small = jnp.pad(small, ((0, 0), (0, pad - few), (0, 0)))
    grad_output = mul(mixed_mine, grad_branch, TN).astype(BF)
    grad_output = grad_output.reshape(n_tp, n_ep, part, width).transpose(1, 0, 2, 3)
    grad_output = jnp.concatenate([grad_output.reshape(n_ep, n_tp * part, width), small], axis=1)
    if fine:
        core, chip = lax.rem(ep_at, 2), lax.div(ep_at, 2)
        grad_output = grad_output.reshape((n_ep // 2, 2) + grad_output.shape[1:])
        other_output = lax.dynamic_index_in_dim(grad_output, 1 - core, 1, False)
        grad_output = lax.dynamic_index_in_dim(grad_output, core, 1, False)
        grad_mixed, out, out_got, other_output, grad_output = join(
            grad_mixed, out, out_got, other_output, grad_output
        )
        out = sum_last(out, out_got)
        other_output = swap(other_output, 1)
    else:
        out = sum_whole(out_near, out_far)
    result_mine = (attended + out).astype(BF)

    result_mine, grad_mixed = join(result_mine, grad_mixed)
    result_steps = [step_both(result_mine, result_mine)]
    *blocks, grad_qkv, end_block = attend_back(grad_mixed, query, key, value, logs, tables, qkv_weights, tp_at)
    if fine:
        blocks, grad_qkv, end_block, result_steps[0], other_output, grad_expert, inputs = join(
            blocks, grad_qkv, end_block, result_steps[0], other_output, grad_expert, inputs
        )
    else:
        blocks, grad_qkv, end_block, result_steps[0] = join(blocks, grad_qkv, end_block, result_steps[0])

    inputs32 = inputs.astype(F32)
    normed = inputs32 * lax.rsqrt(jnp.mean(inputs32 * inputs32, axis=-1, keepdims=True) + EPS)
    normed = (normed * norm_gain).astype(BF)
    grad_qkv_w = mul(normed, grad_qkv, TN).astype(BF)

    def chip_halves(half, *places):
        rows = grad_output.shape[1] // 2
        picked = []
        for j in places:
            chip_at = (jnp.bitwise_xor(chip, j), half * rows, 0)
            size = (1, rows, width)
            picked.append(
                add(
                    lax.dynamic_slice(grad_output, chip_at, size)[0],
                    lax.dynamic_slice(other_output, chip_at, size)[0],
                )
            )
        return jnp.concatenate(picked, axis=0)

    if fine:
        got = join(chip_halves(0, 2, 3), chip_halves(1, 1, 3))
        got = (swap(got[0], 4), swap(got[1], 2))
    result_steps.append(step_both(*result_steps[-1], 1))
    sent = step_ends(end_block, end_block, 0, 1)
    if fine:
        sent, result_steps[-1], got, grad_qkv_w = join(sent, result_steps[-1], got, grad_qkv_w)
        sums, got = sum_second((chip_halves(0, 0, 1), None, chip_halves(1, 0, 2)), got)
    else:
        sent, result_steps[-1], grad_qkv_w, grad_expert = join(
            sent, result_steps[-1], grad_qkv_w, grad_expert
        )
    grad_qkv_w = lax.psum(grad_qkv_w, "ep")
    sent = by_side(sent, 0, 1)
    result_last = None
    for t in range(2, n_tp):
        sent = step_both(add(blocks[n_tp - t], sent[0]), add(blocks[t], sent[1]), 0, t)
        if t < n_tp - 1:
            result_last = step_ends(*result_steps[-1], t, n_tp - 1)
            if fine:
                sent, result_last, got, sums = join(sent, result_last, got, sums)
                grad_output = sum_last(sums, got).astype(BF)
            else:
                sent, result_last = join(sent, result_last)
                grad_output = lax.psum_scatter(grad_output, "ep", scatter_dimension=0, tiled=False)
            pieces = [
                jnp.concatenate([grad_output[s * part : (s + 1) * part], grad_output[n_tp * part :][:small_rows]], axis=0)
                for s in range(n_tp)
            ]
    got = [turn(pieces[s], -s) for s in range(1, n_tp)]
    sent, result_steps, result_last = join(sent, result_steps, result_last)
    grad_normed = blocks[0].astype(F32) + sent[0].astype(F32) + sent[1].astype(F32)
    inputs_mine = mine(inputs).astype(F32)
    inverse_one = lax.rsqrt(jnp.mean(inputs_mine * inputs_mine, axis=-1, keepdims=True) + EPS)
    unit_one = inputs_mine * inverse_one
    scaled_one = grad_normed * norm_gain
    grad_inputs = grad_attended + inverse_one * (
        scaled_one - unit_one * jnp.mean(scaled_one * unit_one, axis=-1, keepdims=True)
    )
    grad_inputs = grad_inputs.astype(BF)
    grad_norm = jnp.sum(grad_normed * unit_one, axis=0)
    used = -(-(part + small_rows + 1) // 32) * 32

    grad_inputs, grad_norm = join(grad_inputs, grad_norm)
    input_steps = [step_both(grad_inputs, grad_inputs)]
    grad_norm = grad_norm[None]
    norm_got = [turn(grad_norm, s) for s in range(1, n_tp)]
    got, norm_got, input_steps[0] = join(got, norm_got, input_steps[0])
    grad_norm = (grad_norm + sum(norm_got))[0]
    grad_output = (pieces[0].astype(F32) + sum(v.astype(F32) for v in got)).astype(BF)
    grad_output = jnp.pad(grad_output, ((0, used - grad_output.shape[0]), (0, 0)))
    grad_output = grad_output.at[used - 1].set(grad_norm.astype(BF))
    if fine:
        got = [swap(grad_output, k) for k in (2, 4, 6)]
    grad_expert = grad_expert.reshape(3, -1, width).astype(F32)
    grad_gate_w, grad_up_w, grad_down_w = grad_expert[0].T, grad_expert[1].T, grad_expert[2]
    for t in range(1, n_tp - 2):
        input_steps.append(step_both(*input_steps[-1], t))
    if fine:
        got, input_steps[-1], grad_gate_w, grad_up_w, grad_down_w = join(
            got, input_steps[-1], grad_gate_w, grad_up_w, grad_down_w
        )
        near = jnp.concatenate([grad_output] + got, axis=0)
        far = swap(near, 1)
        far, grad_qkv_w = join(far, grad_qkv_w)
        devices = jnp.stack([jnp.bitwise_xor(ep_at, jnp.int32(k)) for k in (0, 2, 4, 6, 1, 3, 5, 7)])
        grad_output, small, grad_norm = set_rows(devices, near, far, part, small_rows)
        small = small.reshape(n_ep, small_rows, width)
        grad_norm = grad_norm[0]
    else:
        gathered = lax.all_gather(grad_output, "ep")
        small = gathered[:, part : part + small_rows].astype(F32)
        grad_norm = jnp.sum(gathered[:, used - 1].astype(F32), axis=0)
        grad_output = gathered[:, :part].reshape(heads_width, width).astype(F32)
    small = small[:, :few].reshape(n_ep * few, width)[: 1 + experts]
    result = spread(result_mine, result_steps, result_last)
    input_last = step_ends(*input_steps[-1], n_tp - 2, n_tp - 1)
    grad_qkv_w = grad_qkv_w.astype(F32)
    qkv_grads = (
        grad_qkv_w[:, :heads_width],
        grad_qkv_w[:, heads_width : heads_width + groups_width],
        grad_qkv_w[:, heads_width + groups_width :],
    )
    grad_norm, small, grad_output, input_last, qkv_grads, result = join(
        grad_norm, small, grad_output, input_last, qkv_grads, result
    )
    grad_inputs = spread(grad_inputs, input_steps, input_last)
    return (
        result,
        grad_inputs,
        grad_norm,
        *qkv_grads,
        grad_output,
        small[0],
        small[1:].T,
        grad_gate_w[None],
        grad_up_w[None],
        grad_down_w[None],
    )


def solution(mesh):
    placed = (
        P("ep", None),
        P("ep", None),
        P(),
        P(None, "tp"),
        P(None, "tp"),
        P(None, "tp"),
        P("tp", None),
        P(),
        P(),
        P("ep", None, "tp"),
        P("ep", None, "tp"),
        P("ep", "tp", None),
        P("ep", None),
    )
    return jax.shard_map(
        body,
        mesh=mesh,
        in_specs=placed,
        out_specs=(
            P("ep", None),
            P("ep", None),
            P(),
            P(None, "tp"),
            P(None, "tp"),
            P(None, "tp"),
            P("tp", None),
            P(),
            P(),
            P("ep", None, "tp"),
            P("ep", None, "tp"),
            P("ep", "tp", None),
        ),
        check_vma=False,
    )
```

```python
import functools

import jax
import jax.numpy as jnp
import numpy as np
from jax import lax
from jax.experimental import pallas as pl
from jax.experimental.pallas import tpu as pltpu
from jax.sharding import PartitionSpec as P

HD = 64
LEN = 1024
EPS = 1e-06
MASKED = -1e30
BF = jnp.bfloat16
F32 = jnp.float32
BLOCK = 256
LANES = 128
NT = (((1,), (1,)), ((), ()))
TN = (((0,), (0,)), ((), ()))


def takes(us):
    return pl.CostEstimate(flops=int(us * 1.15e9), bytes_accessed=0, transcendentals=0)


def mul(a, b, dims=(((1,), (0,)), ((), ()))):
    return lax.dot_general(a, b, dims, preferred_element_type=F32)


def rotate_lanes(y, cos, sin):
    half = HD // 2
    first = lax.broadcasted_iota(jnp.int32, y.shape, 1) % HD < half
    return y * cos + jnp.where(first, pltpu.roll(y, 128 - half, 1), pltpu.roll(y, half, 1)) * sin


def rotary_lanes(tokens):
    lane = np.arange(128)
    freqs = np.float32(10000.0) ** (-(lane % (HD // 2)).astype(np.float32) * np.float32(2.0 / HD))
    angles = (np.arange(tokens) % LEN).astype(np.float32)[:, None] * freqs[None, :].astype(np.float32)
    sign = np.where(lane % HD < HD // 2, np.float32(-1.0), np.float32(1.0))
    return jnp.asarray(np.cos(angles), F32), jnp.asarray(np.sin(angles) * sign, F32)


def causal(block):
    key_at = lax.broadcasted_iota(jnp.int32, (block, block), 0)
    query_at = lax.broadcasted_iota(jnp.int32, (block, block), 1)
    return key_at <= query_at


def attend_kernel(at_ref, x_ref, gain_ref, wq_ref, wk_ref, wv_ref, cos_ref, sin_ref, *refs):
    pieces, (q_ref, k_ref, v_ref, log_ref, w_ref, vt_ref, out_ref) = refs[:-7], refs[-7:]
    tokens = x_ref.shape[0]
    heads, groups = q_ref.shape[0], k_ref.shape[0]
    repeat = heads // groups
    per = 128 // HD
    scale = HD ** (-0.5)
    w_ref[...] = jnp.concatenate([wq_ref[...], wk_ref[...], wv_ref[...]], axis=1)

    @pl.loop(0, tokens // BLOCK)
    def _(i):
        at = pl.multiple_of(i * BLOCK, BLOCK)
        rows = pl.ds(at, BLOCK)
        x = x_ref[rows, :].astype(F32)
        inverse = lax.rsqrt(jnp.mean(x * x, axis=-1, keepdims=True) + EPS)
        normed = (x * inverse * gain_ref[...]).astype(BF)
        raw = mul(normed, w_ref[...])
        tables = (cos_ref[rows, :], sin_ref[rows, :])
        for h in range(0, heads, per):
            turned = rotate_lanes(raw[:, h * HD : h * HD + 128], *tables) * scale
            for u in range(per):
                q_ref[h + u, rows, :] = turned[:, u * HD : (u + 1) * HD].astype(BF)
        for g in range(0, groups, per):
            lane = (heads + g) * HD
            turned = rotate_lanes(raw[:, lane : lane + 128], *tables)
            lane = (heads + groups + g) * HD
            value = raw[:, lane : lane + 128]
            turned_value = value.T
            for u in range(per):
                k_ref[g + u, rows, :] = turned[:, u * HD : (u + 1) * HD].astype(BF)
                v_ref[g + u, rows, :] = value[:, u * HD : (u + 1) * HD].astype(BF)
                vt_ref[g + u, :, rows] = turned_value[u * HD : (u + 1) * HD].astype(BF)

    keep = causal(BLOCK)

    @pl.loop(0, heads)
    def _(h):
        g = h // repeat
        for i in range(tokens // BLOCK):
            start, stop = i * BLOCK, (i + 1) * BLOCK
            query = q_ref[h, start:stop, :]
            parts = [jnp.where(keep, mul(k_ref[g, start:stop, :], query, NT), MASKED)]
            if i:
                parts.append(mul(k_ref[g, :start, :], query, NT))
            peak = jnp.max(parts[0], axis=0, keepdims=True)
            for part in parts[1:]:
                peak = jnp.maximum(peak, jnp.max(part, axis=0, keepdims=True))
            weights = [jnp.exp(part - peak) for part in parts]
            total = sum(jnp.sum(w, axis=0, keepdims=True) for w in weights)
            shrink = 1.0 / total
            mixed = mul(vt_ref[g, :, start:stop], weights[0].astype(BF))
            if i:
                mixed += mul(vt_ref[g, :, :start], weights[1].astype(BF))
            out_ref[h, :, start:stop] = mixed * shrink
            log_ref[h, :, start:stop] = peak + jnp.log(total)

    for s, piece_ref in enumerate(pieces):
        span = pl.ds(pl.multiple_of(lax.rem(at_ref[0] + s, len(pieces)) * BLOCK, BLOCK), BLOCK)
        for h in range(0, heads, per):
            pair = jnp.concatenate([out_ref[h + u, :, span] for u in range(per)], axis=0)
            piece_ref[:, h * HD : h * HD + 128] = pair.T.astype(BF)


VMEM = pl.BlockSpec(memory_space=pltpu.VMEM)
SMEM = pl.BlockSpec(memory_space=pltpu.SMEM)


def attend(x, gain, weights, tables, heads, groups, at):
    tokens, width = x.shape
    count = tokens // BLOCK
    return pl.pallas_call(
        attend_kernel,
        in_specs=[SMEM] + [VMEM] * 7,
        out_shape=[jax.ShapeDtypeStruct((BLOCK, heads * HD), BF)] * count
        + [
            jax.ShapeDtypeStruct((heads, tokens, HD), BF),
            jax.ShapeDtypeStruct((groups, tokens, HD), BF),
            jax.ShapeDtypeStruct((groups, tokens, HD), BF),
            jax.ShapeDtypeStruct((heads, 1, tokens), F32),
        ],
        scratch_shapes=[
            pltpu.VMEM((width, (heads + 2 * groups) * HD), BF),
            pltpu.VMEM((groups, HD, tokens), BF),
            pltpu.VMEM((heads, HD, tokens), F32),
        ],
        compiler_params=pltpu.CompilerParams(vmem_limit_bytes=48 << 20),
        cost_estimate=takes(20),
    )(at[None], x, gain[None], *weights, *tables)


def attend_back_kernel(at_ref, q_ref, k_ref, v_ref, log_ref, cos_ref, sin_ref, wq_ref, wk_ref, wv_ref, *refs):
    w_ref, do_ref, kt_ref, dq_ref, dk_ref, dv_ref = refs[-6:]
    out_ref, end_ref = refs[-8:-6]
    count = (len(refs) - 8) // 2
    grad_refs, block_refs = refs[:count], refs[count:-8]
    tokens = q_ref.shape[1]
    heads, groups = q_ref.shape[0], k_ref.shape[0]
    repeat = heads // groups
    per = 128 // HD
    scale = HD ** (-0.5)
    w_ref[...] = jnp.concatenate([wq_ref[...], wk_ref[...], wv_ref[...]], axis=1)
    dk_ref[...] = jnp.zeros_like(dk_ref)
    dv_ref[...] = jnp.zeros_like(dv_ref)

    def span_of(s):
        return pl.ds(pl.multiple_of(lax.rem(at_ref[0] + s, count) * BLOCK, BLOCK), BLOCK)

    for s, grad_ref in enumerate(grad_refs):
        for h in range(heads):
            do_ref[h, span_of(s), :] = grad_ref[:, h * HD : (h + 1) * HD]

    @pl.loop(0, tokens // BLOCK)
    def _(i):
        rows = pl.ds(pl.multiple_of(i * BLOCK, BLOCK), BLOCK)
        for g in range(groups):
            kt_ref[g, :, rows] = k_ref[g, rows, :].astype(F32).T.astype(BF)

    keep = causal(BLOCK)

    @pl.loop(0, heads)
    def _(h):
        g = h // repeat
        for i in range(tokens // BLOCK):
            start, stop = i * BLOCK, (i + 1) * BLOCK
            query = q_ref[h, start:stop, :]
            grads = do_ref[h, start:stop, :]
            log_total = log_ref[h, :, start:stop]
            spans = [(start, stop)] + ([(0, start)] if i else [])
            probs, grad_probs = [], []
            for lo, hi in spans:
                scores = mul(k_ref[g, lo:hi, :], query, NT)
                if hi == stop:
                    scores = jnp.where(keep, scores, MASKED)
                probs.append(jnp.exp(scores - log_total))
                grad_probs.append(mul(v_ref[g, lo:hi, :], grads, NT))
            inner = sum(jnp.sum(p * d, axis=0, keepdims=True) for p, d in zip(probs, grad_probs))
            dq = None
            for (lo, hi), p, d in zip(spans, probs, grad_probs):
                ds = (p * (d - inner)).astype(BF)
                dk_ref[g, lo:hi, :] += mul(ds, query)
                dv_ref[g, lo:hi, :] += mul(p.astype(BF), grads)
                term = mul(kt_ref[g, :, lo:hi], ds)
                dq = term if dq is None else dq + term
            dq_ref[h, :, start:stop] = dq * scale

    @pl.loop(0, tokens // BLOCK)
    def _(i):
        rows = pl.ds(pl.multiple_of(i * BLOCK, BLOCK), BLOCK)
        tables = (cos_ref[rows, :], -sin_ref[rows, :])
        for h in range(0, heads, per):
            pair = jnp.concatenate([dq_ref[h + u, :, rows] for u in range(per)], axis=0).T
            out_ref[rows, h * HD : h * HD + 128] = rotate_lanes(pair, *tables).astype(BF)
        for g in range(0, groups, per):
            pair = jnp.concatenate([dk_ref[g + u, rows, :] for u in range(per)], axis=1)
            lane = (heads + g) * HD
            out_ref[rows, lane : lane + 128] = rotate_lanes(pair, *tables).astype(BF)
            pair = jnp.concatenate([dv_ref[g + u, rows, :] for u in range(per)], axis=1)
            lane = (heads + groups + g) * HD
            out_ref[rows, lane : lane + 128] = pair.astype(BF)


    for s, block_ref in enumerate(block_refs):
        block_ref[...] = mul(out_ref[span_of(s), :], w_ref[...], NT).astype(BF)

    @pl.when(at_ref[0] < count // 2)
    def _():
        end_ref[...] = block_refs[count - 1][...]

    @pl.when(at_ref[0] >= count // 2)
    def _():
        end_ref[...] = block_refs[1][...]


def attend_back(grad_pieces, q, k, v, logs, tables, weights, at):
    heads, tokens, _ = q.shape
    groups = k.shape[0]
    count = len(grad_pieces)
    lanes = (heads + 2 * groups) * HD
    width = weights[0].shape[0]
    block = jax.ShapeDtypeStruct((BLOCK, width), BF)
    return pl.pallas_call(
        attend_back_kernel,
        in_specs=[SMEM] + [VMEM] * (9 + count),
        out_shape=[block] * count + [jax.ShapeDtypeStruct((tokens, lanes), BF), block],
        scratch_shapes=[
            pltpu.VMEM((width, lanes), BF),
            pltpu.VMEM((heads, tokens, HD), BF),
            pltpu.VMEM((groups, HD, tokens), BF),
            pltpu.VMEM((heads, HD, tokens), F32),
            pltpu.VMEM((groups, tokens, HD), F32),
            pltpu.VMEM((groups, tokens, HD), F32),
        ],
        compiler_params=pltpu.CompilerParams(vmem_limit_bytes=48 << 20),
        cost_estimate=takes(20),
    )(at[None], q, k, v, logs, *tables, *weights, *grad_pieces)


def pack_kernel(gate_ref, up_ref, down_ref, out_ref):
    part = down_ref.shape[0]
    out_ref[:part, :] = gate_ref[...].astype(F32).T.astype(BF)
    out_ref[part : 2 * part, :] = up_ref[...].astype(F32).T.astype(BF)
    out_ref[2 * part :, :] = down_ref[...]


def pack(gate, up, down):
    return pl.pallas_call(
        pack_kernel,
        out_shape=jax.ShapeDtypeStruct((3 * down.shape[0], down.shape[1]), BF),
        compiler_params=pltpu.CompilerParams(vmem_limit_bytes=32 << 20),
        cost_estimate=takes(3),
    )(gate, up, down)


def expert_kernel(order_ref, near_ref, far_ref, extra_near_ref, extra_far_ref, router_ref, parts_ref, *refs, top, count):
    out_refs, gin_refs, terms_ref = refs[:2], refs[2:5], refs[5]
    weights_ref, sums_ref = refs[6:]
    step = pl.program_id(0)
    steps = pl.num_programs(0)
    hidden_width, width = weights_ref.shape[0] // 3, weights_ref.shape[1]
    gate_up = slice(0, 2 * hidden_width)
    down = slice(2 * hidden_width, 3 * hidden_width)
    own = order_ref[0]
    experts = order_ref[1]
    part = hidden_width // count
    spans = [
        (pl.ds((3 * s + j) * part, part), pl.ds(j * hidden_width + s * part, part))
        for s in range(count)
        for j in range(3)
    ]

    @pl.when(step == 0)
    def _():
        sums_ref[...] = jnp.zeros_like(sums_ref)
        for there, here in spans:
            weights_ref[here, :] = parts_ref[there, :]

    near = step < steps // 2
    rows = jnp.where(near, near_ref[...], far_ref[...])
    extra = jnp.where(near, extra_near_ref[...], extra_far_ref[...])
    grads32 = extra[:, :width].astype(F32)
    named = extra[:, width:].astype(F32)

    lane = lax.broadcasted_iota(jnp.int32, (rows.shape[0], LANES), 1)
    lane32 = lane.astype(F32)
    chosen = lane32 == named[:, 0:1]
    for k in range(1, top):
        chosen = chosen | (lane32 == named[:, k : k + 1])
    logits = jnp.where(chosen, mul(rows, router_ref[...]), MASKED)
    weights = jnp.where(chosen, jnp.exp(logits - jnp.max(logits, axis=-1, keepdims=True)), 0.0)
    mine = jnp.sum(jnp.where(lane == own, weights, 0.0), axis=-1, keepdims=True)
    gate = mine / jnp.sum(weights, axis=-1, keepdims=True)

    both = mul(rows, weights_ref[gate_up, :], NT)
    gate_vals = both[:, :hidden_width]
    up_vals = both[:, hidden_width:]
    sigma = jax.nn.sigmoid(gate_vals)
    active = gate_vals * sigma
    hidden = (active * up_vals).astype(BF)
    grad_out = (gate * grads32).astype(BF)
    grad_hidden = mul(grad_out, weights_ref[down, :], NT)
    expert_out = mul(hidden, weights_ref[down, :])
    combined = (gate * expert_out).astype(BF)
    score = jnp.sum(grads32 * expert_out, axis=-1, keepdims=True)
    high = score.astype(BF).astype(F32)
    scores = jnp.where(lane == own, high, jnp.where(lane == own + experts, score - high, 0.0)).astype(BF)
    grad_gate_vals = (grad_hidden * up_vals * sigma * (1.0 + gate_vals * (1.0 - sigma))).astype(BF)
    grad_up_vals = (grad_hidden * active).astype(BF)
    grad_both = jnp.concatenate([grad_gate_vals, grad_up_vals], axis=1)
    grad_in = mul(grad_both, weights_ref[gate_up, :]).astype(BF)
    sums_ref[gate_up, :] += mul(grad_both, rows, TN)
    sums_ref[down, :] += mul(hidden, grad_out, TN)
    far_step = step - steps // 2
    for k, now in enumerate((near, jnp.logical_not(near))):

        @pl.when(now)
        def _():
            out_refs[k][...] = combined

    even = lax.rem(step, 2) == 0
    for k, now in enumerate((near, (far_step >= 0) & even, (far_step >= 0) & jnp.logical_not(even))):

        @pl.when(now)
        def _():
            gin_refs[k][:, :width] = grad_in
            gin_refs[k][:, width:] = scores

    @pl.when(step == steps - 1)
    def _():
        for there, here in spans:
            terms_ref[there, :] = sums_ref[here, :].astype(BF)


def run_experts(order, near, far, extra_near, extra_far, router, parts, top, count):
    total, width = 2 * near.shape[0], near.shape[1]
    steps = total // BLOCK
    half_steps = steps // 2
    wide = extra_near.shape[1]
    hidden = parts.shape[0] // 3

    def by_set(lanes):
        return [
            pl.BlockSpec((BLOCK, lanes), lambda i, o: (jnp.minimum(i, half_steps - 1), 0)),
            pl.BlockSpec((BLOCK, lanes), lambda i, o: (jnp.maximum(i - half_steps, 0), 0)),
        ]

    half = by_set(width)
    far_pair = pl.BlockSpec((BLOCK, wide), lambda i, o: (jnp.maximum(i - half_steps, 0) // 2, 0))
    half_wide = [by_set(wide)[0], far_pair, far_pair]
    whole = pl.BlockSpec((3 * hidden, width), lambda i, o: (0, 0), pipeline_mode=pl.Buffered(1))
    return pl.pallas_call(
        functools.partial(expert_kernel, top=top, count=count),
        grid_spec=pltpu.PrefetchScalarGridSpec(
            num_scalar_prefetch=1,
            grid=(steps,),
            in_specs=[
                *by_set(width),
                *by_set(wide),
                pl.BlockSpec((width, LANES), lambda i, o: (0, 0)),
                whole,
            ],
            out_specs=half + half_wide + [whole],
            scratch_shapes=[
                pltpu.VMEM((3 * hidden, width), BF),
                pltpu.VMEM((3 * hidden, width), F32),
            ],
        ),
        out_shape=[jax.ShapeDtypeStruct((total // 2, width), BF)] * 2
        + [jax.ShapeDtypeStruct((total // 2, wide), BF)]
        + [jax.ShapeDtypeStruct((total // 4, wide), BF)] * 2
        + [jax.ShapeDtypeStruct((3 * hidden, width), BF)],
        compiler_params=pltpu.CompilerParams(vmem_limit_bytes=58 << 20),
        cost_estimate=takes(5 * steps),
    )(order, near, far, extra_near, extra_far, router, parts)


def keep_kernel(x_ref, out_ref):
    out_ref[...] = x_ref[...]


def keep(x, us):
    return pl.pallas_call(
        keep_kernel, out_shape=jax.ShapeDtypeStruct(x.shape, x.dtype), cost_estimate=takes(us)
    )(x)


def set_rows_kernel(order_ref, near_ref, far_ref, out_ref, small_ref, norm_ref, *, part, few_rows):
    rows, width = near_ref.shape[0] // 4, near_ref.shape[1]
    norm = jnp.zeros((1, width), F32)
    for k in range(8):
        source = near_ref if k < 4 else far_ref
        block = source[(k % 4) * rows : (k % 4 + 1) * rows, :].astype(F32)
        device = order_ref[k]
        out_ref[pl.ds(pl.multiple_of(device * part, 8), part), :] = block[:part]
        small_ref[pl.ds(pl.multiple_of(device * few_rows, 8), few_rows), :] = block[part : part + few_rows]
        norm += block[rows - 1 :]
    norm_ref[...] = norm


def set_rows(order, near, far, part, few_rows):
    width = near.shape[1]
    return pl.pallas_call(
        functools.partial(set_rows_kernel, part=part, few_rows=few_rows),
        in_specs=[SMEM, VMEM, VMEM],
        out_shape=[
            jax.ShapeDtypeStruct((8 * part, width), F32),
            jax.ShapeDtypeStruct((8 * few_rows, width), F32),
            jax.ShapeDtypeStruct((1, width), F32),
        ],
        compiler_params=pltpu.CompilerParams(vmem_limit_bytes=32 << 20),
        cost_estimate=takes(3),
    )(order, near, far)


def join(*values):
    return lax.optimization_barrier(values)


def add(a, b):
    return (a.astype(F32) + b.astype(F32)).astype(BF)


def swap(x, bit):
    return lax.ppermute(x, "ep", [(i, i ^ bit) for i in range(lax.axis_size("ep"))])


def turn(x, by):
    n = lax.axis_size("tp")
    return lax.ppermute(x, "tp", [(i, (i + by) % n) for i in range(n)])


def step_both(right, left, low=0, high=None):
    n = lax.axis_size("tp")
    pairs = [(i, i + 1) for i in range(low, n - 1 if high is None else high)]
    mirror = [(n - 1 - i, n - 1 - j) for i, j in pairs]
    return lax.ppermute(right, "tp", pairs), lax.ppermute(left, "tp", mirror)


def step_ends(right, left, low, high):
    n = lax.axis_size("tp")
    at = lax.axis_index("tp")
    pairs = [(i, i + 1) for i in range(low, high)]
    give = right if right is left else jnp.where((at >= low) & (at < high), right, left)
    return lax.ppermute(give, "tp", pairs + [(n - 1 - i, n - 1 - j) for i, j in pairs])


def by_side(got, low, high):
    at = lax.axis_index("tp")
    ahead = (at > low) & (at <= high)
    return jnp.where(ahead, got, 0), jnp.where(ahead, 0, got)


def gather_first(x):
    half = x.shape[0] // 2
    return swap(x[:half], 2), swap(x[half:], 4)


def gather_second(x, got):
    half = x.shape[0] // 2
    first, second = join(
        jnp.concatenate([x[:half], got[0]], axis=0), jnp.concatenate([x[half:], got[1]], axis=0)
    )
    return (first, second), (swap(first, 4), swap(second, 2))


def gather_near(held, got):
    return jnp.concatenate([held[0], got[0], held[1], got[1]], axis=0)


def gather_halves():
    n = lax.axis_size("ep")
    if n != 8:
        return [(jnp.int32(k // 2), k % 2) for k in range(2 * n)]
    at = lax.axis_index("ep").astype(jnp.int32)
    near = [(0, 0), (2, 0), (4, 0), (6, 0), (0, 1), (4, 1), (2, 1), (6, 1)]
    return [(jnp.bitwise_xor(at, k + core), half) for core in (0, 1) for k, half in near]


def gather_whole(x):
    whole = lax.all_gather(x, "ep", tiled=True)
    return whole[: whole.shape[0] // 2], whole[whole.shape[0] // 2 :]


def sum_cores(near, far):
    rows = near.shape[0] // 4
    return join(*[add(near[j * rows : (j + 1) * rows], far[j * rows : (j + 1) * rows]) for j in range(4)])


def sum_first(sums):
    return swap(sums[1], 4), swap(sums[3], 2)


def sum_second(sums, got):
    first, second = join(add(sums[0], got[0]), add(sums[2], got[1]))
    half = first.shape[0] // 2
    return (first, second), (swap(first[half:], 2), swap(second[half:], 4))


def sum_last(sums, got):
    half = sums[0].shape[0] // 2
    return jnp.concatenate([s[:half].astype(F32) + g.astype(F32) for s, g in zip(sums, got)], axis=0)


def sum_whole(near, far):
    n = lax.axis_size("ep")
    terms = jnp.concatenate([near, far], axis=0).reshape(n, -1, near.shape[1])
    return lax.psum_scatter(terms, "ep", scatter_dimension=0, tiled=False).astype(F32)


def spread(own, steps, last):
    n = lax.axis_size("tp")
    at = lax.axis_index("tp").astype(jnp.int32)
    rows, width = own.shape
    out = jnp.zeros((n * rows, width), BF)
    for t, step in enumerate(steps):
        for got, place in zip(step, (at - t - 1, at + t + 1)):
            place = jnp.where((place >= 0) & (place < n), place, at)
            out = lax.dynamic_update_slice(out, got, (place * rows, 0))
    place = jnp.where(at == n - 1, 0, jnp.where(at == 0, n - 1, at))
    out = lax.dynamic_update_slice(out, last, (place * rows, 0))
    return lax.dynamic_update_slice(out, own, (at * rows, 0))


def body(
    inputs,
    routes,
    norm_gain,
    query_weight,
    key_weight,
    value_weight,
    output_weight,
    mixer_gain,
    router_weight,
    gate_weight,
    up_weight,
    down_weight,
    cotangent,
):
    tokens, width = inputs.shape
    experts = router_weight.shape[1]
    top = routes.shape[1]
    n_ep = lax.axis_size("ep")
    n_tp = lax.axis_size("tp")
    fine = n_ep == 8
    ep_at = lax.axis_index("ep").astype(jnp.int32)
    tp_at = lax.axis_index("tp").astype(jnp.int32)
    quarter = tokens // n_tp
    heads_width = query_weight.shape[1]
    groups_width = key_weight.shape[1]

    def mine(x):
        return lax.dynamic_slice_in_dim(x, tp_at * quarter, quarter, 0)

    part = output_weight.shape[0] // n_ep
    output_part = lax.dynamic_slice_in_dim(output_weight, ep_at * part, part, 0)
    output_parts = [output_part] + [turn(output_part, -s) for s in range(1, n_tp)]

    hidden_part = gate_weight.shape[2]
    expert_part = pack(gate_weight[0], up_weight[0], down_weight[0])
    expert_parts = lax.all_gather(expert_part, "tp", tiled=True)

    routes_mine = mine(routes)
    grad_top_mine = mine(cotangent)
    named = jnp.pad(routes_mine.astype(BF), ((0, 0), (0, LANES - top)), constant_values=-1.0)
    extra = jnp.concatenate([grad_top_mine, named], axis=1)
    tables = rotary_lanes(tokens)
    qkv_weights = (query_weight, key_weight, value_weight)
    if fine:
        extra_got = gather_first(extra)
        qkv_weights, expert_part = join(qkv_weights, expert_part)
    else:
        output_part = jnp.concatenate(output_parts, axis=0)
        extra_near, extra_far = gather_whole(extra)

    *mixed, query, key, value, logs = attend(
        inputs,
        norm_gain,
        qkv_weights,
        tables,
        heads_width // HD,
        groups_width // HD,
        tp_at,
    )
    if fine:
        mixed, output_parts, extra_got = join(mixed, output_parts, extra_got)
        output_part = jnp.concatenate(output_parts, axis=0)

    router = jnp.pad(router_weight, ((0, 0), (0, LANES - experts)))

    ends = [turn(mixed[s], s) for s in (1, n_tp - 1)]
    if fine:
        output_got = gather_first(output_part)
        ends, output_got, mixed, router = join(ends, output_got, mixed, router)
        router = keep(router, 20)
    mixed = [mixed[0], ends[0]] + [turn(mixed[s], s) for s in range(2, n_tp - 1)] + [ends[1]]
    if fine:
        output_held, output_got = gather_second(output_part, output_got)
        mixed, output_held, output_got, router, extra, extra_got = join(
            mixed, output_held, output_got, router, extra, extra_got
        )
        near = gather_near(output_held, output_got)
        far = swap(near, 1)
        extra_held, extra_got = gather_second(extra, extra_got)
    else:
        near, far = gather_whole(output_part)
    halves = gather_halves()
    output_whole = jnp.zeros((n_tp, n_ep, part, width), BF)
    for j, blocks in enumerate((near, far)):
        blocks = blocks.reshape(n_ep, n_tp // 2, part, width)
        for k in range(n_ep):
            device, half = halves[j * n_ep + k]
            for u in range(n_tp // 2):
                place = (n_tp - half * (n_tp // 2) - u) % n_tp
                output_whole = lax.dynamic_update_slice(
                    output_whole, blocks[k, u][None, None], (place, device, 0, 0)
                )
    output_whole = output_whole.reshape(n_tp * heads_width, width)

    mixed_mine = jnp.concatenate(mixed, axis=1)
    branch = mul(mixed_mine, output_whole)
    inputs_mine = mine(inputs).astype(F32)
    attended = inputs_mine + branch
    inverse_two = lax.rsqrt(jnp.mean(attended * attended, axis=-1, keepdims=True) + EPS)
    unit_two = attended * inverse_two
    routed_in = (unit_two * mixer_gain).astype(BF)
    logits = mul(routed_in, router_weight)
    ids = jnp.arange(experts, dtype=jnp.int32)
    chosen = jnp.any(routes_mine[:, :, None] == ids[None, None, :], axis=1)
    logits = jnp.where(chosen, logits, MASKED)
    weights = jnp.where(chosen, jnp.exp(logits - jnp.max(logits, axis=-1, keepdims=True)), 0.0)
    gates = weights / jnp.sum(weights, axis=-1, keepdims=True)

    order = jnp.concatenate([ep_at[None], jnp.full((1,), experts, jnp.int32)])
    if fine:
        got = gather_first(routed_in)
        got, gates, router, order, extra_held, extra_got = join(
            got, gates, router, order, extra_held, extra_got
        )
        extra_near = gather_near(extra_held, extra_got)
        extra_far = swap(extra_near, 1)
        held, got = gather_second(routed_in, got)
        held, got = join(held, got)
        near = gather_near(held, got)
        far = swap(near, 1)
    else:
        near, far = gather_whole(routed_in)
    out_near, out_far, gin_near, gin_even, gin_odd, terms = run_experts(
        order, near, far, extra_near, extra_far, router, expert_parts, top, n_tp
    )

    grad_expert = lax.psum_scatter(terms, "tp", scatter_dimension=0, tiled=True)

    if fine:
        gin_near = [gin_near[j * quarter : (j + 1) * quarter] for j in range(4)]
        other = swap(gin_odd, 1)
        gin = join(add(gin_near[1], other[:quarter]), add(gin_near[3], other[quarter:]))
        got = (swap(gin[0], 4), swap(gin[1], 2))
        out_far, gin_even, gin, gates = join(out_far, gin_even, gin, gates)
        gates = keep(gates, 20)
        gin_even = swap(gin_even, 1)
        out_far = swap(out_far, 1)
        got, out_far, gin_even, gates = join(got, out_far, gin_even, gates)
        gin = join(
            add(gin_near[0].astype(F32) + gin_even[:quarter].astype(F32), got[0]),
            add(gin_near[2].astype(F32) + gin_even[quarter:].astype(F32), got[1]),
        )
        got = [swap(g[quarter // 2 :], bit) for g, bit in zip(gin, (2, 4))]
        out = sum_cores(out_near, out_far)
        out_got = sum_first(out)
        gin, got = join(gin, got)
        grad_in = sum_last(gin, got)
    else:
        gin_far = jnp.stack([v.reshape(-1, quarter, v.shape[1]) for v in (gin_even, gin_odd)], axis=1)
        grad_in = sum_whole(gin_near, gin_far.reshape(gin_near.shape))
    grad_gates = grad_in[:, width : width + experts] + grad_in[:, width + experts : width + 2 * experts]
    inner_gate = jnp.sum(gates * grad_gates, axis=-1, keepdims=True)
    grad_logits = (gates * (grad_gates - inner_gate)).astype(BF)
    grad_routed = grad_in[:, :width] + mul(grad_logits, router_weight, NT)
    grad_top = grad_top_mine.astype(F32)
    scaled_two = grad_routed * mixer_gain
    grad_attended = grad_top + inverse_two * (
        scaled_two - unit_two * jnp.mean(scaled_two * unit_two, axis=-1, keepdims=True)
    )
    grad_branch = grad_attended.astype(BF)
    grad_mixed = mul(grad_branch, output_whole, NT).astype(BF)
    grad_mixed = [grad_mixed[:, s * heads_width : (s + 1) * heads_width] for s in range(n_tp)]

    grad_mixed, grad_branch = join(grad_mixed, grad_branch)
    grad_mixed = [grad_mixed[0]] + [turn(grad_mixed[s], -s) for s in range(1, n_tp)]
    if fine:
        out, out_got = sum_second(out, out_got)

    few = -(-(1 + experts) // n_ep)
    pad = 16 * (few // 16 + 1)
    small_rows = -(-few // 8) * 8
    grad_router = mul(routed_in, grad_logits, TN)
    grad_mixer = jnp.sum(grad_routed * unit_two, axis=0)
    small = jnp.concatenate([grad_mixer[None], grad_router.T], axis=0).astype(BF)
    small = jnp.pad(small, ((0, few * n_ep - 1 - experts), (0, 0))).reshape(n_ep, few, width)
    small = jnp.pad(small, ((0, 0), (0, pad - few), (0, 0)))
    grad_output = mul(mixed_mine, grad_branch, TN).astype(BF)
    grad_output = grad_output.reshape(n_tp, n_ep, part, width).transpose(1, 0, 2, 3)
    grad_output = jnp.concatenate([grad_output.reshape(n_ep, n_tp * part, width), small], axis=1)
    if fine:
        core, chip = lax.rem(ep_at, 2), lax.div(ep_at, 2)
        grad_output = grad_output.reshape((n_ep // 2, 2) + grad_output.shape[1:])
        other_output = lax.dynamic_index_in_dim(grad_output, 1 - core, 1, False)
        grad_output = lax.dynamic_index_in_dim(grad_output, core, 1, False)
        grad_mixed, out, out_got, other_output, grad_output = join(
            grad_mixed, out, out_got, other_output, grad_output
        )
        out = sum_last(out, out_got)
        other_output = swap(other_output, 1)
    else:
        out = sum_whole(out_near, out_far)
    result_mine = (attended + out).astype(BF)

    result_mine, grad_mixed = join(result_mine, grad_mixed)
    result_steps = [step_both(result_mine, result_mine)]
    *blocks, grad_qkv, end_block = attend_back(grad_mixed, query, key, value, logs, tables, qkv_weights, tp_at)
    if fine:
        blocks, grad_qkv, end_block, result_steps[0], other_output, grad_expert, inputs = join(
            blocks, grad_qkv, end_block, result_steps[0], other_output, grad_expert, inputs
        )
    else:
        blocks, grad_qkv, end_block, result_steps[0] = join(blocks, grad_qkv, end_block, result_steps[0])

    inputs32 = inputs.astype(F32)
    normed = inputs32 * lax.rsqrt(jnp.mean(inputs32 * inputs32, axis=-1, keepdims=True) + EPS)
    normed = (normed * norm_gain).astype(BF)
    grad_qkv_w = mul(normed, grad_qkv, TN).astype(BF)

    def chip_halves(half, *places):
        rows = grad_output.shape[1] // 2
        picked = []
        for j in places:
            chip_at = (jnp.bitwise_xor(chip, j), half * rows, 0)
            size = (1, rows, width)
            picked.append(
                add(
                    lax.dynamic_slice(grad_output, chip_at, size)[0],
                    lax.dynamic_slice(other_output, chip_at, size)[0],
                )
            )
        return jnp.concatenate(picked, axis=0)

    if fine:
        got = join(chip_halves(0, 2, 3), chip_halves(1, 1, 3))
        got = (swap(got[0], 4), swap(got[1], 2))
    result_steps.append(step_both(*result_steps[-1], 1))
    sent = step_ends(end_block, end_block, 0, 1)
    if fine:
        sent, result_steps[-1], got, grad_qkv_w = join(sent, result_steps[-1], got, grad_qkv_w)
        sums, got = sum_second((chip_halves(0, 0, 1), None, chip_halves(1, 0, 2)), got)
    else:
        sent, result_steps[-1], grad_qkv_w, grad_expert = join(
            sent, result_steps[-1], grad_qkv_w, grad_expert
        )
    grad_qkv_w = lax.psum(grad_qkv_w, "ep")
    sent = by_side(sent, 0, 1)
    result_last = None
    for t in range(2, n_tp):
        sent = step_both(add(blocks[n_tp - t], sent[0]), add(blocks[t], sent[1]), 0, t)
        if t < n_tp - 1:
            result_last = step_ends(*result_steps[-1], t, n_tp - 1)
            if fine:
                sent, result_last, got, sums = join(sent, result_last, got, sums)
                grad_output = sum_last(sums, got).astype(BF)
            else:
                sent, result_last = join(sent, result_last)
                grad_output = lax.psum_scatter(grad_output, "ep", scatter_dimension=0, tiled=False)
            pieces = [
                jnp.concatenate([grad_output[s * part : (s + 1) * part], grad_output[n_tp * part :][:small_rows]], axis=0)
                for s in range(n_tp)
            ]
    got = [turn(pieces[s], -s) for s in range(1, n_tp)]
    sent, result_steps, result_last = join(sent, result_steps, result_last)
    grad_normed = blocks[0].astype(F32) + sent[0].astype(F32) + sent[1].astype(F32)
    inputs_mine = mine(inputs).astype(F32)
    inverse_one = lax.rsqrt(jnp.mean(inputs_mine * inputs_mine, axis=-1, keepdims=True) + EPS)
    unit_one = inputs_mine * inverse_one
    scaled_one = grad_normed * norm_gain
    grad_inputs = grad_attended + inverse_one * (
        scaled_one - unit_one * jnp.mean(scaled_one * unit_one, axis=-1, keepdims=True)
    )
    grad_inputs = grad_inputs.astype(BF)
    grad_norm = jnp.sum(grad_normed * unit_one, axis=0)
    used = -(-(part + small_rows + 1) // 32) * 32

    grad_inputs, grad_norm = join(grad_inputs, grad_norm)
    input_steps = [step_both(grad_inputs, grad_inputs)]
    grad_norm = grad_norm[None]
    norm_got = [turn(grad_norm, s) for s in range(1, n_tp)]
    got, norm_got, input_steps[0] = join(got, norm_got, input_steps[0])
    grad_norm = (grad_norm + sum(norm_got))[0]
    grad_output = (pieces[0].astype(F32) + sum(v.astype(F32) for v in got)).astype(BF)
    grad_output = jnp.pad(grad_output, ((0, used - grad_output.shape[0]), (0, 0)))
    grad_output = grad_output.at[used - 1].set(grad_norm.astype(BF))
    if fine:
        got = [swap(grad_output, k) for k in (2, 4, 6)]
    grad_expert = grad_expert.reshape(3, -1, width).astype(F32)
    grad_gate_w, grad_up_w, grad_down_w = grad_expert[0].T, grad_expert[1].T, grad_expert[2]
    for t in range(1, n_tp - 2):
        input_steps.append(step_both(*input_steps[-1], t))
    if fine:
        got, input_steps[-1], grad_gate_w, grad_up_w, grad_down_w = join(
            got, input_steps[-1], grad_gate_w, grad_up_w, grad_down_w
        )
        near = jnp.concatenate([grad_output] + got, axis=0)
        far = swap(near, 1)
        far, grad_qkv_w = join(far, grad_qkv_w)
        devices = jnp.stack([jnp.bitwise_xor(ep_at, jnp.int32(k)) for k in (0, 2, 4, 6, 1, 3, 5, 7)])
        grad_output, small, grad_norm = set_rows(devices, near, far, part, small_rows)
        small = small.reshape(n_ep, small_rows, width)
        grad_norm = grad_norm[0]
    else:
        gathered = lax.all_gather(grad_output, "ep")
        small = gathered[:, part : part + small_rows].astype(F32)
        grad_norm = jnp.sum(gathered[:, used - 1].astype(F32), axis=0)
        grad_output = gathered[:, :part].reshape(heads_width, width).astype(F32)
    small = small[:, :few].reshape(n_ep * few, width)[: 1 + experts]
    result = spread(result_mine, result_steps, result_last)
    input_last = step_ends(*input_steps[-1], n_tp - 2, n_tp - 1)
    grad_qkv_w = grad_qkv_w.astype(F32)
    qkv_grads = (
        grad_qkv_w[:, :heads_width],
        grad_qkv_w[:, heads_width : heads_width + groups_width],
        grad_qkv_w[:, heads_width + groups_width :],
    )
    grad_norm, small, grad_output, input_last, qkv_grads, result = join(
        grad_norm, small, grad_output, input_last, qkv_grads, result
    )
    grad_inputs = spread(grad_inputs, input_steps, input_last)
    return (
        result,
        grad_inputs,
        grad_norm,
        *qkv_grads,
        grad_output,
        small[0],
        small[1:].T,
        grad_gate_w[None],
        grad_up_w[None],
        grad_down_w[None],
    )


def solution(mesh):
    placed = (
        P("ep", None),
        P("ep", None),
        P(),
        P(None, "tp"),
        P(None, "tp"),
        P(None, "tp"),
        P("tp", None),
        P(),
        P(),
        P("ep", None, "tp"),
        P("ep", None, "tp"),
        P("ep", "tp", None),
        P("ep", None),
    )
    return jax.shard_map(
        body,
        mesh=mesh,
        in_specs=placed,
        out_specs=(
            P("ep", None),
            P("ep", None),
            P(),
            P(None, "tp"),
            P(None, "tp"),
            P(None, "tp"),
            P("tp", None),
            P(),
            P(),
            P("ep", None, "tp"),
            P("ep", None, "tp"),
            P("ep", "tp", None),
        ),
        check_vma=False,
    )
```

```python
import functools

import jax
import jax.numpy as jnp
import numpy as np
from jax import lax
from jax.experimental import pallas as pl
from jax.experimental.pallas import tpu as pltpu
from jax.sharding import PartitionSpec as P

HD = 64
LEN = 1024
EPS = 1e-06
MASKED = -1e30
BF = jnp.bfloat16
F32 = jnp.float32
BLOCK = 256
LANES = 128
NT = (((1,), (1,)), ((), ()))
TN = (((0,), (0,)), ((), ()))


def takes(us):
    return pl.CostEstimate(flops=int(us * 1.15e9), bytes_accessed=0, transcendentals=0)


def mul(a, b, dims=(((1,), (0,)), ((), ()))):
    return lax.dot_general(a, b, dims, preferred_element_type=F32)


def rotate_lanes(y, cos, sin):
    half = HD // 2
    first = lax.broadcasted_iota(jnp.int32, y.shape, 1) % HD < half
    return y * cos + jnp.where(first, pltpu.roll(y, 128 - half, 1), pltpu.roll(y, half, 1)) * sin


def rotary_lanes(tokens):
    lane = np.arange(128)
    freqs = np.float32(10000.0) ** (-(lane % (HD // 2)).astype(np.float32) * np.float32(2.0 / HD))
    angles = (np.arange(tokens) % LEN).astype(np.float32)[:, None] * freqs[None, :].astype(np.float32)
    sign = np.where(lane % HD < HD // 2, np.float32(-1.0), np.float32(1.0))
    return jnp.asarray(np.cos(angles), F32), jnp.asarray(np.sin(angles) * sign, F32)


def causal(block):
    key_at = lax.broadcasted_iota(jnp.int32, (block, block), 0)
    query_at = lax.broadcasted_iota(jnp.int32, (block, block), 1)
    return key_at <= query_at


def attend_kernel(at_ref, x_ref, gain_ref, wq_ref, wk_ref, wv_ref, cos_ref, sin_ref, *refs):
    pieces, (q_ref, k_ref, v_ref, log_ref, w_ref, vt_ref, out_ref) = refs[:-7], refs[-7:]
    tokens = x_ref.shape[0]
    heads, groups = q_ref.shape[0], k_ref.shape[0]
    repeat = heads // groups
    per = 128 // HD
    scale = HD ** (-0.5)
    w_ref[...] = jnp.concatenate([wq_ref[...], wk_ref[...], wv_ref[...]], axis=1)

    @pl.loop(0, tokens // BLOCK)
    def _(i):
        at = pl.multiple_of(i * BLOCK, BLOCK)
        rows = pl.ds(at, BLOCK)
        x = x_ref[rows, :].astype(F32)
        inverse = lax.rsqrt(jnp.mean(x * x, axis=-1, keepdims=True) + EPS)
        normed = (x * inverse * gain_ref[...]).astype(BF)
        raw = mul(normed, w_ref[...])
        tables = (cos_ref[rows, :], sin_ref[rows, :])
        for h in range(0, heads, per):
            turned = rotate_lanes(raw[:, h * HD : h * HD + 128], *tables) * scale
            for u in range(per):
                q_ref[h + u, rows, :] = turned[:, u * HD : (u + 1) * HD].astype(BF)
        for g in range(0, groups, per):
            lane = (heads + g) * HD
            turned = rotate_lanes(raw[:, lane : lane + 128], *tables)
            lane = (heads + groups + g) * HD
            value = raw[:, lane : lane + 128]
            turned_value = value.T
            for u in range(per):
                k_ref[g + u, rows, :] = turned[:, u * HD : (u + 1) * HD].astype(BF)
                v_ref[g + u, rows, :] = value[:, u * HD : (u + 1) * HD].astype(BF)
                vt_ref[g + u, :, rows] = turned_value[u * HD : (u + 1) * HD].astype(BF)

    keep = causal(BLOCK)

    @pl.loop(0, heads)
    def _(h):
        g = h // repeat
        for i in range(tokens // BLOCK):
            start, stop = i * BLOCK, (i + 1) * BLOCK
            query = q_ref[h, start:stop, :]
            parts = [jnp.where(keep, mul(k_ref[g, start:stop, :], query, NT), MASKED)]
            if i:
                parts.append(mul(k_ref[g, :start, :], query, NT))
            peak = jnp.max(parts[0], axis=0, keepdims=True)
            for part in parts[1:]:
                peak = jnp.maximum(peak, jnp.max(part, axis=0, keepdims=True))
            weights = [jnp.exp(part - peak) for part in parts]
            total = sum(jnp.sum(w, axis=0, keepdims=True) for w in weights)
            shrink = 1.0 / total
            mixed = mul(vt_ref[g, :, start:stop], weights[0].astype(BF))
            if i:
                mixed += mul(vt_ref[g, :, :start], weights[1].astype(BF))
            out_ref[h, :, start:stop] = mixed * shrink
            log_ref[h, :, start:stop] = peak + jnp.log(total)

    for s, piece_ref in enumerate(pieces):
        span = pl.ds(pl.multiple_of(lax.rem(at_ref[0] + s, len(pieces)) * BLOCK, BLOCK), BLOCK)
        for h in range(0, heads, per):
            pair = jnp.concatenate([out_ref[h + u, :, span] for u in range(per)], axis=0)
            piece_ref[:, h * HD : h * HD + 128] = pair.T.astype(BF)


VMEM = pl.BlockSpec(memory_space=pltpu.VMEM)
SMEM = pl.BlockSpec(memory_space=pltpu.SMEM)


def attend(x, gain, weights, tables, heads, groups, at):
    tokens, width = x.shape
    count = tokens // BLOCK
    return pl.pallas_call(
        attend_kernel,
        in_specs=[SMEM] + [VMEM] * 7,
        out_shape=[jax.ShapeDtypeStruct((BLOCK, heads * HD), BF)] * count
        + [
            jax.ShapeDtypeStruct((heads, tokens, HD), BF),
            jax.ShapeDtypeStruct((groups, tokens, HD), BF),
            jax.ShapeDtypeStruct((groups, tokens, HD), BF),
            jax.ShapeDtypeStruct((heads, 1, tokens), F32),
        ],
        scratch_shapes=[
            pltpu.VMEM((width, (heads + 2 * groups) * HD), BF),
            pltpu.VMEM((groups, HD, tokens), BF),
            pltpu.VMEM((heads, HD, tokens), F32),
        ],
        compiler_params=pltpu.CompilerParams(vmem_limit_bytes=48 << 20),
        cost_estimate=takes(20),
    )(at[None], x, gain[None], *weights, *tables)


def attend_back_kernel(at_ref, q_ref, k_ref, v_ref, log_ref, cos_ref, sin_ref, wq_ref, wk_ref, wv_ref, *refs):
    w_ref, do_ref, kt_ref, dq_ref, dk_ref, dv_ref = refs[-6:]
    out_ref, end_ref = refs[-8:-6]
    count = (len(refs) - 8) // 2
    grad_refs, block_refs = refs[:count], refs[count:-8]
    tokens = q_ref.shape[1]
    heads, groups = q_ref.shape[0], k_ref.shape[0]
    repeat = heads // groups
    per = 128 // HD
    scale = HD ** (-0.5)
    w_ref[...] = jnp.concatenate([wq_ref[...], wk_ref[...], wv_ref[...]], axis=1)
    dk_ref[...] = jnp.zeros_like(dk_ref)
    dv_ref[...] = jnp.zeros_like(dv_ref)

    def span_of(s):
        return pl.ds(pl.multiple_of(lax.rem(at_ref[0] + s, count) * BLOCK, BLOCK), BLOCK)

    for s, grad_ref in enumerate(grad_refs):
        for h in range(heads):
            do_ref[h, span_of(s), :] = grad_ref[:, h * HD : (h + 1) * HD]

    @pl.loop(0, tokens // BLOCK)
    def _(i):
        rows = pl.ds(pl.multiple_of(i * BLOCK, BLOCK), BLOCK)
        for g in range(groups):
            kt_ref[g, :, rows] = k_ref[g, rows, :].astype(F32).T.astype(BF)

    keep = causal(BLOCK)

    @pl.loop(0, heads)
    def _(h):
        g = h // repeat
        for i in range(tokens // BLOCK):
            start, stop = i * BLOCK, (i + 1) * BLOCK
            query = q_ref[h, start:stop, :]
            grads = do_ref[h, start:stop, :]
            log_total = log_ref[h, :, start:stop]
            spans = [(start, stop)] + ([(0, start)] if i else [])
            probs, grad_probs = [], []
            for lo, hi in spans:
                scores = mul(k_ref[g, lo:hi, :], query, NT)
                if hi == stop:
                    scores = jnp.where(keep, scores, MASKED)
                probs.append(jnp.exp(scores - log_total))
                grad_probs.append(mul(v_ref[g, lo:hi, :], grads, NT))
            inner = sum(jnp.sum(p * d, axis=0, keepdims=True) for p, d in zip(probs, grad_probs))
            dq = None
            for (lo, hi), p, d in zip(spans, probs, grad_probs):
                ds = (p * (d - inner)).astype(BF)
                dk_ref[g, lo:hi, :] += mul(ds, query)
                dv_ref[g, lo:hi, :] += mul(p.astype(BF), grads)
                term = mul(kt_ref[g, :, lo:hi], ds)
                dq = term if dq is None else dq + term
            dq_ref[h, :, start:stop] = dq * scale

    @pl.loop(0, tokens // BLOCK)
    def _(i):
        rows = pl.ds(pl.multiple_of(i * BLOCK, BLOCK), BLOCK)
        tables = (cos_ref[rows, :], -sin_ref[rows, :])
        for h in range(0, heads, per):
            pair = jnp.concatenate([dq_ref[h + u, :, rows] for u in range(per)], axis=0).T
            out_ref[rows, h * HD : h * HD + 128] = rotate_lanes(pair, *tables).astype(BF)
        for g in range(0, groups, per):
            pair = jnp.concatenate([dk_ref[g + u, rows, :] for u in range(per)], axis=1)
            lane = (heads + g) * HD
            out_ref[rows, lane : lane + 128] = rotate_lanes(pair, *tables).astype(BF)
            pair = jnp.concatenate([dv_ref[g + u, rows, :] for u in range(per)], axis=1)
            lane = (heads + groups + g) * HD
            out_ref[rows, lane : lane + 128] = pair.astype(BF)


    for s, block_ref in enumerate(block_refs):
        block_ref[...] = mul(out_ref[span_of(s), :], w_ref[...], NT).astype(BF)

    @pl.when(at_ref[0] < count // 2)
    def _():
        end_ref[...] = block_refs[count - 1][...]

    @pl.when(at_ref[0] >= count // 2)
    def _():
        end_ref[...] = block_refs[1][...]


def attend_back(grad_pieces, q, k, v, logs, tables, weights, at):
    heads, tokens, _ = q.shape
    groups = k.shape[0]
    count = len(grad_pieces)
    lanes = (heads + 2 * groups) * HD
    width = weights[0].shape[0]
    block = jax.ShapeDtypeStruct((BLOCK, width), BF)
    return pl.pallas_call(
        attend_back_kernel,
        in_specs=[SMEM] + [VMEM] * (9 + count),
        out_shape=[block] * count + [jax.ShapeDtypeStruct((tokens, lanes), BF), block],
        scratch_shapes=[
            pltpu.VMEM((width, lanes), BF),
            pltpu.VMEM((heads, tokens, HD), BF),
            pltpu.VMEM((groups, HD, tokens), BF),
            pltpu.VMEM((heads, HD, tokens), F32),
            pltpu.VMEM((groups, tokens, HD), F32),
            pltpu.VMEM((groups, tokens, HD), F32),
        ],
        compiler_params=pltpu.CompilerParams(vmem_limit_bytes=48 << 20),
        cost_estimate=takes(20),
    )(at[None], q, k, v, logs, *tables, *weights, *grad_pieces)


def pack_kernel(gate_ref, up_ref, down_ref, out_ref):
    part = down_ref.shape[0]
    out_ref[:part, :] = gate_ref[...].astype(F32).T.astype(BF)
    out_ref[part : 2 * part, :] = up_ref[...].astype(F32).T.astype(BF)
    out_ref[2 * part :, :] = down_ref[...]


def pack(gate, up, down):
    return pl.pallas_call(
        pack_kernel,
        out_shape=jax.ShapeDtypeStruct((3 * down.shape[0], down.shape[1]), BF),
        compiler_params=pltpu.CompilerParams(vmem_limit_bytes=32 << 20),
        cost_estimate=takes(3),
    )(gate, up, down)


def expert_kernel(order_ref, near_ref, far_ref, extra_near_ref, extra_far_ref, router_ref, parts_ref, *refs, top, count):
    out_refs, gin_refs, terms_ref = refs[:2], refs[2:5], refs[5]
    weights_ref, sums_ref = refs[6:]
    step = pl.program_id(0)
    steps = pl.num_programs(0)
    hidden_width, width = weights_ref.shape[0] // 3, weights_ref.shape[1]
    gate_up = slice(0, 2 * hidden_width)
    down = slice(2 * hidden_width, 3 * hidden_width)
    own = order_ref[0]
    experts = order_ref[1]
    part = hidden_width // count
    spans = [
        (pl.ds((3 * s + j) * part, part), pl.ds(j * hidden_width + s * part, part))
        for s in range(count)
        for j in range(3)
    ]

    @pl.when(step == 0)
    def _():
        sums_ref[...] = jnp.zeros_like(sums_ref)
        for there, here in spans:
            weights_ref[here, :] = parts_ref[there, :]

    near = step < steps // 2
    rows = jnp.where(near, near_ref[...], far_ref[...])
    extra = jnp.where(near, extra_near_ref[...], extra_far_ref[...])
    grads32 = extra[:, :width].astype(F32)
    named = extra[:, width:].astype(F32)

    lane = lax.broadcasted_iota(jnp.int32, (rows.shape[0], LANES), 1)
    lane32 = lane.astype(F32)
    chosen = lane32 == named[:, 0:1]
    for k in range(1, top):
        chosen = chosen | (lane32 == named[:, k : k + 1])
    logits = jnp.where(chosen, mul(rows, router_ref[...]), MASKED)
    weights = jnp.where(chosen, jnp.exp(logits - jnp.max(logits, axis=-1, keepdims=True)), 0.0)
    mine = jnp.sum(jnp.where(lane == own, weights, 0.0), axis=-1, keepdims=True)
    gate = mine / jnp.sum(weights, axis=-1, keepdims=True)

    both = mul(rows, weights_ref[gate_up, :], NT)
    gate_vals = both[:, :hidden_width]
    up_vals = both[:, hidden_width:]
    sigma = jax.nn.sigmoid(gate_vals)
    active = gate_vals * sigma
    hidden = (active * up_vals).astype(BF)
    grad_out = (gate * grads32).astype(BF)
    grad_hidden = mul(grad_out, weights_ref[down, :], NT)
    expert_out = mul(hidden, weights_ref[down, :])
    combined = (gate * expert_out).astype(BF)
    score = jnp.sum(grads32 * expert_out, axis=-1, keepdims=True)
    high = score.astype(BF).astype(F32)
    scores = jnp.where(lane == own, high, jnp.where(lane == own + experts, score - high, 0.0)).astype(BF)
    grad_gate_vals = (grad_hidden * up_vals * sigma * (1.0 + gate_vals * (1.0 - sigma))).astype(BF)
    grad_up_vals = (grad_hidden * active).astype(BF)
    grad_both = jnp.concatenate([grad_gate_vals, grad_up_vals], axis=1)
    grad_in = mul(grad_both, weights_ref[gate_up, :]).astype(BF)
    sums_ref[gate_up, :] += mul(grad_both, rows, TN)
    sums_ref[down, :] += mul(hidden, grad_out, TN)
    far_step = step - steps // 2
    for k, now in enumerate((near, jnp.logical_not(near))):

        @pl.when(now)
        def _():
            out_refs[k][...] = combined

    even = lax.rem(step, 2) == 0
    for k, now in enumerate((near, (far_step >= 0) & even, (far_step >= 0) & jnp.logical_not(even))):

        @pl.when(now)
        def _():
            gin_refs[k][:, :width] = grad_in
            gin_refs[k][:, width:] = scores

    @pl.when(step == steps - 1)
    def _():
        for there, here in spans:
            terms_ref[there, :] = sums_ref[here, :].astype(BF)


def run_experts(order, near, far, extra_near, extra_far, router, parts, top, count):
    total, width = 2 * near.shape[0], near.shape[1]
    steps = total // BLOCK
    half_steps = steps // 2
    wide = extra_near.shape[1]
    hidden = parts.shape[0] // 3

    def by_set(lanes):
        return [
            pl.BlockSpec((BLOCK, lanes), lambda i, o: (jnp.minimum(i, half_steps - 1), 0)),
            pl.BlockSpec((BLOCK, lanes), lambda i, o: (jnp.maximum(i - half_steps, 0), 0)),
        ]

    half = by_set(width)
    far_pair = pl.BlockSpec((BLOCK, wide), lambda i, o: (jnp.maximum(i - half_steps, 0) // 2, 0))
    half_wide = [by_set(wide)[0], far_pair, far_pair]
    whole = pl.BlockSpec((3 * hidden, width), lambda i, o: (0, 0), pipeline_mode=pl.Buffered(1))
    return pl.pallas_call(
        functools.partial(expert_kernel, top=top, count=count),
        grid_spec=pltpu.PrefetchScalarGridSpec(
            num_scalar_prefetch=1,
            grid=(steps,),
            in_specs=[
                *by_set(width),
                *by_set(wide),
                pl.BlockSpec((width, LANES), lambda i, o: (0, 0)),
                whole,
            ],
            out_specs=half + half_wide + [whole],
            scratch_shapes=[
                pltpu.VMEM((3 * hidden, width), BF),
                pltpu.VMEM((3 * hidden, width), F32),
            ],
        ),
        out_shape=[jax.ShapeDtypeStruct((total // 2, width), BF)] * 2
        + [jax.ShapeDtypeStruct((total // 2, wide), BF)]
        + [jax.ShapeDtypeStruct((total // 4, wide), BF)] * 2
        + [jax.ShapeDtypeStruct((3 * hidden, width), BF)],
        compiler_params=pltpu.CompilerParams(vmem_limit_bytes=58 << 20),
        cost_estimate=takes(5 * steps),
    )(order, near, far, extra_near, extra_far, router, parts)


def keep_kernel(x_ref, out_ref):
    out_ref[...] = x_ref[...]


def keep(x, us):
    return pl.pallas_call(
        keep_kernel, out_shape=jax.ShapeDtypeStruct(x.shape, x.dtype), cost_estimate=takes(us)
    )(x)


def set_rows_kernel(order_ref, near_ref, far_ref, out_ref, small_ref, norm_ref, *, part, few_rows):
    rows, width = near_ref.shape[0] // 4, near_ref.shape[1]
    norm = jnp.zeros((1, width), F32)
    for k in range(8):
        source = near_ref if k < 4 else far_ref
        block = source[(k % 4) * rows : (k % 4 + 1) * rows, :].astype(F32)
        device = order_ref[k]
        out_ref[pl.ds(pl.multiple_of(device * part, 8), part), :] = block[:part]
        small_ref[pl.ds(pl.multiple_of(device * few_rows, 8), few_rows), :] = block[part : part + few_rows]
        norm += block[rows - 1 :]
    norm_ref[...] = norm


def set_rows(order, near, far, part, few_rows):
    width = near.shape[1]
    return pl.pallas_call(
        functools.partial(set_rows_kernel, part=part, few_rows=few_rows),
        in_specs=[SMEM, VMEM, VMEM],
        out_shape=[
            jax.ShapeDtypeStruct((8 * part, width), F32),
            jax.ShapeDtypeStruct((8 * few_rows, width), F32),
            jax.ShapeDtypeStruct((1, width), F32),
        ],
        compiler_params=pltpu.CompilerParams(vmem_limit_bytes=32 << 20),
        cost_estimate=takes(3),
    )(order, near, far)


def join(*values):
    return lax.optimization_barrier(values)


def add(a, b):
    return (a.astype(F32) + b.astype(F32)).astype(BF)


def swap(x, bit):
    return lax.ppermute(x, "ep", [(i, i ^ bit) for i in range(lax.axis_size("ep"))])


def turn(x, by):
    n = lax.axis_size("tp")
    return lax.ppermute(x, "tp", [(i, (i + by) % n) for i in range(n)])


def step_both(right, left, low=0, high=None):
    n = lax.axis_size("tp")
    pairs = [(i, i + 1) for i in range(low, n - 1 if high is None else high)]
    mirror = [(n - 1 - i, n - 1 - j) for i, j in pairs]
    return lax.ppermute(right, "tp", pairs), lax.ppermute(left, "tp", mirror)


def step_ends(right, left, low, high):
    n = lax.axis_size("tp")
    at = lax.axis_index("tp")
    pairs = [(i, i + 1) for i in range(low, high)]
    give = right if right is left else jnp.where((at >= low) & (at < high), right, left)
    return lax.ppermute(give, "tp", pairs + [(n - 1 - i, n - 1 - j) for i, j in pairs])


def by_side(got, low, high):
    at = lax.axis_index("tp")
    ahead = (at > low) & (at <= high)
    return jnp.where(ahead, got, 0), jnp.where(ahead, 0, got)


def gather_first(x):
    half = x.shape[0] // 2
    return swap(x[:half], 2), swap(x[half:], 4)


def gather_second(x, got):
    half = x.shape[0] // 2
    first, second = join(
        jnp.concatenate([x[:half], got[0]], axis=0), jnp.concatenate([x[half:], got[1]], axis=0)
    )
    return (first, second), (swap(first, 4), swap(second, 2))


def gather_near(held, got):
    return jnp.concatenate([held[0], got[0], held[1], got[1]], axis=0)


def gather_halves():
    n = lax.axis_size("ep")
    if n != 8:
        return [(jnp.int32(k // 2), k % 2) for k in range(2 * n)]
    at = lax.axis_index("ep").astype(jnp.int32)
    near = [(0, 0), (2, 0), (4, 0), (6, 0), (0, 1), (4, 1), (2, 1), (6, 1)]
    return [(jnp.bitwise_xor(at, k + core), half) for core in (0, 1) for k, half in near]


def gather_whole(x):
    whole = lax.all_gather(x, "ep", tiled=True)
    return whole[: whole.shape[0] // 2], whole[whole.shape[0] // 2 :]


def sum_cores(near, far):
    rows = near.shape[0] // 4
    return join(*[add(near[j * rows : (j + 1) * rows], far[j * rows : (j + 1) * rows]) for j in range(4)])


def sum_first(sums):
    return swap(sums[1], 4), swap(sums[3], 2)


def sum_second(sums, got):
    first, second = join(add(sums[0], got[0]), add(sums[2], got[1]))
    half = first.shape[0] // 2
    return (first, second), (swap(first[half:], 2), swap(second[half:], 4))


def sum_last(sums, got):
    half = sums[0].shape[0] // 2
    return jnp.concatenate([s[:half].astype(F32) + g.astype(F32) for s, g in zip(sums, got)], axis=0)


def sum_whole(near, far):
    n = lax.axis_size("ep")
    terms = jnp.concatenate([near, far], axis=0).reshape(n, -1, near.shape[1])
    return lax.psum_scatter(terms, "ep", scatter_dimension=0, tiled=False).astype(F32)


def spread(own, steps, last):
    n = lax.axis_size("tp")
    at = lax.axis_index("tp").astype(jnp.int32)
    rows, width = own.shape
    out = jnp.zeros((n * rows, width), BF)
    for t, step in enumerate(steps):
        for got, place in zip(step, (at - t - 1, at + t + 1)):
            place = jnp.where((place >= 0) & (place < n), place, at)
            out = lax.dynamic_update_slice(out, got, (place * rows, 0))
    place = jnp.where(at == n - 1, 0, jnp.where(at == 0, n - 1, at))
    out = lax.dynamic_update_slice(out, last, (place * rows, 0))
    return lax.dynamic_update_slice(out, own, (at * rows, 0))


def body(
    inputs,
    routes,
    norm_gain,
    query_weight,
    key_weight,
    value_weight,
    output_weight,
    mixer_gain,
    router_weight,
    gate_weight,
    up_weight,
    down_weight,
    cotangent,
):
    tokens, width = inputs.shape
    experts = router_weight.shape[1]
    top = routes.shape[1]
    n_ep = lax.axis_size("ep")
    n_tp = lax.axis_size("tp")
    fine = n_ep == 8
    ep_at = lax.axis_index("ep").astype(jnp.int32)
    tp_at = lax.axis_index("tp").astype(jnp.int32)
    quarter = tokens // n_tp
    heads_width = query_weight.shape[1]
    groups_width = key_weight.shape[1]

    def mine(x):
        return lax.dynamic_slice_in_dim(x, tp_at * quarter, quarter, 0)

    part = output_weight.shape[0] // n_ep
    output_part = lax.dynamic_slice_in_dim(output_weight, ep_at * part, part, 0)
    output_parts = [output_part] + [turn(output_part, -s) for s in range(1, n_tp)]

    hidden_part = gate_weight.shape[2]
    expert_part = pack(gate_weight[0], up_weight[0], down_weight[0])
    expert_parts = lax.all_gather(expert_part, "tp", tiled=True)

    routes_mine = mine(routes)
    grad_top_mine = mine(cotangent)
    named = jnp.pad(routes_mine.astype(BF), ((0, 0), (0, LANES - top)), constant_values=-1.0)
    extra = jnp.concatenate([grad_top_mine, named], axis=1)
    tables = rotary_lanes(tokens)
    qkv_weights = (query_weight, key_weight, value_weight)
    if fine:
        extra_got = gather_first(extra)
        qkv_weights, expert_part = join(qkv_weights, expert_part)
    else:
        output_part = jnp.concatenate(output_parts, axis=0)
        extra_near, extra_far = gather_whole(extra)

    *mixed, query, key, value, logs = attend(
        inputs,
        norm_gain,
        qkv_weights,
        tables,
        heads_width // HD,
        groups_width // HD,
        tp_at,
    )
    if fine:
        mixed, output_parts, extra_got = join(mixed, output_parts, extra_got)
        output_part = jnp.concatenate(output_parts, axis=0)

    router = jnp.pad(router_weight, ((0, 0), (0, LANES - experts)))

    ends = [turn(mixed[s], s) for s in (1, n_tp - 1)]
    if fine:
        output_got = gather_first(output_part)
        ends, output_got, mixed, router = join(ends, output_got, mixed, router)
        router = keep(router, 20)
    mixed = [mixed[0], ends[0]] + [turn(mixed[s], s) for s in range(2, n_tp - 1)] + [ends[1]]
    if fine:
        output_held, output_got = gather_second(output_part, output_got)
        mixed, output_held, output_got, router, extra, extra_got = join(
            mixed, output_held, output_got, router, extra, extra_got
        )
        near = gather_near(output_held, output_got)
        far = swap(near, 1)
        extra_held, extra_got = gather_second(extra, extra_got)
    else:
        near, far = gather_whole(output_part)
    halves = gather_halves()
    output_whole = jnp.zeros((n_tp, n_ep, part, width), BF)
    for j, blocks in enumerate((near, far)):
        blocks = blocks.reshape(n_ep, n_tp // 2, part, width)
        for k in range(n_ep):
            device, half = halves[j * n_ep + k]
            for u in range(n_tp // 2):
                place = (n_tp - half * (n_tp // 2) - u) % n_tp
                output_whole = lax.dynamic_update_slice(
                    output_whole, blocks[k, u][None, None], (place, device, 0, 0)
                )
    output_whole = output_whole.reshape(n_tp * heads_width, width)

    mixed_mine = jnp.concatenate(mixed, axis=1)
    branch = mul(mixed_mine, output_whole)
    inputs_mine = mine(inputs).astype(F32)
    attended = inputs_mine + branch
    inverse_two = lax.rsqrt(jnp.mean(attended * attended, axis=-1, keepdims=True) + EPS)
    unit_two = attended * inverse_two
    routed_in = (unit_two * mixer_gain).astype(BF)
    logits = mul(routed_in, router_weight)
    ids = jnp.arange(experts, dtype=jnp.int32)
    chosen = jnp.any(routes_mine[:, :, None] == ids[None, None, :], axis=1)
    logits = jnp.where(chosen, logits, MASKED)
    weights = jnp.where(chosen, jnp.exp(logits - jnp.max(logits, axis=-1, keepdims=True)), 0.0)
    gates = weights / jnp.sum(weights, axis=-1, keepdims=True)

    order = jnp.concatenate([ep_at[None], jnp.full((1,), experts, jnp.int32)])
    if fine:
        got = gather_first(routed_in)
        got, gates, router, order, extra_held, extra_got = join(
            got, gates, router, order, extra_held, extra_got
        )
        extra_near = gather_near(extra_held, extra_got)
        extra_far = swap(extra_near, 1)
        held, got = gather_second(routed_in, got)
        held, got = join(held, got)
        (near,) = join(gather_near(held, got))
        far = swap(near, 1)
    else:
        near, far = gather_whole(routed_in)
    out_near, out_far, gin_near, gin_even, gin_odd, terms = run_experts(
        order, near, far, extra_near, extra_far, router, expert_parts, top, n_tp
    )

    grad_expert = lax.psum_scatter(terms, "tp", scatter_dimension=0, tiled=True)

    if fine:
        gin_near = [gin_near[j * quarter : (j + 1) * quarter] for j in range(4)]
        other = swap(gin_odd, 1)
        gin = join(add(gin_near[1], other[:quarter]), add(gin_near[3], other[quarter:]))
        got = (swap(gin[0], 4), swap(gin[1], 2))
        out_far, gin_even, gin, gates = join(out_far, gin_even, gin, gates)
        gates = keep(gates, 20)
        gin_even = swap(gin_even, 1)
        out_far = swap(out_far, 1)
        got, out_far, gin_even, gates = join(got, out_far, gin_even, gates)
        gin = join(
            add(gin_near[0].astype(F32) + gin_even[:quarter].astype(F32), got[0]),
            add(gin_near[2].astype(F32) + gin_even[quarter:].astype(F32), got[1]),
        )
        got = [swap(g[quarter // 2 :], bit) for g, bit in zip(gin, (2, 4))]
        out = sum_cores(out_near, out_far)
        out_got = sum_first(out)
        gin, got = join(gin, got)
        grad_in = sum_last(gin, got)
    else:
        gin_far = jnp.stack([v.reshape(-1, quarter, v.shape[1]) for v in (gin_even, gin_odd)], axis=1)
        grad_in = sum_whole(gin_near, gin_far.reshape(gin_near.shape))
    grad_gates = grad_in[:, width : width + experts] + grad_in[:, width + experts : width + 2 * experts]
    inner_gate = jnp.sum(gates * grad_gates, axis=-1, keepdims=True)
    grad_logits = (gates * (grad_gates - inner_gate)).astype(BF)
    grad_routed = grad_in[:, :width] + mul(grad_logits, router_weight, NT)
    grad_top = grad_top_mine.astype(F32)
    scaled_two = grad_routed * mixer_gain
    grad_attended = grad_top + inverse_two * (
        scaled_two - unit_two * jnp.mean(scaled_two * unit_two, axis=-1, keepdims=True)
    )
    grad_branch = grad_attended.astype(BF)
    grad_mixed = mul(grad_branch, output_whole, NT).astype(BF)
    grad_mixed = [grad_mixed[:, s * heads_width : (s + 1) * heads_width] for s in range(n_tp)]

    grad_mixed, grad_branch = join(grad_mixed, grad_branch)
    grad_mixed = [grad_mixed[0]] + [turn(grad_mixed[s], -s) for s in range(1, n_tp)]
    if fine:
        out, out_got = sum_second(out, out_got)

    few = -(-(1 + experts) // n_ep)
    pad = 16 * (few // 16 + 1)
    small_rows = -(-few // 8) * 8
    grad_router = mul(routed_in, grad_logits, TN)
    grad_mixer = jnp.sum(grad_routed * unit_two, axis=0)
    small = jnp.concatenate([grad_mixer[None], grad_router.T], axis=0).astype(BF)
    small = jnp.pad(small, ((0, few * n_ep - 1 - experts), (0, 0))).reshape(n_ep, few, width)
    small = jnp.pad(small, ((0, 0), (0, pad - few), (0, 0)))
    grad_output = mul(mixed_mine, grad_branch, TN).astype(BF)
    grad_output = grad_output.reshape(n_tp, n_ep, part, width).transpose(1, 0, 2, 3)
    grad_output = jnp.concatenate([grad_output.reshape(n_ep, n_tp * part, width), small], axis=1)
    if fine:
        core, chip = lax.rem(ep_at, 2), lax.div(ep_at, 2)
        grad_output = grad_output.reshape((n_ep // 2, 2) + grad_output.shape[1:])
        other_output = lax.dynamic_index_in_dim(grad_output, 1 - core, 1, False)
        grad_output = lax.dynamic_index_in_dim(grad_output, core, 1, False)
        grad_mixed, out, out_got, other_output, grad_output = join(
            grad_mixed, out, out_got, other_output, grad_output
        )
        out = sum_last(out, out_got)
        other_output = swap(other_output, 1)
    else:
        out = sum_whole(out_near, out_far)
    result_mine = (attended + out).astype(BF)

    result_mine, grad_mixed = join(result_mine, grad_mixed)
    result_steps = [step_both(result_mine, result_mine)]
    *blocks, grad_qkv, end_block = attend_back(grad_mixed, query, key, value, logs, tables, qkv_weights, tp_at)
    if fine:
        blocks, grad_qkv, end_block, result_steps[0], other_output, grad_expert, inputs = join(
            blocks, grad_qkv, end_block, result_steps[0], other_output, grad_expert, inputs
        )
    else:
        blocks, grad_qkv, end_block, result_steps[0] = join(blocks, grad_qkv, end_block, result_steps[0])

    inputs32 = inputs.astype(F32)
    normed = inputs32 * lax.rsqrt(jnp.mean(inputs32 * inputs32, axis=-1, keepdims=True) + EPS)
    normed = (normed * norm_gain).astype(BF)
    grad_qkv_w = mul(normed, grad_qkv, TN).astype(BF)

    def chip_halves(half, *places):
        rows = grad_output.shape[1] // 2
        picked = []
        for j in places:
            chip_at = (jnp.bitwise_xor(chip, j), half * rows, 0)
            size = (1, rows, width)
            picked.append(
                add(
                    lax.dynamic_slice(grad_output, chip_at, size)[0],
                    lax.dynamic_slice(other_output, chip_at, size)[0],
                )
            )
        return jnp.concatenate(picked, axis=0)

    if fine:
        got = join(chip_halves(0, 2, 3), chip_halves(1, 1, 3))
        got = (swap(got[0], 4), swap(got[1], 2))
    result_steps.append(step_both(*result_steps[-1], 1))
    sent = step_ends(end_block, end_block, 0, 1)
    if fine:
        sent, result_steps[-1], got, grad_qkv_w = join(sent, result_steps[-1], got, grad_qkv_w)
        sums, got = sum_second((chip_halves(0, 0, 1), None, chip_halves(1, 0, 2)), got)
    else:
        sent, result_steps[-1], grad_qkv_w, grad_expert = join(
            sent, result_steps[-1], grad_qkv_w, grad_expert
        )
    grad_qkv_w = lax.psum(grad_qkv_w, "ep")
    sent = by_side(sent, 0, 1)
    result_last = None
    for t in range(2, n_tp):
        sent = step_both(add(blocks[n_tp - t], sent[0]), add(blocks[t], sent[1]), 0, t)
        if t < n_tp - 1:
            result_last = step_ends(*result_steps[-1], t, n_tp - 1)
            if fine:
                sent, result_last, got, sums = join(sent, result_last, got, sums)
                grad_output = sum_last(sums, got).astype(BF)
            else:
                sent, result_last = join(sent, result_last)
                grad_output = lax.psum_scatter(grad_output, "ep", scatter_dimension=0, tiled=False)
            pieces = [
                jnp.concatenate([grad_output[s * part : (s + 1) * part], grad_output[n_tp * part :][:small_rows]], axis=0)
                for s in range(n_tp)
            ]
    got = [turn(pieces[s], -s) for s in range(1, n_tp)]
    sent, result_steps, result_last = join(sent, result_steps, result_last)
    grad_normed = blocks[0].astype(F32) + sent[0].astype(F32) + sent[1].astype(F32)
    inputs_mine = mine(inputs).astype(F32)
    inverse_one = lax.rsqrt(jnp.mean(inputs_mine * inputs_mine, axis=-1, keepdims=True) + EPS)
    unit_one = inputs_mine * inverse_one
    scaled_one = grad_normed * norm_gain
    grad_inputs = grad_attended + inverse_one * (
        scaled_one - unit_one * jnp.mean(scaled_one * unit_one, axis=-1, keepdims=True)
    )
    grad_inputs = grad_inputs.astype(BF)
    grad_norm = jnp.sum(grad_normed * unit_one, axis=0)
    used = -(-(part + small_rows + 1) // 32) * 32

    grad_inputs, grad_norm = join(grad_inputs, grad_norm)
    input_steps = [step_both(grad_inputs, grad_inputs)]
    grad_norm = grad_norm[None]
    norm_got = [turn(grad_norm, s) for s in range(1, n_tp)]
    got, norm_got, input_steps[0] = join(got, norm_got, input_steps[0])
    grad_norm = (grad_norm + sum(norm_got))[0]
    grad_output = (pieces[0].astype(F32) + sum(v.astype(F32) for v in got)).astype(BF)
    grad_output = jnp.pad(grad_output, ((0, used - grad_output.shape[0]), (0, 0)))
    grad_output = grad_output.at[used - 1].set(grad_norm.astype(BF))
    if fine:
        got = [swap(grad_output, k) for k in (2, 4, 6)]
    grad_expert = grad_expert.reshape(3, -1, width).astype(F32)
    grad_gate_w, grad_up_w, grad_down_w = grad_expert[0].T, grad_expert[1].T, grad_expert[2]
    for t in range(1, n_tp - 2):
        input_steps.append(step_both(*input_steps[-1], t))
    if fine:
        got, input_steps[-1], grad_gate_w, grad_up_w, grad_down_w = join(
            got, input_steps[-1], grad_gate_w, grad_up_w, grad_down_w
        )
        near = jnp.concatenate([grad_output] + got, axis=0)
        far = swap(near, 1)
        far, grad_qkv_w = join(far, grad_qkv_w)
        devices = jnp.stack([jnp.bitwise_xor(ep_at, jnp.int32(k)) for k in (0, 2, 4, 6, 1, 3, 5, 7)])
        grad_output, small, grad_norm = set_rows(devices, near, far, part, small_rows)
        small = small.reshape(n_ep, small_rows, width)
        grad_norm = grad_norm[0]
    else:
        gathered = lax.all_gather(grad_output, "ep")
        small = gathered[:, part : part + small_rows].astype(F32)
        grad_norm = jnp.sum(gathered[:, used - 1].astype(F32), axis=0)
        grad_output = gathered[:, :part].reshape(heads_width, width).astype(F32)
    small = small[:, :few].reshape(n_ep * few, width)[: 1 + experts]
    result = spread(result_mine, result_steps, result_last)
    input_last = step_ends(*input_steps[-1], n_tp - 2, n_tp - 1)
    grad_qkv_w = grad_qkv_w.astype(F32)
    qkv_grads = (
        grad_qkv_w[:, :heads_width],
        grad_qkv_w[:, heads_width : heads_width + groups_width],
        grad_qkv_w[:, heads_width + groups_width :],
    )
    grad_norm, small, grad_output, input_last, qkv_grads, result = join(
        grad_norm, small, grad_output, input_last, qkv_grads, result
    )
    grad_inputs = spread(grad_inputs, input_steps, input_last)
    return (
        result,
        grad_inputs,
        grad_norm,
        *qkv_grads,
        grad_output,
        small[0],
        small[1:].T,
        grad_gate_w[None],
        grad_up_w[None],
        grad_down_w[None],
    )


def solution(mesh):
    placed = (
        P("ep", None),
        P("ep", None),
        P(),
        P(None, "tp"),
        P(None, "tp"),
        P(None, "tp"),
        P("tp", None),
        P(),
        P(),
        P("ep", None, "tp"),
        P("ep", None, "tp"),
        P("ep", "tp", None),
        P("ep", None),
    )
    return jax.shard_map(
        body,
        mesh=mesh,
        in_specs=placed,
        out_specs=(
            P("ep", None),
            P("ep", None),
            P(),
            P(None, "tp"),
            P(None, "tp"),
            P(None, "tp"),
            P("tp", None),
            P(),
            P(),
            P("ep", None, "tp"),
            P("ep", None, "tp"),
            P("ep", "tp", None),
        ),
        check_vma=False,
    )
```

```python
import functools

import jax
import jax.numpy as jnp
import numpy as np
from jax import lax
from jax.experimental import pallas as pl
from jax.experimental.pallas import tpu as pltpu
from jax.sharding import PartitionSpec as P

HD = 64
LEN = 1024
EPS = 1e-06
MASKED = -1e30
BF = jnp.bfloat16
F32 = jnp.float32
BLOCK = 256
LANES = 128
NT = (((1,), (1,)), ((), ()))
TN = (((0,), (0,)), ((), ()))


def takes(us):
    return pl.CostEstimate(flops=int(us * 1.15e9), bytes_accessed=0, transcendentals=0)


def mul(a, b, dims=(((1,), (0,)), ((), ()))):
    return lax.dot_general(a, b, dims, preferred_element_type=F32)


def rotate_lanes(y, cos, sin):
    half = HD // 2
    first = lax.broadcasted_iota(jnp.int32, y.shape, 1) % HD < half
    return y * cos + jnp.where(first, pltpu.roll(y, 128 - half, 1), pltpu.roll(y, half, 1)) * sin


def rotary_lanes(tokens):
    lane = np.arange(128)
    freqs = np.float32(10000.0) ** (-(lane % (HD // 2)).astype(np.float32) * np.float32(2.0 / HD))
    angles = (np.arange(tokens) % LEN).astype(np.float32)[:, None] * freqs[None, :].astype(np.float32)
    sign = np.where(lane % HD < HD // 2, np.float32(-1.0), np.float32(1.0))
    return jnp.asarray(np.cos(angles), F32), jnp.asarray(np.sin(angles) * sign, F32)


def causal(block):
    key_at = lax.broadcasted_iota(jnp.int32, (block, block), 0)
    query_at = lax.broadcasted_iota(jnp.int32, (block, block), 1)
    return key_at <= query_at


def attend_kernel(at_ref, x_ref, gain_ref, wq_ref, wk_ref, wv_ref, cos_ref, sin_ref, *refs):
    pieces, (q_ref, k_ref, v_ref, log_ref, w_ref, vt_ref, out_ref) = refs[:-7], refs[-7:]
    tokens = x_ref.shape[0]
    heads, groups = q_ref.shape[0], k_ref.shape[0]
    repeat = heads // groups
    per = 128 // HD
    scale = HD ** (-0.5)
    w_ref[...] = jnp.concatenate([wq_ref[...], wk_ref[...], wv_ref[...]], axis=1)

    @pl.loop(0, tokens // BLOCK)
    def _(i):
        at = pl.multiple_of(i * BLOCK, BLOCK)
        rows = pl.ds(at, BLOCK)
        x = x_ref[rows, :].astype(F32)
        inverse = lax.rsqrt(jnp.mean(x * x, axis=-1, keepdims=True) + EPS)
        normed = (x * inverse * gain_ref[...]).astype(BF)
        raw = mul(normed, w_ref[...])
        tables = (cos_ref[rows, :], sin_ref[rows, :])
        for h in range(0, heads, per):
            turned = rotate_lanes(raw[:, h * HD : h * HD + 128], *tables) * scale
            for u in range(per):
                q_ref[h + u, rows, :] = turned[:, u * HD : (u + 1) * HD].astype(BF)
        for g in range(0, groups, per):
            lane = (heads + g) * HD
            turned = rotate_lanes(raw[:, lane : lane + 128], *tables)
            lane = (heads + groups + g) * HD
            value = raw[:, lane : lane + 128]
            turned_value = value.T
            for u in range(per):
                k_ref[g + u, rows, :] = turned[:, u * HD : (u + 1) * HD].astype(BF)
                v_ref[g + u, rows, :] = value[:, u * HD : (u + 1) * HD].astype(BF)
                vt_ref[g + u, :, rows] = turned_value[u * HD : (u + 1) * HD].astype(BF)

    keep = causal(BLOCK)

    @pl.loop(0, heads)
    def _(h):
        g = h // repeat
        for i in range(tokens // BLOCK):
            start, stop = i * BLOCK, (i + 1) * BLOCK
            query = q_ref[h, start:stop, :]
            parts = [jnp.where(keep, mul(k_ref[g, start:stop, :], query, NT), MASKED)]
            if i:
                parts.append(mul(k_ref[g, :start, :], query, NT))
            peak = jnp.max(parts[0], axis=0, keepdims=True)
            for part in parts[1:]:
                peak = jnp.maximum(peak, jnp.max(part, axis=0, keepdims=True))
            weights = [jnp.exp(part - peak) for part in parts]
            total = sum(jnp.sum(w, axis=0, keepdims=True) for w in weights)
            shrink = 1.0 / total
            mixed = mul(vt_ref[g, :, start:stop], weights[0].astype(BF))
            if i:
                mixed += mul(vt_ref[g, :, :start], weights[1].astype(BF))
            out_ref[h, :, start:stop] = mixed * shrink
            log_ref[h, :, start:stop] = peak + jnp.log(total)

    for s, piece_ref in enumerate(pieces):
        span = pl.ds(pl.multiple_of(lax.rem(at_ref[0] + s, len(pieces)) * BLOCK, BLOCK), BLOCK)
        for h in range(0, heads, per):
            pair = jnp.concatenate([out_ref[h + u, :, span] for u in range(per)], axis=0)
            piece_ref[:, h * HD : h * HD + 128] = pair.T.astype(BF)


VMEM = pl.BlockSpec(memory_space=pltpu.VMEM)
SMEM = pl.BlockSpec(memory_space=pltpu.SMEM)


def attend(x, gain, weights, tables, heads, groups, at):
    tokens, width = x.shape
    count = tokens // BLOCK
    return pl.pallas_call(
        attend_kernel,
        in_specs=[SMEM] + [VMEM] * 7,
        out_shape=[jax.ShapeDtypeStruct((BLOCK, heads * HD), BF)] * count
        + [
            jax.ShapeDtypeStruct((heads, tokens, HD), BF),
            jax.ShapeDtypeStruct((groups, tokens, HD), BF),
            jax.ShapeDtypeStruct((groups, tokens, HD), BF),
            jax.ShapeDtypeStruct((heads, 1, tokens), F32),
        ],
        scratch_shapes=[
            pltpu.VMEM((width, (heads + 2 * groups) * HD), BF),
            pltpu.VMEM((groups, HD, tokens), BF),
            pltpu.VMEM((heads, HD, tokens), F32),
        ],
        compiler_params=pltpu.CompilerParams(vmem_limit_bytes=48 << 20),
        cost_estimate=takes(20),
    )(at[None], x, gain[None], *weights, *tables)


def attend_back_kernel(at_ref, q_ref, k_ref, v_ref, log_ref, cos_ref, sin_ref, wq_ref, wk_ref, wv_ref, *refs):
    w_ref, do_ref, kt_ref, dq_ref, dk_ref, dv_ref = refs[-6:]
    out_ref, end_ref = refs[-8:-6]
    count = (len(refs) - 8) // 2
    grad_refs, block_refs = refs[:count], refs[count:-8]
    tokens = q_ref.shape[1]
    heads, groups = q_ref.shape[0], k_ref.shape[0]
    repeat = heads // groups
    per = 128 // HD
    scale = HD ** (-0.5)
    w_ref[...] = jnp.concatenate([wq_ref[...], wk_ref[...], wv_ref[...]], axis=1)
    dk_ref[...] = jnp.zeros_like(dk_ref)
    dv_ref[...] = jnp.zeros_like(dv_ref)

    def span_of(s):
        return pl.ds(pl.multiple_of(lax.rem(at_ref[0] + s, count) * BLOCK, BLOCK), BLOCK)

    for s, grad_ref in enumerate(grad_refs):
        for h in range(heads):
            do_ref[h, span_of(s), :] = grad_ref[:, h * HD : (h + 1) * HD]

    @pl.loop(0, tokens // BLOCK)
    def _(i):
        rows = pl.ds(pl.multiple_of(i * BLOCK, BLOCK), BLOCK)
        for g in range(groups):
            kt_ref[g, :, rows] = k_ref[g, rows, :].astype(F32).T.astype(BF)

    keep = causal(BLOCK)

    @pl.loop(0, heads)
    def _(h):
        g = h // repeat
        for i in range(tokens // BLOCK):
            start, stop = i * BLOCK, (i + 1) * BLOCK
            query = q_ref[h, start:stop, :]
            grads = do_ref[h, start:stop, :]
            log_total = log_ref[h, :, start:stop]
            spans = [(start, stop)] + ([(0, start)] if i else [])
            probs, grad_probs = [], []
            for lo, hi in spans:
                scores = mul(k_ref[g, lo:hi, :], query, NT)
                if hi == stop:
                    scores = jnp.where(keep, scores, MASKED)
                probs.append(jnp.exp(scores - log_total))
                grad_probs.append(mul(v_ref[g, lo:hi, :], grads, NT))
            inner = sum(jnp.sum(p * d, axis=0, keepdims=True) for p, d in zip(probs, grad_probs))
            dq = None
            for (lo, hi), p, d in zip(spans, probs, grad_probs):
                ds = (p * (d - inner)).astype(BF)
                dk_ref[g, lo:hi, :] += mul(ds, query)
                dv_ref[g, lo:hi, :] += mul(p.astype(BF), grads)
                term = mul(kt_ref[g, :, lo:hi], ds)
                dq = term if dq is None else dq + term
            dq_ref[h, :, start:stop] = dq * scale

    @pl.loop(0, tokens // BLOCK)
    def _(i):
        rows = pl.ds(pl.multiple_of(i * BLOCK, BLOCK), BLOCK)
        tables = (cos_ref[rows, :], -sin_ref[rows, :])
        for h in range(0, heads, per):
            pair = jnp.concatenate([dq_ref[h + u, :, rows] for u in range(per)], axis=0).T
            out_ref[rows, h * HD : h * HD + 128] = rotate_lanes(pair, *tables).astype(BF)
        for g in range(0, groups, per):
            pair = jnp.concatenate([dk_ref[g + u, rows, :] for u in range(per)], axis=1)
            lane = (heads + g) * HD
            out_ref[rows, lane : lane + 128] = rotate_lanes(pair, *tables).astype(BF)
            pair = jnp.concatenate([dv_ref[g + u, rows, :] for u in range(per)], axis=1)
            lane = (heads + groups + g) * HD
            out_ref[rows, lane : lane + 128] = pair.astype(BF)


    for s, block_ref in enumerate(block_refs):
        block_ref[...] = mul(out_ref[span_of(s), :], w_ref[...], NT).astype(BF)

    @pl.when(at_ref[0] < count // 2)
    def _():
        end_ref[...] = block_refs[count - 1][...]

    @pl.when(at_ref[0] >= count // 2)
    def _():
        end_ref[...] = block_refs[1][...]


def attend_back(grad_pieces, q, k, v, logs, tables, weights, at):
    heads, tokens, _ = q.shape
    groups = k.shape[0]
    count = len(grad_pieces)
    lanes = (heads + 2 * groups) * HD
    width = weights[0].shape[0]
    block = jax.ShapeDtypeStruct((BLOCK, width), BF)
    return pl.pallas_call(
        attend_back_kernel,
        in_specs=[SMEM] + [VMEM] * (9 + count),
        out_shape=[block] * count + [jax.ShapeDtypeStruct((tokens, lanes), BF), block],
        scratch_shapes=[
            pltpu.VMEM((width, lanes), BF),
            pltpu.VMEM((heads, tokens, HD), BF),
            pltpu.VMEM((groups, HD, tokens), BF),
            pltpu.VMEM((heads, HD, tokens), F32),
            pltpu.VMEM((groups, tokens, HD), F32),
            pltpu.VMEM((groups, tokens, HD), F32),
        ],
        compiler_params=pltpu.CompilerParams(vmem_limit_bytes=48 << 20),
        cost_estimate=takes(20),
    )(at[None], q, k, v, logs, *tables, *weights, *grad_pieces)


def pack_kernel(gate_ref, up_ref, down_ref, out_ref):
    part = down_ref.shape[0]
    out_ref[:part, :] = gate_ref[...].astype(F32).T.astype(BF)
    out_ref[part : 2 * part, :] = up_ref[...].astype(F32).T.astype(BF)
    out_ref[2 * part :, :] = down_ref[...]


def pack(gate, up, down):
    return pl.pallas_call(
        pack_kernel,
        out_shape=jax.ShapeDtypeStruct((3 * down.shape[0], down.shape[1]), BF),
        compiler_params=pltpu.CompilerParams(vmem_limit_bytes=32 << 20),
        cost_estimate=takes(3),
    )(gate, up, down)


def expert_kernel(order_ref, near_ref, far_ref, extra_near_ref, extra_far_ref, router_ref, parts_ref, *refs, top, count):
    out_refs, gin_refs, terms_ref = refs[:2], refs[2:5], refs[5]
    weights_ref, sums_ref = refs[6:]
    step = pl.program_id(0)
    steps = pl.num_programs(0)
    hidden_width, width = weights_ref.shape[0] // 3, weights_ref.shape[1]
    gate_up = slice(0, 2 * hidden_width)
    down = slice(2 * hidden_width, 3 * hidden_width)
    own = order_ref[0]
    experts = order_ref[1]
    part = hidden_width // count
    spans = [
        (pl.ds((3 * s + j) * part, part), pl.ds(j * hidden_width + s * part, part))
        for s in range(count)
        for j in range(3)
    ]

    @pl.when(step == 0)
    def _():
        sums_ref[...] = jnp.zeros_like(sums_ref)
        for there, here in spans:
            weights_ref[here, :] = parts_ref[there, :]

    near = step < steps // 2
    rows = jnp.where(near, near_ref[...], far_ref[...])
    extra = jnp.where(near, extra_near_ref[...], extra_far_ref[...])
    grads32 = extra[:, :width].astype(F32)
    named = extra[:, width:].astype(F32)

    lane = lax.broadcasted_iota(jnp.int32, (rows.shape[0], LANES), 1)
    lane32 = lane.astype(F32)
    chosen = lane32 == named[:, 0:1]
    for k in range(1, top):
        chosen = chosen | (lane32 == named[:, k : k + 1])
    logits = jnp.where(chosen, mul(rows, router_ref[...]), MASKED)
    weights = jnp.where(chosen, jnp.exp(logits - jnp.max(logits, axis=-1, keepdims=True)), 0.0)
    mine = jnp.sum(jnp.where(lane == own, weights, 0.0), axis=-1, keepdims=True)
    gate = mine / jnp.sum(weights, axis=-1, keepdims=True)

    both = mul(rows, weights_ref[gate_up, :], NT)
    gate_vals = both[:, :hidden_width]
    up_vals = both[:, hidden_width:]
    sigma = jax.nn.sigmoid(gate_vals)
    active = gate_vals * sigma
    hidden = (active * up_vals).astype(BF)
    grad_out = (gate * grads32).astype(BF)
    grad_hidden = mul(grad_out, weights_ref[down, :], NT)
    expert_out = mul(hidden, weights_ref[down, :])
    combined = (gate * expert_out).astype(BF)
    score = jnp.sum(grads32 * expert_out, axis=-1, keepdims=True)
    high = score.astype(BF).astype(F32)
    scores = jnp.where(lane == own, high, jnp.where(lane == own + experts, score - high, 0.0)).astype(BF)
    grad_gate_vals = (grad_hidden * up_vals * sigma * (1.0 + gate_vals * (1.0 - sigma))).astype(BF)
    grad_up_vals = (grad_hidden * active).astype(BF)
    grad_both = jnp.concatenate([grad_gate_vals, grad_up_vals], axis=1)
    grad_in = mul(grad_both, weights_ref[gate_up, :]).astype(BF)
    sums_ref[gate_up, :] += mul(grad_both, rows, TN)
    sums_ref[down, :] += mul(hidden, grad_out, TN)
    far_step = step - steps // 2
    for k, now in enumerate((near, jnp.logical_not(near))):

        @pl.when(now)
        def _():
            out_refs[k][...] = combined

    even = lax.rem(step, 2) == 0
    for k, now in enumerate((near, (far_step >= 0) & even, (far_step >= 0) & jnp.logical_not(even))):

        @pl.when(now)
        def _():
            gin_refs[k][:, :width] = grad_in
            gin_refs[k][:, width:] = scores

    @pl.when(step == steps - 1)
    def _():
        for there, here in spans:
            terms_ref[there, :] = sums_ref[here, :].astype(BF)


def run_experts(order, near, far, extra_near, extra_far, router, parts, top, count):
    total, width = 2 * near.shape[0], near.shape[1]
    steps = total // BLOCK
    half_steps = steps // 2
    wide = extra_near.shape[1]
    hidden = parts.shape[0] // 3

    def by_set(lanes):
        return [
            pl.BlockSpec((BLOCK, lanes), lambda i, o: (jnp.minimum(i, half_steps - 1), 0)),
            pl.BlockSpec((BLOCK, lanes), lambda i, o: (jnp.maximum(i - half_steps, 0), 0)),
        ]

    half = by_set(width)
    far_pair = pl.BlockSpec((BLOCK, wide), lambda i, o: (jnp.maximum(i - half_steps, 0) // 2, 0))
    half_wide = [by_set(wide)[0], far_pair, far_pair]
    whole = pl.BlockSpec((3 * hidden, width), lambda i, o: (0, 0), pipeline_mode=pl.Buffered(1))
    return pl.pallas_call(
        functools.partial(expert_kernel, top=top, count=count),
        grid_spec=pltpu.PrefetchScalarGridSpec(
            num_scalar_prefetch=1,
            grid=(steps,),
            in_specs=[
                *by_set(width),
                *by_set(wide),
                pl.BlockSpec((width, LANES), lambda i, o: (0, 0)),
                whole,
            ],
            out_specs=half + half_wide + [whole],
            scratch_shapes=[
                pltpu.VMEM((3 * hidden, width), BF),
                pltpu.VMEM((3 * hidden, width), F32),
            ],
        ),
        out_shape=[jax.ShapeDtypeStruct((total // 2, width), BF)] * 2
        + [jax.ShapeDtypeStruct((total // 2, wide), BF)]
        + [jax.ShapeDtypeStruct((total // 4, wide), BF)] * 2
        + [jax.ShapeDtypeStruct((3 * hidden, width), BF)],
        compiler_params=pltpu.CompilerParams(vmem_limit_bytes=58 << 20),
        cost_estimate=takes(5 * steps),
    )(order, near, far, extra_near, extra_far, router, parts)


def keep_kernel(x_ref, out_ref):
    out_ref[...] = x_ref[...]


def keep(x, us):
    return pl.pallas_call(
        keep_kernel, out_shape=jax.ShapeDtypeStruct(x.shape, x.dtype), cost_estimate=takes(us)
    )(x)


def set_rows_kernel(order_ref, near_ref, far_ref, out_ref, small_ref, norm_ref, *, part, few_rows):
    rows, width = near_ref.shape[0] // 4, near_ref.shape[1]
    norm = jnp.zeros((1, width), F32)
    for k in range(8):
        source = near_ref if k < 4 else far_ref
        block = source[(k % 4) * rows : (k % 4 + 1) * rows, :].astype(F32)
        device = order_ref[k]
        out_ref[pl.ds(pl.multiple_of(device * part, 8), part), :] = block[:part]
        small_ref[pl.ds(pl.multiple_of(device * few_rows, 8), few_rows), :] = block[part : part + few_rows]
        norm += block[rows - 1 :]
    norm_ref[...] = norm


def set_rows(order, near, far, part, few_rows):
    width = near.shape[1]
    return pl.pallas_call(
        functools.partial(set_rows_kernel, part=part, few_rows=few_rows),
        in_specs=[SMEM, VMEM, VMEM],
        out_shape=[
            jax.ShapeDtypeStruct((8 * part, width), F32),
            jax.ShapeDtypeStruct((8 * few_rows, width), F32),
            jax.ShapeDtypeStruct((1, width), F32),
        ],
        compiler_params=pltpu.CompilerParams(vmem_limit_bytes=32 << 20),
        cost_estimate=takes(3),
    )(order, near, far)


def join(*values):
    return lax.optimization_barrier(values)


def add(a, b):
    return (a.astype(F32) + b.astype(F32)).astype(BF)


def swap(x, bit):
    return lax.ppermute(x, "ep", [(i, i ^ bit) for i in range(lax.axis_size("ep"))])


def turn(x, by):
    n = lax.axis_size("tp")
    return lax.ppermute(x, "tp", [(i, (i + by) % n) for i in range(n)])


def step_both(right, left, low=0, high=None):
    n = lax.axis_size("tp")
    pairs = [(i, i + 1) for i in range(low, n - 1 if high is None else high)]
    mirror = [(n - 1 - i, n - 1 - j) for i, j in pairs]
    return lax.ppermute(right, "tp", pairs), lax.ppermute(left, "tp", mirror)


def step_ends(right, left, low, high):
    n = lax.axis_size("tp")
    at = lax.axis_index("tp")
    pairs = [(i, i + 1) for i in range(low, high)]
    give = right if right is left else jnp.where((at >= low) & (at < high), right, left)
    return lax.ppermute(give, "tp", pairs + [(n - 1 - i, n - 1 - j) for i, j in pairs])


def by_side(got, low, high):
    at = lax.axis_index("tp")
    ahead = (at > low) & (at <= high)
    return jnp.where(ahead, got, 0), jnp.where(ahead, 0, got)


def gather_first(x):
    half = x.shape[0] // 2
    return swap(x[:half], 2), swap(x[half:], 4)


def gather_second(x, got):
    half = x.shape[0] // 2
    first, second = join(
        jnp.concatenate([x[:half], got[0]], axis=0), jnp.concatenate([x[half:], got[1]], axis=0)
    )
    return (first, second), (swap(first, 4), swap(second, 2))


def gather_near(held, got):
    return jnp.concatenate([held[0], got[0], held[1], got[1]], axis=0)


def gather_halves():
    n = lax.axis_size("ep")
    if n != 8:
        return [(jnp.int32(k // 2), k % 2) for k in range(2 * n)]
    at = lax.axis_index("ep").astype(jnp.int32)
    near = [(0, 0), (2, 0), (4, 0), (6, 0), (0, 1), (4, 1), (2, 1), (6, 1)]
    return [(jnp.bitwise_xor(at, k + core), half) for core in (0, 1) for k, half in near]


def gather_whole(x):
    whole = lax.all_gather(x, "ep", tiled=True)
    return whole[: whole.shape[0] // 2], whole[whole.shape[0] // 2 :]


def sum_cores(near, far):
    rows = near.shape[0] // 4
    return join(*[add(near[j * rows : (j + 1) * rows], far[j * rows : (j + 1) * rows]) for j in range(4)])


def sum_first(sums):
    return swap(sums[1], 4), swap(sums[3], 2)


def sum_second(sums, got):
    first, second = join(add(sums[0], got[0]), add(sums[2], got[1]))
    half = first.shape[0] // 2
    return (first, second), (swap(first[half:], 2), swap(second[half:], 4))


def sum_last(sums, got):
    half = sums[0].shape[0] // 2
    return jnp.concatenate([s[:half].astype(F32) + g.astype(F32) for s, g in zip(sums, got)], axis=0)


def sum_whole(near, far):
    n = lax.axis_size("ep")
    terms = jnp.concatenate([near, far], axis=0).reshape(n, -1, near.shape[1])
    return lax.psum_scatter(terms, "ep", scatter_dimension=0, tiled=False).astype(F32)


def spread(own, steps, last):
    n = lax.axis_size("tp")
    at = lax.axis_index("tp").astype(jnp.int32)
    rows, width = own.shape
    out = jnp.zeros((n * rows, width), BF)
    for t, step in enumerate(steps):
        for got, place in zip(step, (at - t - 1, at + t + 1)):
            place = jnp.where((place >= 0) & (place < n), place, at)
            out = lax.dynamic_update_slice(out, got, (place * rows, 0))
    place = jnp.where(at == n - 1, 0, jnp.where(at == 0, n - 1, at))
    out = lax.dynamic_update_slice(out, last, (place * rows, 0))
    return lax.dynamic_update_slice(out, own, (at * rows, 0))


def body(
    inputs,
    routes,
    norm_gain,
    query_weight,
    key_weight,
    value_weight,
    output_weight,
    mixer_gain,
    router_weight,
    gate_weight,
    up_weight,
    down_weight,
    cotangent,
):
    tokens, width = inputs.shape
    experts = router_weight.shape[1]
    top = routes.shape[1]
    n_ep = lax.axis_size("ep")
    n_tp = lax.axis_size("tp")
    fine = n_ep == 8
    ep_at = lax.axis_index("ep").astype(jnp.int32)
    tp_at = lax.axis_index("tp").astype(jnp.int32)
    quarter = tokens // n_tp
    heads_width = query_weight.shape[1]
    groups_width = key_weight.shape[1]

    def mine(x):
        return lax.dynamic_slice_in_dim(x, tp_at * quarter, quarter, 0)

    part = output_weight.shape[0] // n_ep
    output_part = lax.dynamic_slice_in_dim(output_weight, ep_at * part, part, 0)
    output_parts = [output_part] + [turn(output_part, -s) for s in range(1, n_tp)]

    hidden_part = gate_weight.shape[2]
    expert_part = pack(gate_weight[0], up_weight[0], down_weight[0])
    expert_parts = lax.all_gather(expert_part, "tp", tiled=True)

    routes_mine = mine(routes)
    grad_top_mine = mine(cotangent)
    named = jnp.pad(routes_mine.astype(BF), ((0, 0), (0, LANES - top)), constant_values=-1.0)
    extra = jnp.concatenate([grad_top_mine, named], axis=1)
    tables = rotary_lanes(tokens)
    qkv_weights = (query_weight, key_weight, value_weight)
    if fine:
        extra_got = gather_first(extra)
        qkv_weights, expert_part = join(qkv_weights, expert_part)
    else:
        output_part = jnp.concatenate(output_parts, axis=0)
        extra_near, extra_far = gather_whole(extra)

    *mixed, query, key, value, logs = attend(
        inputs,
        norm_gain,
        qkv_weights,
        tables,
        heads_width // HD,
        groups_width // HD,
        tp_at,
    )
    if fine:
        mixed, output_parts, extra_got = join(mixed, output_parts, extra_got)
        output_part = jnp.concatenate(output_parts, axis=0)

    router = jnp.pad(router_weight, ((0, 0), (0, LANES - experts)))

    ends = [turn(mixed[s], s) for s in (1, n_tp - 1)]
    if fine:
        output_got = gather_first(output_part)
        ends, output_got, mixed, router = join(ends, output_got, mixed, router)
        router = keep(router, 20)
    mixed = [mixed[0], ends[0]] + [turn(mixed[s], s) for s in range(2, n_tp - 1)] + [ends[1]]
    if fine:
        output_held, output_got = gather_second(output_part, output_got)
        mixed, output_held, output_got, router, extra, extra_got = join(
            mixed, output_held, output_got, router, extra, extra_got
        )
        (near,) = join(gather_near(output_held, output_got))
        far = swap(near, 1)
        extra_held, extra_got = gather_second(extra, extra_got)
    else:
        near, far = gather_whole(output_part)
    halves = gather_halves()
    output_whole = jnp.zeros((n_tp, n_ep, part, width), BF)
    for j, blocks in enumerate((near, far)):
        blocks = blocks.reshape(n_ep, n_tp // 2, part, width)
        for k in range(n_ep):
            device, half = halves[j * n_ep + k]
            for u in range(n_tp // 2):
                place = (n_tp - half * (n_tp // 2) - u) % n_tp
                output_whole = lax.dynamic_update_slice(
                    output_whole, blocks[k, u][None, None], (place, device, 0, 0)
                )
    output_whole = output_whole.reshape(n_tp * heads_width, width)

    mixed_mine = jnp.concatenate(mixed, axis=1)
    branch = mul(mixed_mine, output_whole)
    inputs_mine = mine(inputs).astype(F32)
    attended = inputs_mine + branch
    inverse_two = lax.rsqrt(jnp.mean(attended * attended, axis=-1, keepdims=True) + EPS)
    unit_two = attended * inverse_two
    routed_in = (unit_two * mixer_gain).astype(BF)
    logits = mul(routed_in, router_weight)
    ids = jnp.arange(experts, dtype=jnp.int32)
    chosen = jnp.any(routes_mine[:, :, None] == ids[None, None, :], axis=1)
    logits = jnp.where(chosen, logits, MASKED)
    weights = jnp.where(chosen, jnp.exp(logits - jnp.max(logits, axis=-1, keepdims=True)), 0.0)
    gates = weights / jnp.sum(weights, axis=-1, keepdims=True)

    order = jnp.concatenate([ep_at[None], jnp.full((1,), experts, jnp.int32)])
    if fine:
        got = gather_first(routed_in)
        got, gates, router, order, extra_held, extra_got = join(
            got, gates, router, order, extra_held, extra_got
        )
        (extra_near,) = join(gather_near(extra_held, extra_got))
        extra_far = swap(extra_near, 1)
        held, got = gather_second(routed_in, got)
        held, got = join(held, got)
        (near,) = join(gather_near(held, got))
        far = swap(near, 1)
    else:
        near, far = gather_whole(routed_in)
    out_near, out_far, gin_near, gin_even, gin_odd, terms = run_experts(
        order, near, far, extra_near, extra_far, router, expert_parts, top, n_tp
    )

    grad_expert = lax.psum_scatter(terms, "tp", scatter_dimension=0, tiled=True)

    if fine:
        gin_near = [gin_near[j * quarter : (j + 1) * quarter] for j in range(4)]
        other = swap(gin_odd, 1)
        gin = join(add(gin_near[1], other[:quarter]), add(gin_near[3], other[quarter:]))
        got = (swap(gin[0], 4), swap(gin[1], 2))
        out_far, gin_even, gin, gates = join(out_far, gin_even, gin, gates)
        gates = keep(gates, 20)
        gin_even = swap(gin_even, 1)
        out_far = swap(out_far, 1)
        got, out_far, gin_even, gates = join(got, out_far, gin_even, gates)
        gin = join(
            add(gin_near[0].astype(F32) + gin_even[:quarter].astype(F32), got[0]),
            add(gin_near[2].astype(F32) + gin_even[quarter:].astype(F32), got[1]),
        )
        got = [swap(g[quarter // 2 :], bit) for g, bit in zip(gin, (2, 4))]
        out = sum_cores(out_near, out_far)
        out_got = sum_first(out)
        gin, got = join(gin, got)
        grad_in = sum_last(gin, got)
    else:
        gin_far = jnp.stack([v.reshape(-1, quarter, v.shape[1]) for v in (gin_even, gin_odd)], axis=1)
        grad_in = sum_whole(gin_near, gin_far.reshape(gin_near.shape))
    grad_gates = grad_in[:, width : width + experts] + grad_in[:, width + experts : width + 2 * experts]
    inner_gate = jnp.sum(gates * grad_gates, axis=-1, keepdims=True)
    grad_logits = (gates * (grad_gates - inner_gate)).astype(BF)
    grad_routed = grad_in[:, :width] + mul(grad_logits, router_weight, NT)
    grad_top = grad_top_mine.astype(F32)
    scaled_two = grad_routed * mixer_gain
    grad_attended = grad_top + inverse_two * (
        scaled_two - unit_two * jnp.mean(scaled_two * unit_two, axis=-1, keepdims=True)
    )
    grad_branch = grad_attended.astype(BF)
    grad_mixed = mul(grad_branch, output_whole, NT).astype(BF)
    grad_mixed = [grad_mixed[:, s * heads_width : (s + 1) * heads_width] for s in range(n_tp)]

    grad_mixed, grad_branch = join(grad_mixed, grad_branch)
    grad_mixed = [grad_mixed[0]] + [turn(grad_mixed[s], -s) for s in range(1, n_tp)]
    if fine:
        out, out_got = sum_second(out, out_got)

    few = -(-(1 + experts) // n_ep)
    pad = 16 * (few // 16 + 1)
    small_rows = -(-few // 8) * 8
    grad_router = mul(routed_in, grad_logits, TN)
    grad_mixer = jnp.sum(grad_routed * unit_two, axis=0)
    small = jnp.concatenate([grad_mixer[None], grad_router.T], axis=0).astype(BF)
    small = jnp.pad(small, ((0, few * n_ep - 1 - experts), (0, 0))).reshape(n_ep, few, width)
    small = jnp.pad(small, ((0, 0), (0, pad - few), (0, 0)))
    grad_output = mul(mixed_mine, grad_branch, TN).astype(BF)
    grad_output = grad_output.reshape(n_tp, n_ep, part, width).transpose(1, 0, 2, 3)
    grad_output = jnp.concatenate([grad_output.reshape(n_ep, n_tp * part, width), small], axis=1)
    if fine:
        core, chip = lax.rem(ep_at, 2), lax.div(ep_at, 2)
        grad_output = grad_output.reshape((n_ep // 2, 2) + grad_output.shape[1:])
        other_output = lax.dynamic_index_in_dim(grad_output, 1 - core, 1, False)
        grad_output = lax.dynamic_index_in_dim(grad_output, core, 1, False)
        grad_mixed, out, out_got, other_output, grad_output = join(
            grad_mixed, out, out_got, other_output, grad_output
        )
        out = sum_last(out, out_got)
        other_output = swap(other_output, 1)
    else:
        out = sum_whole(out_near, out_far)
    result_mine = (attended + out).astype(BF)

    result_mine, grad_mixed = join(result_mine, grad_mixed)
    result_steps = [step_both(result_mine, result_mine)]
    *blocks, grad_qkv, end_block = attend_back(grad_mixed, query, key, value, logs, tables, qkv_weights, tp_at)
    if fine:
        blocks, grad_qkv, end_block, result_steps[0], other_output, grad_expert, inputs = join(
            blocks, grad_qkv, end_block, result_steps[0], other_output, grad_expert, inputs
        )
    else:
        blocks, grad_qkv, end_block, result_steps[0] = join(blocks, grad_qkv, end_block, result_steps[0])

    inputs32 = inputs.astype(F32)
    normed = inputs32 * lax.rsqrt(jnp.mean(inputs32 * inputs32, axis=-1, keepdims=True) + EPS)
    normed = (normed * norm_gain).astype(BF)
    grad_qkv_w = mul(normed, grad_qkv, TN).astype(BF)

    def chip_halves(half, *places):
        rows = grad_output.shape[1] // 2
        picked = []
        for j in places:
            chip_at = (jnp.bitwise_xor(chip, j), half * rows, 0)
            size = (1, rows, width)
            picked.append(
                add(
                    lax.dynamic_slice(grad_output, chip_at, size)[0],
                    lax.dynamic_slice(other_output, chip_at, size)[0],
                )
            )
        return jnp.concatenate(picked, axis=0)

    if fine:
        got = join(chip_halves(0, 2, 3), chip_halves(1, 1, 3))
        got = (swap(got[0], 4), swap(got[1], 2))
    result_steps.append(step_both(*result_steps[-1], 1))
    sent = step_ends(end_block, end_block, 0, 1)
    if fine:
        sent, result_steps[-1], got, grad_qkv_w = join(sent, result_steps[-1], got, grad_qkv_w)
        sums, got = sum_second((chip_halves(0, 0, 1), None, chip_halves(1, 0, 2)), got)
    else:
        sent, result_steps[-1], grad_qkv_w, grad_expert = join(
            sent, result_steps[-1], grad_qkv_w, grad_expert
        )
    grad_qkv_w = lax.psum(grad_qkv_w, "ep")
    sent = by_side(sent, 0, 1)
    result_last = None
    for t in range(2, n_tp):
        sent = step_both(add(blocks[n_tp - t], sent[0]), add(blocks[t], sent[1]), 0, t)
        if t < n_tp - 1:
            result_last = step_ends(*result_steps[-1], t, n_tp - 1)
            if fine:
                sent, result_last, got, sums = join(sent, result_last, got, sums)
                grad_output = sum_last(sums, got).astype(BF)
            else:
                sent, result_last = join(sent, result_last)
                grad_output = lax.psum_scatter(grad_output, "ep", scatter_dimension=0, tiled=False)
            pieces = [
                jnp.concatenate([grad_output[s * part : (s + 1) * part], grad_output[n_tp * part :][:small_rows]], axis=0)
                for s in range(n_tp)
            ]
    got = [turn(pieces[s], -s) for s in range(1, n_tp)]
    sent, result_steps, result_last = join(sent, result_steps, result_last)
    grad_normed = blocks[0].astype(F32) + sent[0].astype(F32) + sent[1].astype(F32)
    inputs_mine = mine(inputs).astype(F32)
    inverse_one = lax.rsqrt(jnp.mean(inputs_mine * inputs_mine, axis=-1, keepdims=True) + EPS)
    unit_one = inputs_mine * inverse_one
    scaled_one = grad_normed * norm_gain
    grad_inputs = grad_attended + inverse_one * (
        scaled_one - unit_one * jnp.mean(scaled_one * unit_one, axis=-1, keepdims=True)
    )
    grad_inputs = grad_inputs.astype(BF)
    grad_norm = jnp.sum(grad_normed * unit_one, axis=0)
    used = -(-(part + small_rows + 1) // 32) * 32

    grad_inputs, grad_norm = join(grad_inputs, grad_norm)
    input_steps = [step_both(grad_inputs, grad_inputs)]
    grad_norm = grad_norm[None]
    norm_got = [turn(grad_norm, s) for s in range(1, n_tp)]
    got, norm_got, input_steps[0] = join(got, norm_got, input_steps[0])
    grad_norm = (grad_norm + sum(norm_got))[0]
    grad_output = (pieces[0].astype(F32) + sum(v.astype(F32) for v in got)).astype(BF)
    grad_output = jnp.pad(grad_output, ((0, used - grad_output.shape[0]), (0, 0)))
    grad_output = grad_output.at[used - 1].set(grad_norm.astype(BF))
    if fine:
        got = [swap(grad_output, k) for k in (2, 4, 6)]
    grad_expert = grad_expert.reshape(3, -1, width).astype(F32)
    grad_gate_w, grad_up_w, grad_down_w = grad_expert[0].T, grad_expert[1].T, grad_expert[2]
    for t in range(1, n_tp - 2):
        input_steps.append(step_both(*input_steps[-1], t))
    if fine:
        got, input_steps[-1], grad_gate_w, grad_up_w, grad_down_w = join(
            got, input_steps[-1], grad_gate_w, grad_up_w, grad_down_w
        )
        near = jnp.concatenate([grad_output] + got, axis=0)
        far = swap(near, 1)
        far, grad_qkv_w = join(far, grad_qkv_w)
        devices = jnp.stack([jnp.bitwise_xor(ep_at, jnp.int32(k)) for k in (0, 2, 4, 6, 1, 3, 5, 7)])
        grad_output, small, grad_norm = set_rows(devices, near, far, part, small_rows)
        small = small.reshape(n_ep, small_rows, width)
        grad_norm = grad_norm[0]
    else:
        gathered = lax.all_gather(grad_output, "ep")
        small = gathered[:, part : part + small_rows].astype(F32)
        grad_norm = jnp.sum(gathered[:, used - 1].astype(F32), axis=0)
        grad_output = gathered[:, :part].reshape(heads_width, width).astype(F32)
    small = small[:, :few].reshape(n_ep * few, width)[: 1 + experts]
    result = spread(result_mine, result_steps, result_last)
    input_last = step_ends(*input_steps[-1], n_tp - 2, n_tp - 1)
    grad_qkv_w = grad_qkv_w.astype(F32)
    qkv_grads = (
        grad_qkv_w[:, :heads_width],
        grad_qkv_w[:, heads_width : heads_width + groups_width],
        grad_qkv_w[:, heads_width + groups_width :],
    )
    grad_norm, small, grad_output, input_last, qkv_grads, result = join(
        grad_norm, small, grad_output, input_last, qkv_grads, result
    )
    grad_inputs = spread(grad_inputs, input_steps, input_last)
    return (
        result,
        grad_inputs,
        grad_norm,
        *qkv_grads,
        grad_output,
        small[0],
        small[1:].T,
        grad_gate_w[None],
        grad_up_w[None],
        grad_down_w[None],
    )


def solution(mesh):
    placed = (
        P("ep", None),
        P("ep", None),
        P(),
        P(None, "tp"),
        P(None, "tp"),
        P(None, "tp"),
        P("tp", None),
        P(),
        P(),
        P("ep", None, "tp"),
        P("ep", None, "tp"),
        P("ep", "tp", None),
        P("ep", None),
    )
    return jax.shard_map(
        body,
        mesh=mesh,
        in_specs=placed,
        out_specs=(
            P("ep", None),
            P("ep", None),
            P(),
            P(None, "tp"),
            P(None, "tp"),
            P(None, "tp"),
            P("tp", None),
            P(),
            P(),
            P("ep", None, "tp"),
            P("ep", None, "tp"),
            P("ep", "tp", None),
        ),
        check_vma=False,
    )
```
